32 devices in a mesh: batch: 8 (over z, x), head: 4 (over y, core).
Axes of the slice: x: 2, y: 2, z: 4, core: 2. Of those that a mesh axis runs over, the one named last changes fastest.
Arguments:
- tokens_in: bfloat16 [32768, 512], P(('batch', 'head')), may hold values from -6 to 6
- norm1_gain: bfloat16 [512], replicated, may hold values from 0.5 to 1.5
- norm1_bias: bfloat16 [512], replicated, may hold values from -3 to 3
- qkv_weight: bfloat16 [512, 3, 512], P(None, None, 'head'), may hold values from -0.25 to 0.25
- qkv_bias: bfloat16 [3, 512], P(None, 'head'), may hold values from -3 to 3
- out_weight: bfloat16 [512, 512], P('head'), may hold values from -1.5 to 1.5
- out_bias: bfloat16 [512], replicated, may hold values from -3 to 3
- norm2_gain: bfloat16 [512], replicated, may hold values from 0.5 to 1.5
- norm2_bias: bfloat16 [512], replicated, may hold values from -3 to 3
- up_weight: bfloat16 [512, 2048], P(None, 'head'), may hold values from -0.25 to 0.25
- up_bias: bfloat16 [2048], P('head'), may hold values from -3 to 3
- down_weight: bfloat16 [2048, 512], P('head'), may hold values from -0.125 to 0.125
- down_bias: bfloat16 [512], replicated, may hold values from -3 to 3
- cotangent: bfloat16 [32768, 512], P(('batch', 'head')), may hold values from -6 to 6
- long_slot: int32 [16], P('batch'), may hold values 0 or 1
Outputs:
- layer_out: bfloat16 [32768, 512], P(('batch', 'head'))
- input_grad: bfloat16 [32768, 512], P(('batch', 'head'))
- norm1_gain_grad: float32 [512], replicated
- norm1_bias_grad: float32 [512], replicated
- qkv_weight_grad: float32 [512, 3, 512], P(None, None, 'head')
- qkv_bias_grad: float32 [3, 512], P(None, 'head')
- out_weight_grad: float32 [512, 512], P('head')
- out_bias_grad: float32 [512], replicated
- norm2_gain_grad: float32 [512], replicated
- norm2_bias_grad: float32 [512], replicated
- up_weight_grad: float32 [512, 2048], P(None, 'head')
- up_bias_grad: float32 [2048], P('head')
- down_weight_grad: float32 [2048, 512], P('head')
- down_bias_grad: float32 [512], replicated
The draws below stay inside these ranges and needn't reach their ends.
Inputs may be any that keep to these rules, and one draw needn't show every extreme that they name: `long_slot`: 1: the slot's 2048 tokens are one sequence; 0: they are two sequences of 1024 tokens.
All inputs are finite; a program needn't handle non-finite values. No bound on the sum of `long_slot` on one device may be relied on, other than what follows from the above.
Results may differ from the reference program's by a relative error of at most 0.017.
Values may be sent and summed in bfloat16 or wider, within the bound.
No kernel may reach another device: no remote copies, remote signals or barrier semaphores. Data moves between devices by JAX's collectives and lax.ppermute only.
A program may use at most 256 MiB of HBM per device.

```python
from functools import partial
import jax
import jax.numpy as jnp
from jax import lax

D = 512
H = 8
HD = 64
FF = 2048
SHORT = 1024
LONG = 2048
HH = 512
N_SLOTS = 16
TOKENS = 32768


def touch_ends(drawn, stream_key, least, largest):
    shape = drawn.shape
    index_at = [jax.random.randint(jax.random.fold_in(stream_key, axis), (), 0, shape[axis]) for axis in range(len(shape))]
    drawn = drawn.at[tuple(index_at)].set(least)
    longest = shape.index(max(shape))
    index_at[longest] = (index_at[longest] + 1) % shape[longest]
    return drawn.at[tuple(index_at)].set(largest)


def block_scale(own_key, extent, split, least, largest):
    def one(axis_at, parts):
        draws = jax.random.uniform(jax.random.fold_in(jax.random.fold_in(own_key, 6), axis_at), (parts,), jnp.float32, least / len(split), largest / len(split))
        return jnp.repeat(jnp.exp(draws), extent[axis_at] // parts).reshape((-1,) + (1,) * (len(extent) - axis_at - 1))

    factor_of = one(*split[0])
    for cut in split[1:]:
        factor_of = factor_of * one(*cut)
    return factor_of


def bell_draw(rng, dims, deviation, reach, split=(), held_as=jnp.bfloat16):
    array = jax.random.normal(rng, dims, jnp.float32) * deviation
    if len(split) > 0:
        array = block_scale(rng, dims, split, -0.22, 0.18) * array
    return jnp.clip(array, min=-reach, max=reach).astype(held_as)


def setup_inputs(seed: int = 0) -> dict:
    key_of = jax.random.split(jax.random.key(seed), 16)
    return {
        "tokens_in": bell_draw(key_of[0], (TOKENS, D), 1.0, 6.0, ((0, 32),)),
        "norm1_gain": jnp.clip(1.0 + 0.1 * jax.random.normal(key_of[1], (D,), jnp.float32), 0.5, 1.5).astype(jnp.bfloat16),
        "norm1_bias": bell_draw(key_of[2], (D,), 0.3, 3.0),
        "qkv_weight": bell_draw(key_of[3], (D, 3, HH), D ** -0.5, 0.25, ((2, 4),)),
        "qkv_bias": bell_draw(key_of[4], (3, HH), 0.3, 3.0, ((1, 4),)),
        "out_weight": bell_draw(key_of[5], (HH, D), (D // 32) ** -0.5, 1.5, ((0, 4),)),
        "out_bias": bell_draw(key_of[6], (D,), 0.3, 3.0),
        "norm2_gain": jnp.clip(1.0 + 0.1 * jax.random.normal(key_of[7], (D,), jnp.float32), 0.5, 1.5).astype(jnp.bfloat16),
        "norm2_bias": bell_draw(key_of[8], (D,), 0.3, 3.0),
        "up_weight": bell_draw(key_of[9], (D, FF), D ** -0.5, 0.25, ((1, 4),)),
        "up_bias": bell_draw(key_of[10], (FF,), 0.5, 3.0, ((0, 4),)),
        "down_weight": bell_draw(key_of[11], (FF, D), FF ** -0.5, 0.125, ((0, 4),)),
        "down_bias": bell_draw(key_of[12], (D,), 0.3, 3.0),
        "cotangent": bell_draw(key_of[13], (TOKENS, D), 1.0, 6.0, ((0, 32),)),
        "long_slot": touch_ends((jax.random.randint(key_of[14], (N_SLOTS,), 0, 2) < 1).astype(jnp.int32), jax.random.fold_in(key_of[14], 1), 0, 1),
    }


HIGHEST_PRECISION = lax.Precision.HIGHEST

@jax.custom_vjp
def low(v):
    return lax.optimization_barrier(v.astype(jnp.bfloat16)).astype(jnp.float32)

@jax.custom_vjp
def low_back(v):
    return v

def low_keep(v):
    return (low(v), None)

def low_pass(kept, grad):
    return (grad,)

def back_keep(v):
    return (v, None)

def back_low(kept, grad):
    return (low(grad),)
low.defvjp(low_keep, low_pass)
low_back.defvjp(back_keep, back_low)

def product(left_side, right_side):
    return jnp.dot(left_side, right_side, precision=HIGHEST_PRECISION, preferred_element_type=jnp.float32)

def layer_norm(row_values, gain_vector, bias_vector):
    centered = row_values - lax.optimization_barrier(jnp.mean(row_values, axis=-1, keepdims=True))
    variance = lax.optimization_barrier(jnp.mean(centered * centered, axis=-1, keepdims=True))
    return centered * lax.rsqrt(variance + 1e-05) * gain_vector + bias_vector

def gelu_tanh(pre_activation):
    cubic = pre_activation + 0.044715 * pre_activation * pre_activation * pre_activation
    return 0.5 * pre_activation * (1.0 + jnp.tanh(0.7978845608028654 * cubic))

def head_attend(slot_flag, head_arrays):
    queries, keys_in, values_in = head_arrays
    scores = low_back(product(queries, keys_in.T) * HD ** (-0.5))
    positions = jnp.arange(LONG, dtype=jnp.int32)
    query_pos = positions[:, None]
    key_pos = positions[None, :]
    visible = (key_pos <= query_pos) & ((slot_flag > 0) | (query_pos // SHORT == key_pos // SHORT))
    magnitude = jnp.where(visible, jnp.abs(scores), -1e+30)
    row_top = lax.optimization_barrier(jnp.max(magnitude, axis=1, keepdims=True))
    powers = jnp.where(visible, jnp.exp(magnitude - row_top), 0.0)
    row_total = lax.optimization_barrier(jnp.sum(powers, axis=1, keepdims=True))
    signed = jnp.where(visible, jnp.sign(scores) * (powers - jnp.exp(-row_top)), 0.0) / row_total
    return product(low(signed), values_in)

def slot_forward(weights_in, slot_rows, slot_flag):
    first_gain, first_bias, qkv_matrix, qkv_shift, out_matrix, out_shift, second_gain, second_bias, up_matrix, up_shift, down_matrix, down_shift = weights_in
    normed1 = low(layer_norm(slot_rows, first_gain, first_bias))
    triple = jnp.einsum('td,dch->tch', normed1, qkv_matrix, precision=HIGHEST_PRECISION) + qkv_shift
    triple = low(low_back(triple))
    per_head = triple.reshape(LONG, 3, H, HD).transpose(1, 2, 0, 3)
    attended = lax.map(jax.checkpoint(partial(head_attend, slot_flag)), (per_head[0], per_head[1], per_head[2]))
    attended = attended.transpose(1, 0, 2).reshape(LONG, H * HD)
    attended = low_back(low(attended))
    branch = low_back(product(attended, out_matrix) + out_shift)
    middle = slot_rows + branch
    normed2 = low(layer_norm(middle, second_gain, second_bias))
    pre_activation = low_back(product(normed2, up_matrix) + up_shift)
    activated = low(gelu_tanh(pre_activation))
    return middle + product(activated, down_matrix) + down_shift

def reference(tokens_in, norm1_gain, norm1_bias, qkv_weight, qkv_bias, out_weight, out_bias, norm2_gain, norm2_bias, up_weight, up_bias, down_weight, down_bias, cotangent, long_slot):
    weights_in = tuple((array_in.astype(jnp.float32) for array_in in (norm1_gain, norm1_bias, qkv_weight, qkv_bias, out_weight, out_bias, norm2_gain, norm2_bias, up_weight, up_bias, down_weight, down_bias)))
    all_rows = tokens_in.astype(jnp.float32).reshape(N_SLOTS, LONG, D)
    all_cot = cotangent.astype(jnp.float32).reshape(N_SLOTS, LONG, D)

    def slot_step(running, slot_item):
        slot_rows, slot_cot, slot_flag = slot_item
        slot_out, pullback = jax.vjp(lambda params_in, rows_in: slot_forward(params_in, rows_in, slot_flag), weights_in, slot_rows)
        params_grad, rows_grad = pullback(slot_cot)
        running = tuple((before + extra for before, extra in zip(running, params_grad)))
        return (running, (slot_out.astype(jnp.bfloat16), rows_grad.astype(jnp.bfloat16)))
    start_sums = tuple((jnp.zeros_like(array_in) for array_in in weights_in))
    sums_out, (outs_all, grads_all) = lax.scan(slot_step, start_sums, (all_rows, all_cot, long_slot))
    return (outs_all.reshape(TOKENS, D), grads_all.reshape(TOKENS, D), sums_out[0], sums_out[1], sums_out[2], sums_out[3], sums_out[4], sums_out[5], sums_out[6], sums_out[7], sums_out[8], sums_out[9], sums_out[10], sums_out[11])
```

```python
import functools

import jax
import jax.numpy as jnp
from jax import lax
from jax.experimental import pallas as pl
from jax.experimental.pallas import tpu as pltpu
from jax.sharding import PartitionSpec as P

HD = 64
SHORT = 1024
F32 = jnp.float32
BF = jnp.bfloat16
LOG2E = 1.4426950408889634
GELU_C = 0.7978845608028654
CHUNK = 512
VMEM_LIMIT = 56 * 1024 * 1024


def nt(a, b):
    return lax.dot_general(a, b, (((1,), (1,)), ((), ())), preferred_element_type=F32)


def nn(a, b):
    return lax.dot_general(a, b, (((1,), (0,)), ((), ())), preferred_element_type=F32)


def tn(a, b):
    return lax.dot_general(a, b, (((0,), (0,)), ((), ())), preferred_element_type=F32)


def head_mask(shape, h):
    lane = lax.broadcasted_iota(jnp.int32, shape, len(shape) - 1)
    return (lane >= h * HD) & (lane < (h + 1) * HD)


def lane_sum(e):
    width = min(128, e.shape[1])
    total = e[:, :width]
    for i in range(1, e.shape[1] // width):
        total = total + e[:, i * width : (i + 1) * width]
    return total


def fwd_kernel(bq, bk, nh, W, L, flag_ref, q_ref, k_ref, v_ref, o_ref, st_ref, *rest):
    nck = L // CHUNK
    w_refs = rest[:nck]
    kk, vm = rest[nck:]
    qi = pl.program_id(0)
    nq = L // bq

    @pl.when(qi == 0)
    def _():
        kv = k_ref[...]
        kk[...] = jnp.concatenate([kv, kv], axis=1)
        vv = v_ref[...]
        for h in range(nh):
            vm[h] = jnp.where(head_mask(vv.shape, h), vv, jnp.zeros_like(vv))

    def scaled_queries():
        qf = q_ref[...].astype(F32) * (LOG2E * HD**-0.5)
        hi = qf.astype(BF)
        lo = (qf - hi.astype(F32)).astype(BF)
        qs = []
        z = jnp.zeros_like(hi)
        for h in range(nh):
            m = head_mask(hi.shape, h)
            qs.append(jnp.concatenate([jnp.where(m, hi, z), jnp.where(m, lo, z)], axis=1))
        return qs

    def finish(acc, sums, bases):
        lane = lax.broadcasted_iota(jnp.int32, (bq, 128), 1)
        st = jnp.ones((bq, 128), F32)
        out = jnp.zeros((bq, W), F32)
        for h in range(nh):
            inv = 1.0 / sums[h]
            st = jnp.where(lane == h, inv, st)
            if bases is not None:
                st = jnp.where(lane == 8 + h, bases[h], st)
            out = jnp.where(head_mask(out.shape, h), acc * inv, out)
        st_ref[...] = st
        o_ref[...] = out.astype(BF)

    sq_r = lax.broadcasted_iota(jnp.int32, (bk, bk), 0)
    sq_c = lax.broadcasted_iota(jnp.int32, (bk, bk), 1)

    def fast(c, lo_blk):
        qs = scaled_queries()
        nr = bq // bk
        acc = [None] * nr
        ls = [[None] * nr for _ in range(nh)]
        for kb in range(lo_blk, (c + 1) * nr):
            base = kb * bk
            first = max(0, kb - c * nr)
            r0 = first * bk
            kt = kk[base : base + bk, :]
            wl = []
            for h in range(nh):
                s = nt(qs[h][r0:, :], kt)
                if base >= c * bq:
                    top = jnp.where(sq_c <= sq_r, s[:bk, :], 0.0)
                    s = top if r0 + bk == bq else jnp.concatenate([top, s[bk:, :]], axis=0)
                e = jnp.exp2(jnp.abs(s))
                wv = jnp.where(s < 0, 1.0 - e, e - 1.0).astype(BF)
                t = lane_sum(e)
                for r in range(first, nr):
                    tr = t[(r - first) * bk : (r - first + 1) * bk, :]
                    ls[h][r] = tr if ls[h][r] is None else ls[h][r] + tr
                w_refs[base // CHUNK][h, r0:, base % CHUNK : base % CHUNK + bk] = wv
                wl.append(wv)
            vcat = jnp.concatenate([vm[h, base : base + bk, :] for h in range(nh)], axis=0)
            res = nn(jnp.concatenate(wl, axis=1), vcat)
            for r in range(first, nr):
                part = res[(r - first) * bk : (r - first + 1) * bk, :]
                acc[r] = part if acc[r] is None else acc[r] + part
        row = lax.broadcasted_iota(jnp.int32, (bq, 1), 0)
        extra = (bk - 1 - row % bk).astype(F32)
        sums = [
            jnp.sum(jnp.concatenate(ls[h], axis=0), axis=1, keepdims=True) - extra
            for h in range(nh)
        ]
        finish(jnp.concatenate(acc, axis=0), sums, None)

    for c in range(nq):
        if c * bq < SHORT:
            pl.when(qi == c)(functools.partial(fast, c, 0))
        else:
            pl.when((qi == c) & (flag_ref[0] > 0))(functools.partial(fast, c, 0))
            pl.when((qi == c) & (flag_ref[0] <= 0))(functools.partial(fast, c, SHORT // bk))

    lane = lax.broadcasted_iota(jnp.int32, (bq, 128), 1)
    smallest = jnp.min(jnp.where(lane < nh, st_ref[...], 1.0))

    @pl.when(smallest < 1e-25)
    def _():
        qs = scaled_queries()
        lo_blk = jnp.where((flag_ref[0] > 0) | (qi * bq < SHORT), 0, SHORT // bk)
        hi_blk = (qi + 1) * (bq // bk)
        rows = lax.broadcasted_iota(jnp.int32, (bq, bk), 0) + qi * bq
        cols = lax.broadcasted_iota(jnp.int32, (bq, bk), 1)

        def scores(h, kb):
            kt = kk[pl.ds(pl.multiple_of(kb * bk, bk), bk), :]
            return nt(qs[h], kt), cols + kb * bk <= rows

        def top_step(kb, tops):
            new = []
            for h in range(nh):
                s, vis = scores(h, kb)
                mag = jnp.where(vis, jnp.abs(s), 0.0)
                new.append(jnp.maximum(tops[h], jnp.max(mag, axis=1, keepdims=True)))
            return tuple(new)

        tops = lax.fori_loop(lo_blk, hi_blk, top_step, (jnp.zeros((bq, 1), F32),) * nh)
        bases = [jnp.exp2(-t) for t in tops]

        def step(kb, carry):
            acc, sums = carry
            new = []
            for h in range(nh):
                s, vis = scores(h, kb)
                e = jnp.where(vis, jnp.exp2(jnp.abs(s) - tops[h]), 0.0)
                wv = jnp.where(s < 0, bases[h] - e, e - bases[h])
                wv = jnp.where(vis & (s != 0), wv, 0.0).astype(BF)
                new.append(sums[h] + jnp.sum(e, axis=1, keepdims=True))
                acc = acc + nn(wv, vm[h, pl.ds(pl.multiple_of(kb * bk, bk), bk), :])
                for j in range(nck):

                    @pl.when(kb // (CHUNK // bk) == j)
                    def _():
                        off = pl.multiple_of((kb % (CHUNK // bk)) * bk, bk)
                        w_refs[j][h, :, pl.ds(off, bk)] = wv

            return acc, tuple(new)

        acc, sums = lax.fori_loop(
            lo_blk,
            hi_blk,
            step,
            (jnp.zeros((bq, W), F32), (jnp.zeros((bq, 1), F32),) * nh),
        )
        finish(acc, sums, bases)


def w_specs(nh, bq, L):
    return [
        pl.BlockSpec((nh, bq, CHUNK), lambda qi, j=j: (0, jnp.maximum(qi, j * (CHUNK // bq)), 0))
        for j in range(L // CHUNK)
    ]


def attn_fwd(flag, q, k, v, bq=512, bk=256):
    L, W = q.shape
    nh = W // HD
    S = jax.ShapeDtypeStruct
    whole = pl.BlockSpec((L, W), lambda qi: (0, 0))
    rows = pl.BlockSpec((bq, W), lambda qi: (qi, 0))
    res = pl.pallas_call(
        functools.partial(fwd_kernel, bq, bk, nh, W, L),
        grid=(L // bq,),
        in_specs=[pl.BlockSpec(memory_space=pltpu.SMEM), rows, whole, whole],
        out_specs=[rows, pl.BlockSpec((bq, 128), lambda qi: (qi, 0))] + w_specs(nh, bq, L),
        out_shape=[S((L, W), BF), S((L, 128), F32)] + [S((nh, L, CHUNK), BF)] * (L // CHUNK),
        scratch_shapes=[pltpu.VMEM((L, 2 * W), BF), pltpu.VMEM((nh, L, W), BF)],
        compiler_params=pltpu.CompilerParams(vmem_limit_bytes=VMEM_LIMIT),
        cost_estimate=pl.CostEstimate(
            flops=8 * L * L * W, bytes_accessed=2 * nh * L * L, transcendentals=nh * L * L
        ),
        name="attn_fwd",
    )(flag, q, k, v)
    return res[0], res[1], res[2:]


def bwd_kernel(bq, bk, nh, W, L, flag_ref, q_ref, k_ref, v_ref, o_ref, do_ref, st_ref, *rest):
    nck = L // CHUNK
    w_refs = rest[:nck]
    dq_ref, dk_ref, dv_ref, km, dka, dva = rest[nck:]
    qi = pl.program_id(0)
    nq = L // bq

    @pl.when(qi == 0)
    def _():
        kv = k_ref[...]
        for h in range(nh):
            km[h] = jnp.where(head_mask(kv.shape, h), kv, jnp.zeros_like(kv))
        dka[...] = jnp.zeros_like(dka)
        dva[...] = jnp.zeros_like(dva)

    sq_r = lax.broadcasted_iota(jnp.int32, (bk, bk), 0)
    sq_c = lax.broadcasted_iota(jnp.int32, (bk, bk), 1)

    def body(c, lo_blk):
        nr = bq // bk
        tri = jnp.where(sq_c <= sq_r, 1.0, 0.0).astype(BF)
        st = st_ref[...]
        dof = do_ref[...].astype(F32)
        prod = dof * o_ref[...].astype(F32)
        dos = []
        deltas = []
        e0s = []
        dosum = jnp.zeros((bq, W), F32)
        rep = bk // 128
        for h in range(nh):
            inv = st[:, h : h + 1]
            m = head_mask((bq, W), h)
            x = jnp.where(m, dof * inv, 0.0)
            dosum = dosum + x
            dos.append(x.astype(BF))
            delta = jnp.sum(jnp.where(m, prod, 0.0), axis=1, keepdims=True) * inv
            deltas.append(jnp.concatenate([jnp.broadcast_to(delta, (bq, 128)).astype(BF)] * rep, 1))
            e0 = jnp.broadcast_to(st[:, 8 + h : 9 + h], (bq, 128)).astype(BF)
            e0s.append(jnp.concatenate([e0] * rep, 1))
        do_t = dosum.T.astype(BF)
        q_t = q_ref[...].astype(F32).T.astype(BF)
        dq = [jnp.zeros((bk, W), F32)] * nr
        for kb in range(lo_blk, (c + 1) * nr):
            base = kb * bk
            first = max(0, kb - c * nr)
            r0 = first * bk
            vt = v_ref[base : base + bk, :]
            gl = []
            for h in range(nh):
                wv = w_refs[base // CHUNK][h, r0:, base % CHUNK : base % CHUNK + bk]
                wg = nt(dos[h][r0:, :], vt).astype(BF)
                dl = deltas[h][r0:, :]
                e0 = e0s[h][r0:, :]
                if base >= c * bq:
                    top = e0[:bk, :] * tri
                    e0 = top if r0 + bk == bq else jnp.concatenate([top, e0[bk:, :]], axis=0)
                zero = jnp.zeros_like(wv)
                d = jnp.where(wv < 0, -dl, jnp.where(wv > 0, dl, zero))
                g = (jnp.abs(wv) + e0) * (wg - d)
                cols = slice(base, base + bk)
                lanes = slice(h * HD, (h + 1) * HD)
                dva[lanes, cols] += nn(do_t[lanes, r0:], wv)
                dka[lanes, cols] += nn(q_t[lanes, r0:], g)
                gl.append(g)
            kcat = jnp.concatenate([km[h, base : base + bk, :] for h in range(nh)], axis=0)
            res = nn(jnp.concatenate(gl, axis=1), kcat)
            for r in range(first, nr):
                dq[r] = dq[r] + res[(r - first) * bk : (r - first + 1) * bk, :]
        dq_ref[...] = (jnp.concatenate(dq, axis=0) * (HD**-0.5)).astype(BF)

    for c in range(nq):
        if c * bq < SHORT:
            pl.when(qi == c)(functools.partial(body, c, 0))
        else:
            pl.when((qi == c) & (flag_ref[0] > 0))(functools.partial(body, c, 0))
            pl.when((qi == c) & (flag_ref[0] <= 0))(functools.partial(body, c, SHORT // bk))

    @pl.when(qi == nq - 1)
    def _():
        dk_ref[...] = (dka[...] * (HD**-0.5)).T.astype(BF)
        dv_ref[...] = dva[...].T.astype(BF)


def attn_bwd(flag, q, k, v, o, do, st, ws, bq=512, bk=256):
    L, W = q.shape
    nh = W // HD
    whole = pl.BlockSpec((L, W), lambda qi: (0, 0))
    rows = pl.BlockSpec((bq, W), lambda qi: (qi, 0))
    return pl.pallas_call(
        functools.partial(bwd_kernel, bq, bk, nh, W, L),
        grid=(L // bq,),
        in_specs=[
            pl.BlockSpec(memory_space=pltpu.SMEM),
            rows,
            whole,
            whole,
            rows,
            rows,
            pl.BlockSpec((bq, 128), lambda qi: (qi, 0)),
        ]
        + w_specs(nh, bq, L),
        out_specs=[rows, whole, whole],
        out_shape=[jax.ShapeDtypeStruct((L, W), BF)] * 3,
        scratch_shapes=[
            pltpu.VMEM((nh, L, W), BF),
            pltpu.VMEM((W, L), F32),
            pltpu.VMEM((W, L), F32),
        ],
        compiler_params=pltpu.CompilerParams(vmem_limit_bytes=VMEM_LIMIT),
        cost_estimate=pl.CostEstimate(
            flops=16 * L * L * W, bytes_accessed=2 * nh * L * L, transcendentals=0
        ),
        name="attn_bwd",
    )(flag, q, k, v, o, do, st, *ws)


def ln_stats(v):
    c = v - jnp.mean(v, axis=1, keepdims=True)
    r = lax.rsqrt(jnp.mean(c * c, axis=1, keepdims=True) + 1e-5)
    return c * r, r


def ffn_kernel(
    nf,
    x_ref,
    att_ref,
    cot_ref,
    ow_ref,
    vec_ref,
    up_ref,
    upb_ref,
    dn_ref,
    lo_ref,
    mg_ref,
    atg_ref,
    ug_ref,
    dg_ref,
    og_ref,
    vg_ref,
    ubg_ref,
    mids,
    n2,
    n2t,
    cott,
    oacc,
    nacc,
):
    f = pl.program_id(0)

    @pl.when(f == 0)
    def _():
        mid = x_ref[...].astype(F32) + nn(att_ref[...], ow_ref[...]) + vec_ref[0:1, :]
        mids[...] = mid
        oacc[...] = mid + vec_ref[3:4, :]
        nacc[...] = jnp.zeros_like(nacc)
        xh, _ = ln_stats(mid)
        y = xh * vec_ref[1:2, :] + vec_ref[2:3, :]
        n2[...] = y.astype(BF)
        n2t[...] = y.T.astype(BF)
        cott[...] = cot_ref[...].astype(F32).T.astype(BF)

    up = up_ref[...]
    dn = dn_ref[...]
    cot = cot_ref[...]
    u = nn(n2[...], up) + upb_ref[...]
    ag = nt(cot, dn)
    u2 = u * u
    t = jnp.tanh(u * (GELU_C + (GELU_C * 0.044715) * u2))
    h = 0.5 + 0.5 * t
    act = (u * h).astype(BF)
    slope = h + u * (0.5 - 0.5 * t * t) * (GELU_C + (3 * GELU_C * 0.044715) * u2)
    pgf = ag * slope
    pg = pgf.astype(BF)
    ubg_ref[...] = jnp.sum(pgf, axis=0, keepdims=True)
    oacc[...] += nn(act, dn)
    nacc[...] += nt(pg, up)
    ug_ref[...] = nn(n2t[...], pg).astype(BF)
    dg_ref[...] = nn(cott[...], act).T.astype(BF)

    @pl.when(f == nf - 1)
    def _():
        lo_ref[...] = oacc[...].astype(BF)
        xh, r = ln_stats(mids[...])
        ng = nacc[...]
        e = ng * vec_ref[1:2, :]
        cf = cot.astype(F32)
        back = e - jnp.mean(e, axis=1, keepdims=True) - xh * jnp.mean(e * xh, axis=1, keepdims=True)
        mg = cf + r * back
        mg_ref[...] = mg
        bg = mg.astype(BF)
        atg_ref[...] = nt(bg, ow_ref[...]).astype(BF)
        og_ref[...] = tn(att_ref[...], bg).astype(BF)

        def total(a):
            return jnp.sum(a, axis=0, keepdims=True)

        z = jnp.zeros((4, vg_ref.shape[1]), F32)
        vg_ref[...] = jnp.concatenate(
            [total(bg.astype(F32)), total(ng * xh), total(ng), total(cf), z], axis=0
        )


def ffn(x, att, cot, ow, vec, up, upb, dn, fb=512):
    R, D = x.shape
    F = up.shape[1]
    nf = F // fb
    S = jax.ShapeDtypeStruct

    def full(a):
        return pl.BlockSpec(a.shape, lambda f: (0,) * len(a.shape))

    outs = [
        S((R, D), BF),
        S((R, D), F32),
        S((R, D), BF),
        S((D, F), BF),
        S((F, D), BF),
        S((D, D), BF),
        S((8, D), F32),
        S((1, F), F32),
    ]
    colb = pl.BlockSpec((D, fb), lambda f: (0, f))
    rowb = pl.BlockSpec((fb, D), lambda f: (f, 0))
    vecb = pl.BlockSpec((1, fb), lambda f: (0, f))
    return pl.pallas_call(
        functools.partial(ffn_kernel, nf),
        grid=(nf,),
        in_specs=[full(x), full(att), full(cot), full(ow), full(vec), colb, vecb, rowb],
        out_specs=[full(o) for o in outs[:3]] + [colb, rowb, full(outs[5]), full(outs[6]), vecb],
        out_shape=outs,
        scratch_shapes=[
            pltpu.VMEM((R, D), F32),
            pltpu.VMEM((R, D), BF),
            pltpu.VMEM((D, R), BF),
            pltpu.VMEM((D, R), BF),
            pltpu.VMEM((R, D), F32),
            pltpu.VMEM((R, D), F32),
        ],
        compiler_params=pltpu.CompilerParams(vmem_limit_bytes=VMEM_LIMIT),
        cost_estimate=pl.CostEstimate(
            flops=12 * R * D * F, bytes_accessed=16 * R * D, transcendentals=R * F
        ),
        name="ffn",
    )(x, att, cot, ow, vec, up, upb, dn)


def per_device(
    tokens_in,
    norm1_gain,
    norm1_bias,
    qkv_weight,
    qkv_bias,
    out_weight,
    out_bias,
    norm2_gain,
    norm2_bias,
    up_weight,
    up_bias,
    down_weight,
    down_bias,
    cotangent,
    long_slot,
):
    n = lax.axis_size("head")
    nb = lax.axis_size("batch")
    me = lax.axis_index("head")
    bi = lax.axis_index("batch")
    slots = long_slot.shape[0]
    g = n // slots
    p = me % g
    R, D = tokens_in.shape
    L = R * g
    W = qkv_weight.shape[2]
    FS = up_weight.shape[1]
    flag = lax.dynamic_slice(long_slot, (me // g,), (1,))

    def cross(x, r):
        return lax.ppermute(x, "head", [(i, (i + r * g) % n) for i in range(n)])

    def rot(x, r):
        return lax.ppermute(x, "head", [(i, i // g * g + (i % g - r) % g) for i in range(n)])

    def flip(x, bit):
        return lax.ppermute(x, "batch", [(i, i ^ bit) for i in range(nb)])

    def phases(x):
        return [x] + [cross(x, r) for r in range(1, slots)]

    def group(x):
        return [x] + [rot(x, r) for r in range(1, g)]

    def rows_of(x, member):
        return lax.dynamic_slice_in_dim(x, member * R, R, 0)

    qw = phases(qkv_weight.reshape(D, 3 * W))
    ow = phases(out_weight)
    uw = phases(up_weight)
    dw = phases(down_weight)
    qb = phases(qkv_bias.reshape(3, 1, W))
    ub = phases(up_bias.reshape(1, FS))

    x = tokens_in.astype(F32)
    gain1 = norm1_gain.astype(F32)
    xh1, r1 = ln_stats(x)
    n1 = (xh1 * gain1 + norm1_bias.astype(F32)).astype(BF)
    pieces = group(n1)
    n1all = jnp.zeros((L, D), BF)
    for r in range(g):
        n1all = lax.dynamic_update_slice_in_dim(n1all, pieces[r], (p + r) % g * R, 0)

    att_cols = []
    saved = []
    for ph in range(slots):
        w3 = qw[ph].reshape(D, 3, W)
        q, k, v = (
            (nn(n1all, w3[:, i]) + qb[ph][i].astype(F32)).astype(BF) for i in range(3)
        )
        o, st, ws = attn_fwd(flag, q, k, v)
        saved.append((q, k, v, o, st, ws))
        cols = [None] * g
        cols[0] = rows_of(o, p)
        for r in range(1, g):
            cols[r] = rot(rows_of(o, (p - r) % g), r)
        att_cols += cols
    att = jnp.concatenate(att_cols, axis=1)

    owf = jnp.concatenate([b for a in ow for b in group(a)], axis=0)
    uwf = jnp.concatenate([b for a in uw for b in group(a)], axis=1)
    dwf = jnp.concatenate([b for a in dw for b in group(a)], axis=0)
    ubf = jnp.concatenate([b for a in ub for b in group(a)], axis=1).astype(F32)
    vec = jnp.stack([out_bias, norm2_gain, norm2_bias, down_bias] + [out_bias] * 4).astype(F32)
    layer_out, mg, atg, ug, dg, og, vg, ubg = ffn(
        tokens_in, att, cotangent, owf, vec, uwf, ubf, dwf
    )

    def reduce_batch(a):
        bits = []
        bit = 1
        while bit < nb:
            bits.append(bit)
            bit *= 2
        for bit in bits:
            half = a.shape[0] // 2
            up_side = (bi & bit) > 0
            lo_half, hi_half = a[:half], a[half:]
            got = flip(jnp.where(up_side, lo_half, hi_half), bit)
            keep = jnp.where(up_side, hi_half, lo_half)
            a = (keep.astype(F32) + got.astype(F32)).astype(BF)
        for bit in bits[::-1]:
            up_side = (bi & bit) > 0
            got = flip(a, bit)
            a = jnp.concatenate([jnp.where(up_side, got, a), jnp.where(up_side, a, got)], axis=0)
        return a

    def reduce_group(parts):
        out = []
        for ph in range(slots):
            a = parts[ph][0].astype(F32)
            for r in range(1, g):
                a = a + rot(parts[ph][r], g - r).astype(F32)
            out.append(a.astype(BF))
        return out

    def reduce_cross(parts):
        a = parts[0].astype(F32)
        for r in range(1, slots):
            a = a + cross(parts[r], slots - r).astype(F32)
        return a.astype(BF)

    def cols(a, i, w):
        return a[:, i * w : (i + 1) * w]

    def rows(a, i, w):
        return a[i * w : (i + 1) * w]

    ug_own = reduce_batch(
        reduce_cross(
            reduce_group([[cols(ug, ph * g + r, FS) for r in range(g)] for ph in range(slots)])
        )
    )
    dg_own = reduce_batch(
        reduce_cross(
            reduce_group(
                [
                    [
                        jnp.concatenate([rows(dg, ph * g + r, FS), rows(og, ph * g + r, W)], 0)
                        for r in range(g)
                    ]
                    for ph in range(slots)
                ]
            )
        )
    )

    n1g = jnp.zeros((L, D), F32)
    qg_parts = []
    qbg_parts = []
    for ph in range(slots):
        q, k, v, o, st, ws = saved[ph]
        mine = [cols(atg, ph * g + r, W) for r in range(g)]
        do = jnp.zeros((L, W), BF)
        do = lax.dynamic_update_slice_in_dim(do, mine[0], p * R, 0)
        for r in range(1, g):
            do = lax.dynamic_update_slice_in_dim(do, rot(mine[r], g - r), (p - r) % g * R, 0)
        tg = jnp.concatenate(attn_bwd(flag, q, k, v, o, do, st, ws), axis=1)
        qg_parts.append(tn(n1all, tg).astype(BF))
        qbg_parts.append(jnp.sum(tg.astype(F32), axis=0))
        n1g = n1g + nt(tg, qw[ph])
    qg_own = reduce_batch(reduce_cross(qg_parts))

    ng = rows_of(n1g, p)
    for r in range(1, g):
        ng = ng + rot(rows_of(n1g, (p - r) % g).astype(BF), r).astype(F32)
    e = ng * gain1
    back = e - jnp.mean(e, axis=1, keepdims=True) - xh1 * jnp.mean(e * xh1, axis=1, keepdims=True)
    input_grad = (mg + r1 * back).astype(BF)

    shard_w = 3 * W + FS
    shard_vec = jnp.zeros((n, shard_w), F32)
    for ph in range(slots):
        owner = (me - ph * g) % n
        own_row = jnp.concatenate([qbg_parts[ph], jnp.zeros((FS,), F32)])
        shard_vec = lax.dynamic_update_slice(shard_vec, own_row[None], (owner, 0))
        for r in range(g):
            shard = (me - ph * g) % n // g * g + (p + r) % g
            shard_vec = lax.dynamic_update_slice(
                shard_vec, cols(ubg, ph * g + r, FS), (shard, 3 * W)
            )
    small = jnp.concatenate(
        [shard_vec.reshape(-1), vg[:4].reshape(-1), jnp.sum(ng * xh1, 0), jnp.sum(ng, 0)]
    ).reshape(-1, 128)
    bit = 1
    while bit < n:
        small = small + lax.ppermute(small, "head", [(i, i ^ bit) for i in range(n)])
        bit *= 2
    bit = 1
    while bit < nb:
        small = small + flip(small, bit)
        bit *= 2
    small = small.reshape(-1)
    shard_sum = lax.dynamic_slice(small[: n * shard_w].reshape(n, shard_w), (me, 0), (1, shard_w))[0]
    vs = small[n * shard_w :].reshape(6, D)
    return (
        layer_out,
        input_grad,
        vs[4],
        vs[5],
        qg_own.astype(F32).reshape(D, 3, W),
        shard_sum[: 3 * W].reshape(3, W),
        dg_own[FS:].astype(F32),
        vs[0],
        vs[1],
        vs[2],
        ug_own.astype(F32),
        shard_sum[3 * W :],
        dg_own[:FS].astype(F32),
        vs[3],
    )


def solution(mesh):
    rows = P(("batch", "head"), None)
    return jax.shard_map(
        per_device,
        mesh=mesh,
        in_specs=(
            rows,
            P(),
            P(),
            P(None, None, "head"),
            P(None, "head"),
            P("head", None),
            P(),
            P(),
            P(),
            P(None, "head"),
            P("head"),
            P("head", None),
            P(),
            rows,
            P("batch"),
        ),
        out_specs=(
            rows,
            rows,
            P(),
            P(),
            P(None, None, "head"),
            P(None, "head"),
            P("head", None),
            P(),
            P(),
            P(),
            P(None, "head"),
            P("head"),
            P("head", None),
            P(),
        ),
        check_vma=False,
    )
```

```python
import functools

import jax
import jax.numpy as jnp
from jax import lax
from jax.experimental import pallas as pl
from jax.experimental.pallas import tpu as pltpu
from jax.sharding import PartitionSpec as P

HD = 64
SHORT = 1024
F32 = jnp.float32
BF = jnp.bfloat16
LOG2E = 1.4426950408889634
GELU_C = 0.7978845608028654
CHUNK = 512
PAD = 32
VROWS = 16
MIB = 1024 * 1024
FWD_MIB = 16
BWD_MIB = 16
FFN_MIB = 24
BACK_MIB = 14
SUM_MIB = 8
S = jax.ShapeDtypeStruct
ANY = pl.BlockSpec(memory_space=pl.ANY)
SMEM = pl.BlockSpec(memory_space=pltpu.SMEM)
VMEM = pl.BlockSpec(memory_space=pltpu.VMEM)


def nt(a, b):
    return lax.dot_general(a, b, (((1,), (1,)), ((), ())), preferred_element_type=F32)


def nn(a, b):
    return lax.dot_general(a, b, (((1,), (0,)), ((), ())), preferred_element_type=F32)


def tn(a, b):
    return lax.dot_general(a, b, (((0,), (0,)), ((), ())), preferred_element_type=F32)


def head_mask(shape, h):
    lane = lax.broadcasted_iota(jnp.int32, shape, len(shape) - 1)
    return (lane >= h * HD) & (lane < (h + 1) * HD)


def lane_sum(e):
    width = min(128, e.shape[1])
    total = e[:, :width]
    for i in range(1, e.shape[1] // width):
        total = total + e[:, i * width : (i + 1) * width]
    return total


def ln_stats(v):
    c = v - jnp.mean(v, axis=1, keepdims=True)
    r = lax.rsqrt(jnp.mean(c * c, axis=1, keepdims=True) + 1e-5)
    return c * r, r


def load_rows(ref, start, count):
    return ref[pl.ds(pl.multiple_of(start, count), count), :]


def kept(shape, dtype):
    return pltpu.VMEM(shape, dtype)


def in_hbm(x):
    return pltpu.with_memory_space_constraint(x, pltpu.HBM)


def params(mib):
    return pltpu.CompilerParams(vmem_limit_bytes=mib * MIB)


def qkv_kernel(g, norm, step, s_ref, *rest):
    rows = rest[:g]
    rest = rest[g:]
    if norm:
        gain_ref, bias_ref = (rest[0].at[pl.ds(i, 1), :] for i in range(2))
        rest = rest[1:]
    w_ref, q_ref, k_ref, v_ref, wt_ref = rest[:5]
    norm_out = rest[5:]
    R, D = rows[0].shape
    W = q_ref.shape[1]
    wt_ref[...] = w_ref[0:D, :].astype(F32).T.astype(BF)
    for r in range(g):
        base = (s_ref[1] + r) % g * R
        for j in range(0, R, step):
            a = rows[r][j : j + step, :]
            if norm:
                xh, _ = ln_stats(a.astype(F32))
                a = (xh * gain_ref[...].astype(F32) + bias_ref[...].astype(F32)).astype(BF)
                norm_out[r][j : j + step, :] = a
            t = (nn(a, w_ref[0:D, :]) + w_ref[D : D + 1, :].astype(F32)).astype(BF)
            at = pl.ds(pl.multiple_of(base + j, step), step)
            q_ref[at, :] = t[:, :W]
            k_ref[at, :] = t[:, W : 2 * W]
            v_ref[at, :] = t[:, 2 * W :]


def project(scal, rows, w, vecs=None, step=256):
    g = len(rows)
    R, D = rows[0].shape
    W = w.shape[1] // 3
    L = g * R
    norm = vecs is not None
    args = [*rows] + ([vecs] if norm else []) + [w]
    res = pl.pallas_call(
        functools.partial(qkv_kernel, g, norm, step),
        in_specs=[SMEM] + [VMEM] * len(args),
        out_specs=[VMEM] * (4 + g * norm),
        out_shape=[kept((L, W), BF)] * 3 + [kept((3 * W, D), BF)] + [kept((R, D), BF)] * (g * norm),
        compiler_params=params(12),
        cost_estimate=pl.CostEstimate(flops=6 * L * D * W, bytes_accessed=4 * L * D, transcendentals=0),
        name="norm_qkv" if norm else "qkv",
    )(scal, *args)
    return res[:3], res[3], res[4:]


def fwd_kernel(bq, bk, nh, W, L, g, s_ref, q_ref, k_ref, v_ref, *rest):
    nck = L // CHUNK
    o_ref, st_ref = rest[:2]
    w_refs = rest[2 : 2 + nck]
    sends = rest[2 + nck :]
    nq = L // bq
    R = L // g
    long = s_ref[0] > 0
    place = s_ref[1]

    def scaled_queries(at):
        qf = q_ref[at, :].astype(F32) * (LOG2E * HD**-0.5)
        hi = qf.astype(BF)
        lo = (qf - hi.astype(F32)).astype(BF)
        qs = []
        z = jnp.zeros_like(hi)
        for h in range(nh):
            m = head_mask(hi.shape, h)
            qs.append(jnp.concatenate([jnp.where(m, hi, z), jnp.where(m, lo, z)], axis=1))
        return qs

    def keys(at):
        kt = k_ref[at, :]
        return jnp.concatenate([kt, kt], axis=1)

    def values(at):
        vt = v_ref[at, :]
        z = jnp.zeros_like(vt)
        return [jnp.where(head_mask(vt.shape, h), vt, z) for h in range(nh)]

    def finish(at, acc, sums, bases):
        lane = lax.broadcasted_iota(jnp.int32, (bq, 128), 1)
        st = jnp.ones((bq, 128), F32)
        out = jnp.zeros((bq, W), F32)
        for h in range(nh):
            inv = 1.0 / sums[h]
            st = jnp.where(lane == h, inv, st)
            if bases is not None:
                st = jnp.where(lane == 8 + h, bases[h], st)
            out = jnp.where(head_mask(out.shape, h), acc * inv, out)
        st_ref[at, :] = st
        o_ref[at, :] = out.astype(BF)

    sq_r = lax.broadcasted_iota(jnp.int32, (bk, bk), 0)
    sq_c = lax.broadcasted_iota(jnp.int32, (bk, bk), 1)

    def fast(c, lo_blk):
        at = slice(c * bq, (c + 1) * bq)
        qs = scaled_queries(at)
        nr = bq // bk
        acc = [None] * nr
        ls = [[None] * nr for _ in range(nh)]
        for kb in range(lo_blk, (c + 1) * nr):
            base = kb * bk
            first = max(0, kb - c * nr)
            r0 = first * bk
            kt = keys(slice(base, base + bk))
            chunk = base // CHUNK
            top_row = c * bq - chunk * CHUNK
            wl = []
            for h in range(nh):
                s = nt(qs[h][r0:, :], kt)
                if base >= c * bq:
                    top = jnp.where(sq_c <= sq_r, s[:bk, :], 0.0)
                    s = top if r0 + bk == bq else jnp.concatenate([top, s[bk:, :]], axis=0)
                e = jnp.exp2(jnp.abs(s))
                x = (e - 1.0).astype(BF)
                wv = jnp.where(s.astype(BF) < 0, -x, x)
                t = lane_sum(e)
                for r in range(first, nr):
                    tr = t[(r - first) * bk : (r - first + 1) * bk, :]
                    ls[h][r] = tr if ls[h][r] is None else ls[h][r] + tr
                w_refs[chunk][h, top_row + r0 : top_row + bq, base % CHUNK : base % CHUNK + bk] = wv
                wl.append(wv)
            vcat = jnp.concatenate(values(slice(base, base + bk)), axis=0)
            res = nn(jnp.concatenate(wl, axis=1), vcat)
            for r in range(first, nr):
                part = res[(r - first) * bk : (r - first + 1) * bk, :]
                acc[r] = part if acc[r] is None else acc[r] + part
        row = lax.broadcasted_iota(jnp.int32, (bq, 1), 0)
        extra = (bk - 1 - row % bk).astype(F32)
        sums = [
            jnp.sum(jnp.concatenate(ls[h], axis=0), axis=1, keepdims=True) - extra
            for h in range(nh)
        ]
        finish(at, jnp.concatenate(acc, axis=0), sums, None)

    for c in range(nq):
        if c * bq < SHORT:
            fast(c, 0)
        else:
            pl.when(long)(functools.partial(fast, c, 0))
            pl.when(~long)(functools.partial(fast, c, SHORT // bk))

    lane = lax.broadcasted_iota(jnp.int32, (L, 128), 1)
    smallest = jnp.min(jnp.where(lane < nh, st_ref[...], 1.0))

    def slow(qi, _):
        at = pl.ds(pl.multiple_of(qi * bq, bq), bq)
        qs = scaled_queries(at)
        lo_blk = jnp.where(long | (qi * bq < SHORT), 0, SHORT // bk)
        hi_blk = (qi + 1) * (bq // bk)
        rows = lax.broadcasted_iota(jnp.int32, (bq, bk), 0) + qi * bq
        cols = lax.broadcasted_iota(jnp.int32, (bq, bk), 1)

        def scores(h, kb):
            kt = keys(pl.ds(pl.multiple_of(kb * bk, bk), bk))
            return nt(qs[h], kt), cols + kb * bk <= rows

        def top_step(kb, tops):
            new = []
            for h in range(nh):
                s, vis = scores(h, kb)
                mag = jnp.where(vis, jnp.abs(s), 0.0)
                new.append(jnp.maximum(tops[h], jnp.max(mag, axis=1, keepdims=True)))
            return tuple(new)

        tops = lax.fori_loop(lo_blk, hi_blk, top_step, (jnp.zeros((bq, 1), F32),) * nh)
        bases = [jnp.exp2(-t) for t in tops]

        def step(kb, carry):
            acc, sums = carry
            new = []
            vs = values(pl.ds(pl.multiple_of(kb * bk, bk), bk))
            for h in range(nh):
                s, vis = scores(h, kb)
                e = jnp.where(vis, jnp.exp2(jnp.abs(s) - tops[h]), 0.0)
                wv = jnp.where(s < 0, bases[h] - e, e - bases[h])
                wv = jnp.where(vis & (s != 0), wv, 0.0).astype(BF)
                new.append(sums[h] + jnp.sum(e, axis=1, keepdims=True))
                acc = acc + nn(wv, vs[h])
                for j in range(nck):

                    @pl.when(kb // (CHUNK // bk) == j)
                    def _():
                        top_row = pl.multiple_of(qi * bq - j * CHUNK, bq)
                        off = pl.multiple_of((kb % (CHUNK // bk)) * bk, bk)
                        w_refs[j][h, pl.ds(top_row, bq), pl.ds(off, bk)] = wv

            return acc, tuple(new)

        acc, sums = lax.fori_loop(
            lo_blk,
            hi_blk,
            step,
            (jnp.zeros((bq, W), F32), (jnp.zeros((bq, 1), F32),) * nh),
        )
        finish(at, acc, sums, bases)
        return 0

    @pl.when(smallest < 1e-25)
    def _():
        lax.fori_loop(0, nq, slow, 0)

    for r in range(1, g):
        sends[r - 1][...] = load_rows(o_ref, (place + r) % g * R, R)


def attn_fwd(scal, q, k, v, g, bq=512, bk=256):
    L, W = q.shape
    nh = W // HD
    nck = L // CHUNK
    res = pl.pallas_call(
        functools.partial(fwd_kernel, bq, bk, nh, W, L, g),
        in_specs=[SMEM] + [VMEM] * 3,
        out_specs=[VMEM] * (2 + nck + g - 1),
        out_shape=[kept((L, W), BF), kept((L, 128), F32)]
        + [kept((nh, L - j * CHUNK, CHUNK), BF) for j in range(nck)]
        + [S((L // g, W), BF)] * (g - 1),
        compiler_params=params(FWD_MIB),
        cost_estimate=pl.CostEstimate(
            flops=8 * L * L * W, bytes_accessed=2 * nh * L * L, transcendentals=nh * L * L
        ),
        name="attn_fwd",
    )(scal, q, k, v)
    return res[0], res[1], res[2 : 2 + nck], res[2 + nck :]


def bwd_kernel(heads, bq, bk, g, s_ref, q_ref, k_ref, v_ref, st_ref, o_ref, wt_ref, *rest):
    L, W = q_ref.shape
    nck = L // CHUNK
    nh = len(heads)
    do_refs = rest[:g]
    w_refs = rest[g : g + nck]
    n1_refs = rest[g + nck : 2 * g + nck]
    t_ref, gq_ref, vec_ref, bias_ref, dka, dva = rest[2 * g + nck :]
    D = wt_ref.shape[1]
    nq = L // bq
    R = L // g
    long = s_ref[0] > 0
    place = s_ref[1]
    sq_r = lax.broadcasted_iota(jnp.int32, (bk, bk), 0)
    sq_c = lax.broadcasted_iota(jnp.int32, (bk, bk), 1)

    def body(c, lo_blk):
        nr = bq // bk
        rep = bk // 128
        at = slice(c * bq, (c + 1) * bq)
        tri = jnp.where(sq_c <= sq_r, 1.0, 0.0).astype(BF)
        st = st_ref[at, :]
        rows = []
        for lo in range(c * bq, (c + 1) * bq, min(bq, R)):
            here = slice(lo % R, lo % R + min(bq, R))
            x = do_refs[0][here, :]
            for r in range(1, g):
                x = jnp.where(lo // R == (place + r) % g, do_refs[r][here, :], x)
            rows.append(x)
        do_all = jnp.concatenate(rows, axis=0).astype(F32)
        of = o_ref[at, :].astype(F32)
        qt_all = q_ref[at, :].astype(F32).T.astype(BF)
        deltas, e0s, dos, dots, qts = [], [], [], [], []
        for h in heads:
            m = head_mask((bq, W), h)
            do = jnp.where(m, do_all * st[:, h : h + 1], 0.0)
            delta = jnp.sum(do * of, axis=1, keepdims=True)
            deltas.append(jnp.concatenate([jnp.broadcast_to(delta, (bq, 128)).astype(BF)] * rep, 1))
            e0 = jnp.broadcast_to(st[:, 8 + h : 9 + h], (bq, 128)).astype(BF)
            e0s.append(jnp.concatenate([e0] * rep, 1))
            dos.append(do.astype(BF))
            dots.append(do.T[h * HD : (h + 1) * HD, :].astype(BF))
            qts.append(qt_all[h * HD : (h + 1) * HD, :])
        dq = [[None] * nr for _ in heads]
        for kb in range(lo_blk, (c + 1) * nr):
            base = kb * bk
            first = max(0, kb - c * nr)
            r0 = first * bk
            chunk = base // CHUNK
            top_row = c * bq - chunk * CHUNK
            cols = slice(base, base + bk)
            for i, h in enumerate(heads):
                wv = w_refs[chunk][h, top_row + r0 : top_row + bq, base % CHUNK : base % CHUNK + bk]
                wg = nt(dos[i][r0:, :], v_ref[cols, :]).astype(BF)
                dl = deltas[i][r0:, :]
                e = e0s[i][r0:, :]
                if base >= c * bq:
                    top = e[:bk, :] * tri
                    e = top if r0 + bk == bq else jnp.concatenate([top, e[bk:, :]], axis=0)
                zero = jnp.zeros_like(wv)
                d = jnp.where(wv < 0, -dl, jnp.where(wv > 0, dl, zero))
                gr = (jnp.abs(wv) + e) * (wg - d)
                dv = nn(dots[i][:, r0:], wv)
                dk = nn(qts[i][:, r0:], gr)
                own = slice(i * HD, (i + 1) * HD)
                if base >= c * bq:
                    dva[own, cols] = dv
                    dka[own, cols] = dk
                else:
                    dva[own, cols] += dv
                    dka[own, cols] += dk
                res = nn(gr, k_ref[cols, :])
                for r in range(first, nr):
                    part = res[(r - first) * bk : (r - first + 1) * bk, :]
                    dq[i][r] = part if dq[i][r] is None else dq[i][r] + part
        for i, h in enumerate(heads):
            x = jnp.concatenate(dq[i], axis=0) * (HD**-0.5)
            t_ref[3 * i * HD : (3 * i + 1) * HD, at] = x.T[h * HD : (h + 1) * HD, :].astype(BF)

    for c in range(nq):
        if c * bq < SHORT:
            body(c, 0)
        else:
            pl.when(long)(functools.partial(body, c, 0))
            pl.when(~long)(functools.partial(body, c, SHORT // bk))

    for i in range(nh):
        own = slice(i * HD, (i + 1) * HD)
        t_ref[(3 * i + 1) * HD : (3 * i + 2) * HD, :] = (dka[own, :] * (HD**-0.5)).astype(BF)
        t_ref[(3 * i + 2) * HD : (3 * i + 3) * HD, :] = dva[own, :].astype(BF)
    gq = jnp.zeros((3 * nh * HD, D), F32)
    for r in range(g):
        start = pl.multiple_of((place + r) % g * R, R)
        gq = gq + nn(t_ref[:, pl.ds(start, R)], n1_refs[r][...])
    gq_ref[...] = gq.astype(BF)
    bias_ref[...] = nt(jnp.ones((VROWS, L), BF), t_ref[...])
    bias = jnp.sum(t_ref[...].astype(F32), axis=1, keepdims=True)
    wt = jnp.concatenate(
        [wt_ref[i * W + h * HD : i * W + (h + 1) * HD, :] for h in heads for i in range(3)], axis=0
    ).astype(F32)
    vec_ref[...] = jnp.concatenate(
        [
            jnp.sum(wt * gq, axis=0, keepdims=True),
            jnp.sum(wt * bias, axis=0, keepdims=True),
            jnp.zeros((6, D), F32),
        ],
        axis=0,
    )


def attn_bwd(scal, heads, q, k, v, st, o, wt, dos, ws, n1s, bq=1024, bk=256):
    L, W = q.shape
    g = len(dos)
    D = wt.shape[1]
    rows = 3 * HD * len(heads)
    args = [q, k, v, st, o, wt, *dos, *ws, *n1s]
    return pl.pallas_call(
        functools.partial(bwd_kernel, heads, bq, bk, g),
        in_specs=[SMEM] + [VMEM] * len(args),
        out_specs=[VMEM] * 4,
        out_shape=[kept((rows, L), BF), kept((rows, D), BF), kept((8, D), F32), kept((VROWS, rows), F32)],
        scratch_shapes=[pltpu.VMEM((HD * len(heads), L), F32)] * 2,
        compiler_params=params(BWD_MIB),
        cost_estimate=pl.CostEstimate(
            flops=16 * L * L * HD * len(heads), bytes_accessed=2 * L * L, transcendentals=0
        ),
        name="attn_bwd",
    )(scal, *args)


def ffn_kernel(g, slots, halves, s_ref, *refs):
    m = g * slots
    it = iter(refs)

    def take(count):
        return [next(it) for _ in range(count)]

    x_hbm, cot_hbm = take(2)
    od_hbm, up_hbm = take(m), take(m)
    o_refs, att_refs = take(slots), take(m - slots)
    (vecs_ref,) = take(1)
    ob_ref, gain_ref, bias_ref, db_ref = (vecs_ref.at[pl.ds(i, 1), :] for i in range(2, 6))
    lo_ref, mg_ref = take(2)
    atg_refs = take(m)
    ug_refs, dg_refs = take(g), take(g)
    xs, cots, ows, ups, dns, mids, n2, n2t, cott, nacc, sems = take(11)
    R, D = x_hbm.shape
    FS = up_hbm[0].shape[1]
    W = od_hbm[0].shape[0] - FS
    oacc = mg_ref
    step = R // halves
    blocks = [slice(j, j + step) for j in range(0, R, step)]

    def copy(i, a, b):
        return pltpu.make_async_copy(a, b, sems.at[i])

    first = [copy(0, x_hbm, xs), copy(1, cot_hbm, cots)]
    first += [copy(2 + i, od_hbm[i].at[pl.ds(0, W)], ows.at[i]) for i in range(m)]

    def weights(i):
        return [
            copy(2 + m + i % 2, up_hbm[i], ups.at[i % 2]),
            copy(4 + m + i % 2, od_hbm[i].at[pl.ds(W, FS)], dns.at[i % 2]),
        ]

    for c in first + weights(0):
        c.start()

    def vec(ref):
        return ref[...].astype(F32)

    def att_rows(at):
        rows = pl.ds(pl.multiple_of(s_ref[1] * R + at.start, step), step)
        return jnp.concatenate([o[rows, :] for o in o_refs] + [a[at, :] for a in att_refs], axis=1)

    for c in first:
        c.wait()
    ow = ows[...].reshape(m * W, D)
    for at in blocks:
        mid = xs[at, :].astype(F32) + nn(att_rows(at), ow) + vec(ob_ref)
        mids[at, :] = mid
        oacc[at, :] = mid + vec(db_ref)
        xh, _ = ln_stats(mid)
        y = xh * vec(gain_ref) + vec(bias_ref)
        n2[at, :] = y.astype(BF)
        n2t[:, at] = y.T.astype(BF)
        cott[:, at] = cots[at, :].astype(F32).T.astype(BF)

    for i in range(m):
        r, ph = i // slots, i % slots
        for c in weights(i):
            c.wait()
        if i + 1 < m:
            for c in weights(i + 1):
                c.start()
        up = ups[i % 2, 0:D, :]
        dn = dns[i % 2]
        ub = ups[i % 2, D : D + 1, :].astype(F32)
        ug = dg = ubg = None
        for at in blocks:
            u = nn(n2[at, :], up) + ub
            ag = nt(cots[at, :], dn)
            u2 = u * u
            t = jnp.tanh(u * (GELU_C + (GELU_C * 0.044715) * u2))
            hh = 0.5 + 0.5 * t
            act = (u * hh).astype(BF)
            slope = hh + u * (0.5 - 0.5 * t * t) * (GELU_C + (3 * GELU_C * 0.044715) * u2)
            pgf = ag * slope
            pg = pgf.astype(BF)
            oacc[at, :] += nn(act, dn)
            back = nt(pg, up)
            if i == 0:
                nacc[at, :] = back
            else:
                nacc[at, :] += back
            bsum = jnp.sum(pgf, axis=0, keepdims=True)
            gu = nn(n2t[:, at], pg)
            gd = nn(cott[:, at], act)
            ubg = bsum if ubg is None else ubg + bsum
            ug = gu if ug is None else ug + gu
            dg = gd if dg is None else dg + gd
        ug_refs[r][ph, 0:D, :] = ug.astype(BF)
        ug_refs[r][ph, D:, :] = jnp.broadcast_to(ubg, (PAD, FS)).astype(BF)
        dg_refs[r][ph, 0:FS, :] = dg.T.astype(BF)

    sums = [None] * 4
    og = None
    for at in blocks:
        lo_ref[at, :] = oacc[at, :].astype(BF)
        xh, rs = ln_stats(mids[at, :])
        ng = nacc[at, :]
        e = ng * vec(gain_ref)
        cf = cots[at, :].astype(F32)
        back = e - jnp.mean(e, axis=1, keepdims=True) - xh * jnp.mean(e * xh, axis=1, keepdims=True)
        mg = cf + rs * back
        mg_ref[at, :] = mg
        bg = mg.astype(BF)
        atg = nt(bg, ow).astype(BF)
        for i in range(m):
            atg_refs[i][at, :] = atg[:, i * W : (i + 1) * W]
        gr = tn(att_rows(at), bg)
        og = gr if og is None else og + gr
        for i, a in enumerate((bg.astype(F32), ng * xh, ng, cf)):
            a = jnp.sum(a, axis=0, keepdims=True)
            sums[i] = a if sums[i] is None else sums[i] + a
    og = og.astype(BF)
    vecs = jnp.concatenate(sums + [jnp.zeros((4, D), F32)], axis=0)
    hi = vecs.astype(BF).astype(F32)
    both = jnp.concatenate([hi, vecs - hi], axis=0).astype(BF)
    for i in range(m):
        r, ph = i // slots, i % slots
        dg_refs[r][ph, FS : FS + W, :] = og[i * W : (i + 1) * W, :]
        dg_refs[r][ph, FS + W :, :] = both


def ffn(scal, g, slots, x, cot, od, up, os, att, vecs, halves=2):
    R, D = x.shape
    FS = up[0].shape[1]
    W = od[0].shape[0] - FS
    m = g * slots
    outs = (
        [S((R, D), BF), kept((R, D), F32)]
        + [kept((R, W), BF)] * m
        + [kept((slots, D + PAD, FS), BF)] * g
        + [kept((slots, FS + W + VROWS, D), BF)] * g
    )
    hbm = [in_hbm(a) for a in (x, cot, *od, *up)]
    res = pl.pallas_call(
        functools.partial(ffn_kernel, g, slots, halves),
        in_specs=[SMEM] + [ANY] * (2 + 2 * m) + [VMEM] * (m + 1),
        out_specs=[VMEM] * len(outs),
        out_shape=outs,
        scratch_shapes=[
            pltpu.VMEM((R, D), BF),
            pltpu.VMEM((R, D), BF),
            pltpu.VMEM((m, W, D), BF),
            pltpu.VMEM((2, D + PAD, FS), BF),
            pltpu.VMEM((2, FS, D), BF),
            pltpu.VMEM((R, D), F32),
            pltpu.VMEM((R, D), BF),
            pltpu.VMEM((D, R), BF),
            pltpu.VMEM((D, R), BF),
            pltpu.VMEM((R, D), F32),
            pltpu.SemaphoreType.DMA((6 + m,)),
        ],
        compiler_params=params(FFN_MIB),
        cost_estimate=pl.CostEstimate(
            flops=12 * R * D * FS * m, bytes_accessed=16 * R * D, transcendentals=R * FS * m
        ),
        name="ffn",
    )(scal, *hbm, *os, *att, vecs)
    return res[0], res[1], res[2 : 2 + m], res[2 + m : 2 + m + g], res[2 + m + g :]


def back_kernel(g, heads, last, rel, s_ref, *refs):
    count = len(heads)
    t_refs, wt_refs = refs[:count], refs[count : 2 * count]
    rest = refs[2 * count :]
    out_ref = rest[-1]
    R = out_ref.shape[0]
    start = pl.multiple_of((s_ref[1] + rel) % g * R, R)
    t = jnp.concatenate([a[:, pl.ds(start, R)] for a in t_refs], axis=0)
    wt = []
    for own, ref in zip(heads, wt_refs):
        W = ref.shape[0] // 3
        wt += [ref[i * W + h * HD : i * W + (h + 1) * HD, :] for h in own for i in range(3)]
    n1g = tn(t, jnp.concatenate(wt, axis=0))
    if not last:
        out_ref[...] = n1g.astype(BF)
        return
    x_ref, mg_ref, vecs_ref = rest[g - 1 : g + 2]
    for a in rest[: g - 1]:
        n1g = n1g + a[...].astype(F32)
    xh, rs = ln_stats(x_ref[...].astype(F32))
    e = n1g * vecs_ref[0:1, :].astype(F32)
    back = e - jnp.mean(e, axis=1, keepdims=True) - xh * jnp.mean(e * xh, axis=1, keepdims=True)
    out_ref[...] = (mg_ref[...] + rs * back).astype(BF)


def row_back(scal, g, rel, heads, ts, wts, R, last=None):
    D = wts[0].shape[1]
    args = [*ts, *wts] + ([] if last is None else [*last[0], *last[1:]])
    return pl.pallas_call(
        functools.partial(back_kernel, g, heads, last is not None, rel),
        in_specs=[SMEM] + [VMEM] * len(args),
        out_specs=VMEM,
        out_shape=kept((R, D), BF) if last is None else S((R, D), BF),
        compiler_params=params(BACK_MIB),
        cost_estimate=pl.CostEstimate(
            flops=2 * R * D * sum(t.shape[0] for t in ts), bytes_accessed=4 * R * D, transcendentals=0
        ),
        name="row_back" if last is None else "norm_back",
    )(scal, *args)


def fuse(body, outs, scal, *args, scratch=()):
    return pl.pallas_call(
        body,
        in_specs=[SMEM] + [VMEM] * len(args),
        out_specs=[VMEM] * len(outs),
        out_shape=outs,
        scratch_shapes=list(scratch),
        compiler_params=params(SUM_MIB),
        name=body.__name__,
    )(scal, *args)


def sum_of(refs, at):
    out = refs[0][at].astype(F32)
    for a in refs[1:]:
        out = out + a[at].astype(F32)
    return out.astype(BF)


def join_vec(v):
    v = v.astype(F32)
    return v[: VROWS // 2] + v[VROWS // 2 :]


def split_vec(v):
    hi = v.astype(BF).astype(F32)
    return jnp.concatenate([hi, v - hi], axis=0).astype(BF)


def vec_of(refs, at):
    return split_vec(functools.reduce(lambda a, b: a + b, [join_vec(a[at]) for a in refs]))


def half_at(s_ref, count, mine):
    place = s_ref[2] if mine else 1 - s_ref[2]
    return pl.ds(pl.multiple_of(place * count, count), count)


def u_members(scal, parts):
    slots, rows, cols = parts[0].shape

    def sum_members(s_ref, *refs):
        ins, outs = refs[: len(parts)], refs[len(parts) :]
        for i in range(slots):
            outs[i][...] = sum_of(ins, i)

    return fuse(sum_members, [kept((rows, cols), BF)] * slots, scal, *parts)


def u_halve(scal, terms):
    rows, cols = terms[0].shape

    def sum_halves(s_ref, *refs):
        ins, (mine, other) = refs[: len(terms)], refs[len(terms) :]
        mine[...] = sum_of(ins, half_at(s_ref, rows // 2, True))
        other[...] = sum_of(ins, half_at(s_ref, rows // 2, False))

    return fuse(sum_halves, [kept((rows // 2, cols), BF)] * 2, scal, *terms)


def add_up(scal, terms, has_vec):
    rows, cols = terms[0].shape
    count = rows - VROWS if has_vec else rows

    def sum_terms(s_ref, *refs):
        ins, out = refs[: len(terms)], refs[len(terms)]
        out[0:count, :] = sum_of(ins, slice(0, count))
        if has_vec:
            out[count:, :] = vec_of(ins, slice(count, rows))

    return fuse(sum_terms, [kept((rows, cols), BF)], scal, *terms)[0]


def d_halve(scal, parts):
    slots, rows, cols = parts[0].shape
    count = (rows - VROWS) // 2

    def sum_parts(s_ref, *refs):
        ins, outs = refs[: len(parts)], refs[len(parts) :]
        vec = vec_of(ins, (0, slice(2 * count, rows)))
        for out, mine in zip(outs, (True, False)):
            at = half_at(s_ref, count, mine)
            for i in range(slots):
                out[i * count : (i + 1) * count, :] = sum_of(ins, (i, at))
            out[slots * count :, :] = vec

    return fuse(sum_parts, [kept((slots * count + VROWS, cols), BF)] * 2, scal, *parts)


def d_slots(scal, slots, terms):
    rows, cols = terms[0].shape
    count = (rows - VROWS) // slots

    def sum_slots(s_ref, *refs):
        ins, outs = refs[: len(terms)], refs[len(terms) :]
        vec = vec_of(ins, slice(slots * count, rows))
        for i in range(slots):
            outs[i][0:count, :] = sum_of(ins, slice(i * count, (i + 1) * count))
            outs[i][count:, :] = vec

    return fuse(sum_slots, [kept((count + VROWS, cols), BF)] * slots, scal, *terms)


def collect(scal, mine, other, count, splits):
    cols = mine.shape[1]

    def gather_halves(s_ref, mine_ref, other_ref, *refs):
        outs, whole = refs[:-1], refs[-1]
        whole[half_at(s_ref, count, True), :] = mine_ref[0:count, :].astype(F32)
        whole[half_at(s_ref, count, False), :] = other_ref[0:count, :].astype(F32)
        first = 0
        for out, size in zip(outs, splits):
            out[...] = whole[first : first + size, :]
            first += size

    return fuse(
        gather_halves,
        [S((a, cols), F32) for a in splits],
        scal,
        mine,
        other,
        scratch=[pltpu.VMEM((2 * count, cols), F32)],
    )


def fill_rows(ref, gs, biases):
    first = 0
    for a in gs:
        ref[first : first + a.shape[0], :] = a[...]
        first += a.shape[0]
    ref[first:, :] = jnp.zeros((ref.shape[0] - first, ref.shape[1]), BF)
    for b in biases:
        count = b.shape[1]
        for i in range(0, count, 3 * HD):
            ref[first : first + VROWS, 0 : 3 * HD] = b[:, i : i + 3 * HD].astype(BF)
            first += VROWS


def q_rows(scal, gs, biases):
    rows, cols = sum(a.shape[0] for a in gs) + PAD, gs[0].shape[1]

    def stack_rows(s_ref, *refs):
        fill_rows(refs[-1], refs[: len(gs)], refs[len(gs) : -1])

    return fuse(stack_rows, [kept((rows, cols), BF)], scal, *gs, *biases)[0]


def q_halve(scal, gs, biases, crossed, vecs):
    rows, cols = sum(a.shape[0] for a in gs) + PAD, gs[0].shape[1]
    count = rows // 2
    sizes = [len(gs), len(biases), len(crossed), len(vecs)]

    def sum_rows(s_ref, *refs):
        it = iter(refs)
        g_refs, b_refs, c_refs, v_refs = ([next(it) for _ in range(n)] for n in sizes)
        mine, other, whole = it
        fill_rows(whole, g_refs, b_refs)
        vec = split_vec(functools.reduce(lambda a, b: a + b, [v[...] for v in v_refs]))
        for out, which in ((mine, True), (other, False)):
            out[0:count, :] = sum_of([whole, *c_refs], half_at(s_ref, count, which))
            out[count:, :] = vec

    return fuse(
        sum_rows,
        [kept((count + VROWS, cols), BF)] * 2,
        scal,
        *gs,
        *biases,
        *crossed,
        *vecs,
        scratch=[pltpu.VMEM((rows, cols), BF)],
    )


def after(x, *deps):
    return lax.optimization_barrier((x,) + deps)[0]


class Chain:
    def __init__(self, steps):
        self.steps = steps
        self.result = None
        self.sent, self.got = next(steps)

    def tick(self, *deps):
        if self.result is None:
            try:
                self.sent, self.got = self.steps.send(after(self.got, *deps))
            except StopIteration as stop:
                self.result = stop.value
                self.sent = []


def vec_split(v):
    hi = lax.reduce_precision(v, 8, 7)
    return jnp.concatenate([hi, v - hi], axis=0).astype(BF)


def vec_join(v):
    half = v.shape[0] // 2
    return v[:half].astype(F32) + v[half:].astype(F32)


def per_device(
    tokens_in,
    norm1_gain,
    norm1_bias,
    qkv_weight,
    qkv_bias,
    out_weight,
    out_bias,
    norm2_gain,
    norm2_bias,
    up_weight,
    up_bias,
    down_weight,
    down_bias,
    cotangent,
    long_slot,
):
    n = lax.axis_size("head")
    nb = lax.axis_size("batch")
    me = lax.axis_index("head")
    bi = lax.axis_index("batch")
    slots = long_slot.shape[0]
    g = n // slots
    R, D = tokens_in.shape
    W = qkv_weight.shape[2]
    FS = up_weight.shape[1]
    nh = W // HD
    splits = [(h,) for h in range(nh)]
    flag = lax.dynamic_slice(long_slot, (me // g,), (1,))[0]
    scal = jnp.stack([flag, me % g, bi % 2]).astype(jnp.int32)
    vecs = jnp.stack(
        [norm1_gain, norm1_bias, out_bias, norm2_gain, norm2_bias, down_bias, out_bias, out_bias]
    )
    bits = []
    while 2 ** len(bits) < nb:
        bits.append(2 ** len(bits))

    def cross(x, r):
        return lax.ppermute(x, "head", [(i, (i + r * g) % n) for i in range(n)])

    def rot(x, r):
        return lax.ppermute(x, "head", [(i, i // g * g + (i % g - r) % g) for i in range(n)])

    def flip(x, bit):
        return lax.ppermute(x, "batch", [(i, i ^ bit) for i in range(nb)])

    def row(v):
        return v.reshape(1, -1)

    def pad(w, b):
        return jnp.concatenate([w, b, jnp.zeros((PAD - b.shape[0], w.shape[1]), w.dtype)], axis=0)

    own = [
        pad(qkv_weight.reshape(D, 3 * W), qkv_bias.reshape(1, 3 * W)),
        jnp.concatenate([out_weight, down_weight], axis=0),
        pad(up_weight, row(up_bias)),
    ]
    own[1] = after(own[1], own[0])
    own[2] = after(own[2], own[1])
    qw, odw, upw = ([a] + [cross(a, r) for r in range(1, slots)] for a in own)
    xs = [tokens_in] + [rot(tokens_in, r) for r in range(1, g)]
    xs[0] = after(xs[0], *own)

    saved = []
    att = []
    n1s = None
    for ph in range(slots):
        if ph == 0:
            qkv, wt, n1s = project(scal, xs, qw[0], vecs)
        else:
            qkv, wt, _ = project(scal, n1s, after(qw[ph], saved[-1][3]))
        o, st, ws, sends = attn_fwd(scal, *qkv, g)
        saved.append((*qkv, st, o, wt, ws))
        att.append([rot(sends[g - r - 1], r) for r in range(1, g)])
    odw, upw = ([a[0]] + [after(b, saved[-1][3]) for b in a[1:]] for a in (odw, upw))

    def pieces(a):
        return [rot(b, r) if r else b for r in range(g) for b in a]

    lo, mg, atg, ugs, dgs = ffn(
        scal,
        g,
        slots,
        tokens_in,
        cotangent,
        pieces(odw),
        pieces(upw),
        [a[4] for a in saved],
        [att[ph][r - 1] for r in range(1, g) for ph in range(slots)],
        vecs,
    )

    def members(parts):
        return [rot(parts[(g - r) % g], r) for r in range(1, g)]

    def over_batch(mat, has_vec):
        for bit in bits[1:]:
            got = yield [mat], flip(mat, bit)
            mat = add_up(scal, [mat, got], has_vec)
        return mat

    def chain_u():
        got = yield list(ugs), members(ugs)
        parts = u_members(scal, [ugs[0]] + got)
        got = yield parts[1:], [cross(parts[slots - r], slots - r) for r in range(1, slots)]
        mine, other = u_halve(scal, [parts[0]] + got)
        got = yield [mine, other], flip(other, bits[0])
        mat = yield from over_batch(add_up(scal, [mine, got], False), False)
        got = yield [mat], flip(mat, bits[0])
        return collect(scal, mat, got, mat.shape[0], (D, PAD))

    def chain_d():
        got = yield list(dgs), members(dgs)
        mine, other = d_halve(scal, [dgs[0]] + got)
        got = yield [mine, other], flip(other, bits[0])
        parts = d_slots(scal, slots, [mine, got])
        got = yield parts, [cross(parts[slots - r], slots - r) for r in range(1, slots)]
        mat = yield from over_batch(add_up(scal, [parts[0]] + got, True), True)
        got = yield [mat], flip(mat, bits[0])
        count = mat.shape[0] - VROWS
        return [*collect(scal, mat, got, count, (FS, W)), mat[count:]]

    dos = [
        [atg[ph]] + [rot(atg[(g - r) * slots + ph], r) for r in range(1, g)] for ph in range(slots)
    ]
    chains = [Chain(chain_u()), Chain(chain_d())]
    grads = {}
    crossing = {}
    dep = ()

    def q_parts(ph):
        return [a[1] for a in grads[ph]], [a[3] for a in grads[ph]]

    for ph in list(range(1, slots)) + [0]:
        q, k, v, st, o, wt, ws = saved[ph]
        grads[ph] = []
        for heads in splits:
            first = after(q, *[a for c in chains for a in c.sent], *dep)
            res = attn_bwd(scal, heads, first, k, v, st, o, wt, dos[ph], ws, n1s)
            grads[ph].append(res)
            dep = (res[1],)
            for c in chains:
                c.tick(res[1])
        if ph:
            crossing[ph] = cross(q_rows(scal, *q_parts(ph)), slots - ph)

    vecs1 = [a[2] for ph in range(slots) for a in grads[ph]]

    def chain_q():
        crossed = [crossing[ph] for ph in range(1, slots)]
        mine, other = q_halve(scal, *q_parts(0), crossed, vecs1)
        got = yield [mine, other], flip(other, bits[0])
        mat = yield from over_batch(add_up(scal, [mine, got], True), True)
        count = mat.shape[0] - VROWS
        vec = mat[count:]
        got, others = yield [mat, vec], (flip(mat, bits[0]), [cross(vec, r) for r in range(1, slots)])
        vec = vec_split(sum(vec_join(a) for a in [vec] + others))
        vec = sum(vec_join(a) for a in [vec] + [rot(vec, r) for r in range(1, g)])
        return [*collect(scal, mat, got, count, (2 * count,)), vec]

    order = [(ph, i) for ph in range(slots) for i in range(len(splits))]
    ts = [grads[ph][i][0] for ph, i in order]
    wts = [saved[ph][5] for ph, i in order]
    head_list = [splits[i] for ph, i in order]
    chains.append(Chain(chain_q()))
    sends = {}
    for r in range(1, g):
        first = after(ts[0], *[a for c in chains for a in c.sent])
        sends[r] = row_back(scal, g, r, head_list, [first] + ts[1:], wts, R)
    got = [rot(sends[(g - r) % g], r) for r in range(1, g)]
    for c in chains:
        c.tick(*sends.values())
    first = after(ts[0], *[a for c in chains for a in c.sent])
    input_grad = row_back(
        scal, g, 0, head_list, [first] + ts[1:], wts, R, (got, tokens_in, mg, vecs)
    )
    while any(c.result is None for c in chains):
        for c in chains:
            c.tick(input_grad)
    (up_grad, up_bias_grad), (down_grad, out_grad, vec2), (qf, vec1) = (c.result for c in chains)
    vec2 = vec_join(vec2)
    gain_grad = (vec1[0] - norm1_bias.astype(F32) * vec1[1]) / norm1_gain.astype(F32)
    body = nh * 3 * HD
    qkv_grad = qf[:body].reshape(nh, 3, HD, D).transpose(3, 1, 0, 2).reshape(D, 3, W)
    bias_rows = qf[body : body + nh * VROWS : VROWS, : 3 * HD]
    qkv_bias_grad = bias_rows.reshape(nh, 3, HD).transpose(1, 0, 2).reshape(3, W)
    return (
        lo,
        input_grad,
        gain_grad,
        vec1[1],
        qkv_grad,
        qkv_bias_grad,
        out_grad,
        vec2[0],
        vec2[1],
        vec2[2],
        up_grad,
        up_bias_grad[0],
        down_grad,
        vec2[3],
    )


def solution(mesh):
    rows = P(("batch", "head"), None)
    return jax.shard_map(
        per_device,
        mesh=mesh,
        in_specs=(
            rows,
            P(),
            P(),
            P(None, None, "head"),
            P(None, "head"),
            P("head", None),
            P(),
            P(),
            P(),
            P(None, "head"),
            P("head"),
            P("head", None),
            P(),
            rows,
            P("batch"),
        ),
        out_specs=(
            rows,
            rows,
            P(),
            P(),
            P(None, None, "head"),
            P(None, "head"),
            P("head", None),
            P(),
            P(),
            P(),
            P(None, "head"),
            P("head"),
            P("head", None),
            P(),
        ),
        check_vma=False,
    )
```

```python
import functools

import jax
import jax.numpy as jnp
from jax import lax
from jax.experimental import pallas as pl
from jax.experimental.pallas import tpu as pltpu
from jax.sharding import PartitionSpec as P

HD = 64
SHORT = 1024
F32 = jnp.float32
BF = jnp.bfloat16
LOG2E = 1.4426950408889634
GELU_C = 0.7978845608028654
CHUNK = 512
PAD = 64
QPAD = 32
VROWS = 16
MIB = 1024 * 1024
FWD_MIB = 11
BWD_MIB = 11
FFN_MIB = 10
BACK_MIB = 6
SUM_MIB = 3
S = jax.ShapeDtypeStruct
ANY = pl.BlockSpec(memory_space=pl.ANY)
SMEM = pl.BlockSpec(memory_space=pltpu.SMEM)
VMEM = pl.BlockSpec(memory_space=pltpu.VMEM)


def nt(a, b):
    return lax.dot_general(a, b, (((1,), (1,)), ((), ())), preferred_element_type=F32)


def nn(a, b):
    return lax.dot_general(a, b, (((1,), (0,)), ((), ())), preferred_element_type=F32)


def tn(a, b):
    return lax.dot_general(a, b, (((0,), (0,)), ((), ())), preferred_element_type=F32)


def head_mask(shape, h):
    lane = lax.broadcasted_iota(jnp.int32, shape, len(shape) - 1)
    return (lane >= h * HD) & (lane < (h + 1) * HD)


def lane_sum(e):
    width = min(128, e.shape[1])
    total = e[:, :width]
    for i in range(1, e.shape[1] // width):
        total = total + e[:, i * width : (i + 1) * width]
    return total


def ln_stats(v):
    c = v - jnp.mean(v, axis=1, keepdims=True)
    r = lax.rsqrt(jnp.mean(c * c, axis=1, keepdims=True) + 1e-5)
    return c * r, r


def as_row(ref):
    return ref[...].astype(F32).reshape(1, -1)


def load_rows(ref, start, count):
    return ref[pl.ds(pl.multiple_of(start, count), count), :]


def kept(shape, dtype):
    return pltpu.VMEM(shape, dtype)


def in_hbm(x):
    return pltpu.with_memory_space_constraint(x, pltpu.HBM)


def place_in(g):
    me = lax.axis_index("head")
    return me % g, me // g


def params(mib):
    return pltpu.CompilerParams(vmem_limit_bytes=mib * MIB)


def qkv_kernel(g, norm, step, *rest):
    place, group = place_in(g)
    if norm:
        s_ref, *rest = rest
        vec_in, rest = rest[:6], rest[6:]
    rows, rest = rest[:g], rest[g:]
    pack_ref, q_ref, k_ref, v_ref = rest[:4]
    R, D = rows[0].shape
    W = q_ref.shape[1]
    if norm:
        flag_ref, vec_ref = rest[4:6]
        norm_out = rest[6:]
        flag_ref[...] = jnp.full((8, 128), (s_ref[group] > 0).astype(F32))
        vec_ref[...] = jnp.concatenate([as_row(a) for a in vec_in] + [jnp.zeros((2, D), F32)], axis=0)
    wt = pack_ref[0 : 3 * W, :]
    bias = pack_ref[4 * W : 4 * W + VROWS, :].astype(F32)[0:1, 0 : 3 * W]
    for r in range(g):
        base = (place + r) % g * R
        for j in range(0, R, step):
            a = rows[r][j : j + step, :]
            if norm:
                xh, _ = ln_stats(a.astype(F32))
                a = (xh * vec_ref[0:1, :] + vec_ref[1:2, :]).astype(BF)
                norm_out[r][j : j + step, :] = a
            t = (nt(a, wt) + bias).astype(BF)
            at = pl.ds(pl.multiple_of(base + j, step), step)
            q_ref[at, :] = t[:, :W]
            k_ref[at, :] = t[:, W : 2 * W]
            v_ref[at, :] = t[:, 2 * W :]


def project(rows, packed, long_slot=None, vecs=(), step=256):
    g = len(rows)
    R, D = rows[0].shape
    W = (packed.shape[0] - VROWS) // 4
    L = g * R
    norm = long_slot is not None
    args = [*vecs, *rows, packed]
    outs = [kept((L, W), BF)] * 3
    if norm:
        outs += [kept((8, 128), F32), kept((8, D), F32)] + [kept((R, D), BF)] * g
    res = pl.pallas_call(
        functools.partial(qkv_kernel, g, norm, step),
        in_specs=[SMEM] * norm + [VMEM] * len(args),
        out_specs=[VMEM] * len(outs),
        out_shape=outs,
        compiler_params=params(4),
        cost_estimate=pl.CostEstimate(flops=1000, bytes_accessed=1000, transcendentals=0),
        name="norm_qkv" if norm else "qkv",
    )(*([long_slot] if norm else []), *args)
    return res[:3], res[3:]


def fwd_kernel(bq, bk, nh, W, L, g, s_ref, q_ref, k_ref, v_ref, *rest):
    nck = L // CHUNK
    o_ref, st_ref = rest[:2]
    w_refs = rest[2 : 2 + nck]
    sends = rest[2 + nck :]
    nq = L // bq
    R = L // g
    place, _ = place_in(g)
    long = jnp.max(s_ref[...]) > 0

    def scaled_queries(at):
        qf = q_ref[at, :].astype(F32) * (LOG2E * HD**-0.5)
        hi = qf.astype(BF)
        lo = (qf - hi.astype(F32)).astype(BF)
        qs = []
        z = jnp.zeros_like(hi)
        for h in range(nh):
            m = head_mask(hi.shape, h)
            qs.append(jnp.concatenate([jnp.where(m, hi, z), jnp.where(m, lo, z)], axis=1))
        return qs

    def keys(at):
        kt = k_ref[at, :]
        return jnp.concatenate([kt, kt], axis=1)

    def values(at):
        vt = v_ref[at, :]
        z = jnp.zeros_like(vt)
        return [jnp.where(head_mask(vt.shape, h), vt, z) for h in range(nh)]

    def finish(at, acc, sums, bases):
        lane = lax.broadcasted_iota(jnp.int32, (bq, 128), 1)
        st = jnp.ones((bq, 128), F32)
        out = jnp.zeros((bq, W), F32)
        for h in range(nh):
            inv = 1.0 / sums[h]
            st = jnp.where(lane == h, inv, st)
            if bases is not None:
                st = jnp.where(lane == 8 + h, bases[h], st)
            out = jnp.where(head_mask(out.shape, h), acc * inv, out)
        st_ref[at, :] = st
        o_ref[at, :] = out.astype(BF)

    sq_r = lax.broadcasted_iota(jnp.int32, (bk, bk), 0)
    sq_c = lax.broadcasted_iota(jnp.int32, (bk, bk), 1)

    def fast(c, lo_blk):
        at = slice(c * bq, (c + 1) * bq)
        qs = scaled_queries(at)
        nr = bq // bk
        acc = [None] * nr
        ls = [[None] * nr for _ in range(nh)]
        for kb in range(lo_blk, (c + 1) * nr):
            base = kb * bk
            first = max(0, kb - c * nr)
            r0 = first * bk
            kt = keys(slice(base, base + bk))
            chunk = base // CHUNK
            top_row = c * bq - chunk * CHUNK
            wl = []
            for h in range(nh):
                s = nt(qs[h][r0:, :], kt)
                if base >= c * bq:
                    top = jnp.where(sq_c <= sq_r, s[:bk, :], 0.0)
                    s = top if r0 + bk == bq else jnp.concatenate([top, s[bk:, :]], axis=0)
                e = jnp.exp2(jnp.abs(s))
                x = (e - 1.0).astype(BF)
                wv = jnp.where(s.astype(BF) < 0, -x, x)
                t = lane_sum(e)
                for r in range(first, nr):
                    tr = t[(r - first) * bk : (r - first + 1) * bk, :]
                    ls[h][r] = tr if ls[h][r] is None else ls[h][r] + tr
                w_refs[chunk][h, top_row + r0 : top_row + bq, base % CHUNK : base % CHUNK + bk] = wv
                wl.append(wv)
            vcat = jnp.concatenate(values(slice(base, base + bk)), axis=0)
            res = nn(jnp.concatenate(wl, axis=1), vcat)
            for r in range(first, nr):
                part = res[(r - first) * bk : (r - first + 1) * bk, :]
                acc[r] = part if acc[r] is None else acc[r] + part
        row = lax.broadcasted_iota(jnp.int32, (bq, 1), 0)
        extra = (bk - 1 - row % bk).astype(F32)
        sums = [
            jnp.sum(jnp.concatenate(ls[h], axis=0), axis=1, keepdims=True) - extra
            for h in range(nh)
        ]
        finish(at, jnp.concatenate(acc, axis=0), sums, None)

    for c in range(nq):
        if c * bq < SHORT:
            fast(c, 0)
        else:
            pl.when(long)(functools.partial(fast, c, 0))
            pl.when(~long)(functools.partial(fast, c, SHORT // bk))

    lane = lax.broadcasted_iota(jnp.int32, (L, 128), 1)
    smallest = jnp.min(jnp.where(lane < nh, st_ref[...], 1.0))

    def slow(qi, _):
        at = pl.ds(pl.multiple_of(qi * bq, bq), bq)
        qs = scaled_queries(at)
        lo_blk = jnp.where(long | (qi * bq < SHORT), 0, SHORT // bk)
        hi_blk = (qi + 1) * (bq // bk)
        rows = lax.broadcasted_iota(jnp.int32, (bq, bk), 0) + qi * bq
        cols = lax.broadcasted_iota(jnp.int32, (bq, bk), 1)

        def scores(h, kb):
            kt = keys(pl.ds(pl.multiple_of(kb * bk, bk), bk))
            return nt(qs[h], kt), cols + kb * bk <= rows

        def top_step(kb, tops):
            new = []
            for h in range(nh):
                s, vis = scores(h, kb)
                mag = jnp.where(vis, jnp.abs(s), 0.0)
                new.append(jnp.maximum(tops[h], jnp.max(mag, axis=1, keepdims=True)))
            return tuple(new)

        tops = lax.fori_loop(lo_blk, hi_blk, top_step, (jnp.zeros((bq, 1), F32),) * nh)
        bases = [jnp.exp2(-t) for t in tops]

        def step(kb, carry):
            acc, sums = carry
            new = []
            vs = values(pl.ds(pl.multiple_of(kb * bk, bk), bk))
            for h in range(nh):
                s, vis = scores(h, kb)
                e = jnp.where(vis, jnp.exp2(jnp.abs(s) - tops[h]), 0.0)
                wv = jnp.where(s < 0, bases[h] - e, e - bases[h])
                wv = jnp.where(vis & (s != 0), wv, 0.0).astype(BF)
                new.append(sums[h] + jnp.sum(e, axis=1, keepdims=True))
                acc = acc + nn(wv, vs[h])
                for j in range(nck):

                    @pl.when(kb // (CHUNK // bk) == j)
                    def _():
                        top_row = pl.multiple_of(qi * bq - j * CHUNK, bq)
                        off = pl.multiple_of((kb % (CHUNK // bk)) * bk, bk)
                        w_refs[j][h, pl.ds(top_row, bq), pl.ds(off, bk)] = wv

            return acc, tuple(new)

        acc, sums = lax.fori_loop(
            lo_blk,
            hi_blk,
            step,
            (jnp.zeros((bq, W), F32), (jnp.zeros((bq, 1), F32),) * nh),
        )
        finish(at, acc, sums, bases)
        return 0

    @pl.when(smallest < 1e-25)
    def _():
        lax.fori_loop(0, nq, slow, 0)

    for r in range(1, g):
        sends[r - 1][...] = load_rows(o_ref, (place + r) % g * R, R)


def attn_fwd(flag, q, k, v, g, bq=512, bk=256):
    L, W = q.shape
    nh = W // HD
    nck = L // CHUNK
    res = pl.pallas_call(
        functools.partial(fwd_kernel, bq, bk, nh, W, L, g),
        in_specs=[VMEM] * 4,
        out_specs=[VMEM] * (2 + nck + g - 1),
        out_shape=[kept((L, W), BF), kept((L, 128), F32)]
        + [kept((nh, L - j * CHUNK, CHUNK), BF) for j in range(nck)]
        + [S((L // g, W), BF)] * (g - 1),
        compiler_params=params(FWD_MIB),
        cost_estimate=pl.CostEstimate(flops=1000, bytes_accessed=1000, transcendentals=0),
        name="attn_fwd",
    )(flag, q, k, v)
    return res[0], res[1], res[2 : 2 + nck], res[2 + nck :]


def bwd_kernel(h, bk, g, second, s_ref, q_ref, k_ref, v_ref, st_ref, o_ref, wt_ref, *rest):
    L, W = q_ref.shape
    nck = L // CHUNK
    do_refs = rest[:g]
    w_refs = rest[g : g + nck]
    n1_refs = rest[g + nck : 2 * g + nck]
    rest = rest[2 * g + nck :]
    if second:
        tq_ref, dk_ref, dv_ref, t_ref, gq_ref, vec_ref, bias_ref = rest
    else:
        tq_ref, dk_ref, dv_ref = rest
    D = wt_ref.shape[1]
    R = L // g
    place, _ = place_in(g)
    long = jnp.max(s_ref[...]) > 0
    sq_r = lax.broadcasted_iota(jnp.int32, (bk, bk), 0)
    sq_c = lax.broadcasted_iota(jnp.int32, (bk, bk), 1)
    lanes = slice(h * HD, (h + 1) * HD)
    bq = SHORT
    scale = HD**-0.5
    q_at, k_at, v_at = (slice(i * HD, (i + 1) * HD) for i in range(3))

    def body(c, lo_blk):
        nr = bq // bk
        rep = bk // 128
        at = slice(c * bq, (c + 1) * bq)
        tri = jnp.where(sq_c <= sq_r, 1.0, 0.0).astype(BF)
        st = st_ref[at, :]
        rows = []
        for lo in range(c * bq, (c + 1) * bq, min(bq, R)):
            here = slice(lo % R, lo % R + min(bq, R))
            x = do_refs[0][here, :]
            for r in range(1, g):
                x = jnp.where(lo // R == (place + r) % g, do_refs[r][here, :], x)
            rows.append(x)
        do = jnp.concatenate(rows, axis=0).astype(F32)
        do = jnp.where(head_mask((bq, W), h), do * st[:, h : h + 1], 0.0)
        delta = jnp.sum(do * o_ref[at, :].astype(F32), axis=1, keepdims=True)
        delta = jnp.concatenate([jnp.broadcast_to(delta, (bq, 128)).astype(BF)] * rep, 1)
        e0 = jnp.broadcast_to(st[:, 8 + h : 9 + h], (bq, 128)).astype(BF)
        e0 = jnp.concatenate([e0] * rep, 1)
        do_b = do.astype(BF)
        do_t = do.T[lanes, :].astype(BF)
        q_t = q_ref[at, :].astype(F32).T[lanes, :].astype(BF)
        dq = [None] * nr
        for kb in range(lo_blk, (c + 1) * nr):
            base = kb * bk
            first = max(0, kb - c * nr)
            r0 = first * bk
            chunk = base // CHUNK
            top_row = c * bq - chunk * CHUNK
            cols = slice(base, base + bk)
            wv = w_refs[chunk][h, top_row + r0 : top_row + bq, base % CHUNK : base % CHUNK + bk]
            wg = nt(do_b[r0:, :], v_ref[cols, :]).astype(BF)
            dl = delta[r0:, :]
            e = e0[r0:, :]
            if base >= c * bq:
                top = e[:bk, :] * tri
                e = top if r0 + bk == bq else jnp.concatenate([top, e[bk:, :]], axis=0)
            zero = jnp.zeros_like(wv)
            d = jnp.where(wv < 0, -dl, jnp.where(wv > 0, dl, zero))
            gr = (jnp.abs(wv) + e) * (wg - d)
            dv = nn(do_t[:, r0:], wv)
            dk = nn(q_t[:, r0:], gr)
            if not second:
                dv_ref[:, cols] = dv
                dk_ref[:, cols] = dk
            else:
                if base < SHORT:
                    dv = dv + dv_ref[:, cols]
                    dk = dk + dk_ref[:, cols]
                t_ref[k_at, cols] = (dk * scale).astype(BF)
                t_ref[v_at, cols] = dv.astype(BF)
            res = nn(gr, k_ref[cols, :])
            for r in range(first, nr):
                part = res[(r - first) * bk : (r - first + 1) * bk, :]
                dq[r] = part if dq[r] is None else dq[r] + part
        dq = (jnp.concatenate(dq, axis=0) * scale).T[lanes, :].astype(BF)
        if second:
            t_ref[q_at, at] = dq
        else:
            tq_ref[...] = dq

    if not second:
        body(0, 0)
        return
    t_ref[q_at, 0:SHORT] = tq_ref[...]
    pl.when(long)(functools.partial(body, 1, 0))

    @pl.when(~long)
    def _():
        t_ref[k_at, 0:SHORT] = (dk_ref[...] * scale).astype(BF)
        t_ref[v_at, 0:SHORT] = dv_ref[...].astype(BF)
        body(1, SHORT // bk)

    gq = jnp.zeros((3 * HD, D), F32)
    for r in range(g):
        start = pl.multiple_of((place + r) % g * R, R)
        gq = gq + nn(t_ref[:, pl.ds(start, R)], n1_refs[r][...])
    gq_ref[...] = gq.astype(BF)
    bias_ref[...] = nt(jnp.ones((VROWS, L), BF), t_ref[...])
    bias = jnp.sum(t_ref[...].astype(F32), axis=1, keepdims=True)
    wt = jnp.concatenate([wt_ref[i * W + h * HD : i * W + (h + 1) * HD, :] for i in range(3)], axis=0)
    wt = wt.astype(F32)
    vec_ref[...] = jnp.concatenate(
        [
            jnp.sum(wt * gq, axis=0, keepdims=True),
            jnp.sum(wt * bias, axis=0, keepdims=True),
            jnp.zeros((6, D), F32),
        ],
        axis=0,
    )


def attn_bwd(flag, h, q, k, v, st, o, wt, dos, ws, n1s, half=None, bk=256):
    L, W = q.shape
    g = len(dos)
    D = wt.shape[1]
    rows = 3 * HD
    second = half is not None
    args = [q, k, v, st, o, wt, *dos, *ws, *n1s, *(half or [])]
    if second:
        outs = [kept((rows, L), BF), kept((rows, D), BF), kept((8, D), F32), kept((VROWS, rows), F32)]
    else:
        outs = [kept((HD, SHORT), BF)] + [kept((HD, SHORT), F32)] * 2
    return pl.pallas_call(
        functools.partial(bwd_kernel, h, bk, g, second),
        in_specs=[VMEM] * (1 + len(args)),
        out_specs=[VMEM] * len(outs),
        out_shape=outs,
        compiler_params=params(BWD_MIB),
        cost_estimate=pl.CostEstimate(flops=1000, bytes_accessed=1000, transcendentals=0),
        name="attn_bwd",
    )(flag, *args)


def ffn_kernel(g, slots, halves, todo, first, last, *refs):
    m = g * slots
    place, _ = place_in(g)
    it = iter(refs)

    def take(count):
        return [next(it) for _ in range(count)]

    ow_refs, up_refs, dn_refs = take(m if first or last else len(todo)), take(len(todo)), take(len(todo))
    (vec_ref,) = take(1)
    if first or last:
        o_refs, att_refs = take(slots), take(m - slots)
    if first:
        x_ref, cot_in = take(2)
    else:
        mids, n2, n2t, cots, cott, oacc_in, nacc_in = take(7)
    if first:
        mids, n2, n2t, cots, cott = take(5)
    if last:
        lo_ref, oacc = take(2)
        atg_refs, og_refs = take(m), take(m)
        (nacc,) = take(1)
        oacc_out = oacc
    else:
        oacc_out, nacc = take(2)
    ug_refs, dg_refs = take(len(todo)), take(len(todo))
    R, D = cots.shape
    FS = up_refs[0].shape[1]
    W = (ow_refs[0].shape[0] - VROWS) // 4
    step = R // halves
    blocks = [slice(j, j + step) for j in range(0, R, step)]

    def vec(i):
        return vec_ref[2 + i : 3 + i, :]

    def att_rows(at):
        rows = pl.ds(pl.multiple_of(place * R + at.start, step), step)
        return jnp.concatenate([o[rows, :] for o in o_refs] + [a[at, :] for a in att_refs], axis=1)

    if first or last:
        ow = jnp.concatenate([a[3 * W : 4 * W, :] for a in ow_refs], axis=0)
    if first:
        cots[...] = cot_in[...]
        for at in blocks:
            mid = x_ref[at, :].astype(F32) + nn(att_rows(at), ow) + vec(0)
            mids[at, :] = mid
            xh, _ = ln_stats(mid)
            y = xh * vec(1) + vec(2)
            n2[at, :] = y.astype(BF)
            n2t[:, at] = y.T.astype(BF)
            cott[:, at] = cots[at, :].astype(F32).T.astype(BF)

    for j, i in enumerate(todo):
        up = up_refs[j][...]
        dn = dn_refs[j][...]
        bias_ref = ow_refs[i if first or last else j]
        ub = bias_ref[4 * W : 4 * W + VROWS, :].astype(F32)[1:2, 0:FS]
        ug = dg = ubg = None
        for at in blocks:
            u = nn(n2[at, :], up) + ub
            ag = nt(cots[at, :], dn)
            u2 = u * u
            t = jnp.tanh(u * (GELU_C + (GELU_C * 0.044715) * u2))
            hh = 0.5 + 0.5 * t
            act = (u * hh).astype(BF)
            slope = hh + u * (0.5 - 0.5 * t * t) * (GELU_C + (3 * GELU_C * 0.044715) * u2)
            pgf = ag * slope
            pg = pgf.astype(BF)
            out = nn(act, dn)
            back = nt(pg, up)
            if j > 0:
                oacc_out[at, :] += out
                nacc[at, :] += back
            elif first:
                oacc_out[at, :] = mids[at, :] + vec(3) + out
                nacc[at, :] = back
            else:
                oacc_out[at, :] = oacc_in[at, :] + out
                nacc[at, :] = nacc_in[at, :] + back
            bsum = jnp.sum(pgf, axis=0, keepdims=True)
            gu = nn(n2t[:, at], pg)
            gd = nn(cott[:, at], act)
            ubg = bsum if ubg is None else ubg + bsum
            ug = gu if ug is None else ug + gu
            dg = gd if dg is None else dg + gd
        ug_refs[j][0:D, :] = ug.astype(BF)
        ug_refs[j][D:, :] = jnp.broadcast_to(ubg, (PAD, FS)).astype(BF)
        dg_refs[j][...] = dg.T.astype(BF)

    if not last:
        return
    mg_ref = oacc
    sums = [None] * 4
    og = None
    for at in blocks:
        lo_ref[at, :] = oacc[at, :].astype(BF)
        xh, rs = ln_stats(mids[at, :])
        ng = nacc[at, :]
        e = ng * vec(1)
        cf = cots[at, :].astype(F32)
        back = e - jnp.mean(e, axis=1, keepdims=True) - xh * jnp.mean(e * xh, axis=1, keepdims=True)
        mg = cf + rs * back
        mg_ref[at, :] = mg
        bg = mg.astype(BF)
        atg = nt(bg, ow).astype(BF)
        for i in range(m):
            atg_refs[i][at, :] = atg[:, i * W : (i + 1) * W]
        gr = tn(att_rows(at), bg)
        og = gr if og is None else og + gr
        for i, a in enumerate((bg.astype(F32), ng * xh, ng, cf)):
            a = jnp.sum(a, axis=0, keepdims=True)
            sums[i] = a if sums[i] is None else sums[i] + a
    og = og.astype(BF)
    both = jnp.concatenate(sums + [jnp.zeros((4, D), F32)], axis=0)
    hi = both.astype(BF).astype(F32)
    both = jnp.concatenate([hi, both - hi], axis=0).astype(BF)
    for i in range(m):
        og_refs[i][0:W, :] = og[i * W : (i + 1) * W, :]
        og_refs[i][W:, :] = both


def ffn(g, slots, todo, ow, up, dn, vecs, attended, start=None, state=None, last=False, halves=2):
    first = state is None
    R, D = (start[0] if first else state[0]).shape
    FS = up[0].shape[1]
    W = (ow[0].shape[0] - VROWS) // 4
    m = g * slots
    args = [*(ow if first or last else [ow[i] for i in todo])]
    args += [up[i] for i in todo] + [dn[i] for i in todo] + [vecs]
    if first or last:
        args += attended
    args += start if first else state
    outs = []
    if first:
        outs += [kept((R, D), F32), kept((R, D), BF), kept((D, R), BF), kept((R, D), BF), kept((D, R), BF)]
    if last:
        outs += [S((R, D), BF), kept((R, D), F32)] + [kept((R, W), BF)] * m + [kept((W + VROWS, D), BF)] * m
        outs += [kept((R, D), F32)]
    else:
        outs += [kept((R, D), F32)] * 2
    total_at = (1, 2 + 2 * m) if last else (5, 6) if first else (0, 1)
    alias = {} if first else {len(args) - 2: total_at[0], len(args) - 1: total_at[1]}
    outs += [kept((D + PAD, FS), BF)] * len(todo) + [kept((FS, D), BF)] * len(todo)
    res = pl.pallas_call(
        functools.partial(ffn_kernel, g, slots, halves, todo, first, last),
        in_specs=[VMEM] * len(args),
        out_specs=[VMEM] * len(outs),
        out_shape=outs,
        input_output_aliases=alias,
        compiler_params=params(FFN_MIB),
        cost_estimate=pl.CostEstimate(flops=1000, bytes_accessed=1000, transcendentals=0),
        name="ffn",
    )(*args)
    ugs, dgs = res[len(res) - 2 * len(todo) : len(res) - len(todo)], res[len(res) - len(todo) :]
    return res[: len(res) - 2 * len(todo)], dict(zip(todo, ugs)), dict(zip(todo, dgs))


def back_kernel(g, heads, last, rel, *refs):
    place, _ = place_in(g)
    count = len(heads)
    t_refs, wt_refs = refs[:count], refs[count : 2 * count]
    rest = refs[2 * count :]
    out_ref = rest[-1]
    R = out_ref.shape[0]
    start = pl.multiple_of((place + rel) % g * R, R)
    t = jnp.concatenate([a[:, pl.ds(start, R)] for a in t_refs], axis=0)
    wt = []
    for own, ref in zip(heads, wt_refs):
        W = (ref.shape[0] - VROWS) // 4
        wt += [ref[i * W + h * HD : i * W + (h + 1) * HD, :] for h in own for i in range(3)]
    n1g = tn(t, jnp.concatenate(wt, axis=0))
    if not last:
        out_ref[...] = n1g.astype(BF)
        return
    x_ref, mg_ref, vec_ref = rest[g - 1 : g + 2]
    for a in rest[: g - 1]:
        n1g = n1g + a[...].astype(F32)
    xh, rs = ln_stats(x_ref[...].astype(F32))
    e = n1g * vec_ref[0:1, :]
    back = e - jnp.mean(e, axis=1, keepdims=True) - xh * jnp.mean(e * xh, axis=1, keepdims=True)
    out_ref[...] = (mg_ref[...] + rs * back).astype(BF)


def row_back(g, rel, heads, ts, wts, R, last=None):
    D = wts[0].shape[1]
    args = [*ts, *wts] + ([] if last is None else [*last[0], *last[1:]])
    return pl.pallas_call(
        functools.partial(back_kernel, g, heads, last is not None, rel),
        in_specs=[VMEM] * len(args),
        out_specs=VMEM,
        out_shape=kept((R, D), BF) if last is None else S((R, D), BF),
        compiler_params=params(BACK_MIB),
        cost_estimate=pl.CostEstimate(flops=1000, bytes_accessed=1000, transcendentals=0),
        name="row_back" if last is None else "norm_back",
    )(*args)


def fuse(body, outs, *args, scratch=()):
    return pl.pallas_call(
        body,
        in_specs=[VMEM] * len(args),
        out_specs=[VMEM] * len(outs),
        out_shape=outs,
        scratch_shapes=list(scratch),
        compiler_params=params(SUM_MIB),
        name=body.__name__,
    )(*args)


def sum_of(refs, at):
    out = refs[0][at].astype(F32)
    for a in refs[1:]:
        out = out + a[at].astype(F32)
    return out.astype(BF)


def join_vec(v):
    v = v.astype(F32)
    return v[: VROWS // 2] + v[VROWS // 2 :]


def split_vec(v):
    hi = v.astype(BF).astype(F32)
    return jnp.concatenate([hi, v - hi], axis=0).astype(BF)


def vec_of(refs, at):
    return split_vec(functools.reduce(lambda a, b: a + b, [join_vec(a[at]) for a in refs]))


def pack_weights(qkv_t, out_weight, qkv_bias, up_bias):
    rows, D = qkv_t.shape
    W = out_weight.shape[0]

    def pack(qt_ref, ow_ref, qb_ref, ub_ref, out):
        out[0:rows, :] = qt_ref[...]
        out[rows : rows + W, :] = ow_ref[...]
        qb = qb_ref[...].astype(F32)
        qb = jnp.concatenate([qb[i : i + 1, :] for i in range(3)], axis=1)
        lines = [qb, as_row(ub_ref), jnp.zeros((VROWS - 2, D), F32)]
        lines = [jnp.pad(a, ((0, 0), (0, D - a.shape[1]))) for a in lines]
        out[rows + W :, :] = jnp.concatenate(lines, axis=0).astype(BF)

    return fuse(pack, [kept((rows + W + VROWS, D), BF)], qkv_t, out_weight, qkv_bias, up_bias)[0]


def half_at(bit, count, mine):
    place = lax.axis_index("batch") // 2**bit % 2
    place = place if mine else 1 - place
    return pl.ds(pl.multiple_of(place * count, count), count)


def add_up(terms, has_vec=False):
    rows, cols = terms[0].shape
    count = rows - VROWS if has_vec else rows

    def sum_terms(*refs):
        ins, out = refs[: len(terms)], refs[len(terms)]
        out[0:count, :] = sum_of(ins, slice(0, count))
        if has_vec:
            out[count:, :] = vec_of(ins, slice(count, rows))

    return fuse(sum_terms, [kept((rows, cols), BF)], *terms)[0]


def halve(bit, terms, has_vec=False):
    rows, cols = terms[0].shape
    count = (rows - VROWS if has_vec else rows) // 2

    def sum_halves(*refs):
        ins, outs = refs[: len(terms)], refs[len(terms) :]
        for out, mine in zip(outs, (True, False)):
            out[0:count, :] = sum_of(ins, half_at(bit, count, mine))
            if has_vec:
                out[count:, :] = vec_of(ins, slice(2 * count, rows))

    return fuse(sum_halves, [kept((count + VROWS * has_vec, cols), BF)] * 2, *terms)


def stack_sums(downs, outs_):
    fs, cols = downs[0].shape
    rows = fs + outs_[0].shape[0]

    def sum_pieces(*refs):
        ins, out = refs[:-1], refs[-1]
        out[0:fs, :] = sum_of(ins[: len(downs)], slice(0, fs))
        out[fs : rows - VROWS, :] = sum_of(ins[len(downs) :], slice(0, rows - fs - VROWS))
        out[rows - VROWS :, :] = vec_of(ins[len(downs) :], slice(rows - fs - VROWS, rows - fs))

    return fuse(sum_pieces, [kept((rows, cols), BF)], *downs, *outs_)[0]


def join(bit, mine, other, count):
    def join_halves(mine_ref, other_ref, out):
        out[half_at(bit, count, True), :] = mine_ref[0:count, :]
        out[half_at(bit, count, False), :] = other_ref[0:count, :]

    return fuse(join_halves, [kept((2 * count, mine.shape[1]), BF)], mine, other)[0]


def collect(mine, other, count, splits):
    cols = mine.shape[1]

    def gather_halves(mine_ref, other_ref, *refs):
        outs, whole = refs[:-1], refs[-1]
        whole[half_at(0, count, True), :] = mine_ref[0:count, :].astype(F32)
        whole[half_at(0, count, False), :] = other_ref[0:count, :].astype(F32)
        first = 0
        for out, size in zip(outs, splits):
            out[...] = whole[first : first + size, :]
            first += size

    return fuse(
        gather_halves,
        [S((a, cols), F32) for a in splits],
        mine,
        other,
        scratch=[pltpu.VMEM((2 * count, cols), F32)],
    )


def fill_rows(ref, g_ref, bias_ref):
    rows = g_ref.shape[0]
    ref[0:rows, :] = g_ref[...]
    ref[rows:, :] = jnp.zeros((ref.shape[0] - rows, ref.shape[1]), BF)
    ref[rows : rows + VROWS, 0 : bias_ref.shape[1]] = bias_ref[...].astype(BF)


def q_rows(gq, bias):
    def stack_rows(g_ref, bias_ref, out):
        fill_rows(out, g_ref, bias_ref)

    return fuse(stack_rows, [kept((gq.shape[0] + QPAD, gq.shape[1]), BF)], gq, bias)[0]


def q_halve(gq, bias, crossed, vecs):
    rows, cols = gq.shape[0] + QPAD, gq.shape[1]
    count = rows // 2
    extra = VROWS if vecs else 0

    def sum_rows(g_ref, bias_ref, *refs):
        c_refs, v_refs = refs[: len(crossed)], refs[len(crossed) : len(crossed) + len(vecs)]
        mine, other, whole = refs[-3:]
        fill_rows(whole, g_ref, bias_ref)
        for out, which in ((mine, True), (other, False)):
            out[0:count, :] = sum_of([whole, *c_refs], half_at(0, count, which))
            if vecs:
                vec = functools.reduce(lambda a, b: a + b, [v[...] for v in v_refs])
                out[count:, :] = split_vec(vec)

    return fuse(
        sum_rows,
        [kept((count + extra, cols), BF)] * 2,
        gq,
        bias,
        *crossed,
        *vecs,
        scratch=[pltpu.VMEM((rows, cols), BF)],
    )


def after(x, *deps):
    return lax.optimization_barrier((x,) + deps)[0]


class Chain:
    def __init__(self, steps):
        self.steps = steps
        self.result = None
        self.sent, self.got = next(steps)

    def tick(self, *deps):
        if self.result is None:
            try:
                self.sent, self.got = self.steps.send(after(self.got, *deps))
            except StopIteration as stop:
                self.result = stop.value
                self.sent = []


def vec_split(v):
    hi = lax.reduce_precision(v, 8, 7)
    return jnp.concatenate([hi, v - hi], axis=0).astype(BF)


def vec_join(v):
    half = v.shape[0] // 2
    return v[:half].astype(F32) + v[half:].astype(F32)


def per_device(
    tokens_in,
    norm1_gain,
    norm1_bias,
    qkv_weight,
    qkv_bias,
    out_weight,
    out_bias,
    norm2_gain,
    norm2_bias,
    up_weight,
    up_bias,
    down_weight,
    down_bias,
    cotangent,
    long_slot,
):
    n = lax.axis_size("head")
    nb = lax.axis_size("batch")
    slots = long_slot.shape[0]
    g = n // slots
    R, D = tokens_in.shape
    W = qkv_weight.shape[2]
    FS = up_weight.shape[1]
    nh = W // HD
    bits = []
    while 2 ** len(bits) < nb:
        bits.append(2 ** len(bits))

    def cross(x, r):
        return lax.ppermute(x, "head", [(i, (i + r * g) % n) for i in range(n)])

    def rot(x, r):
        return lax.ppermute(x, "head", [(i, i // g * g + (i % g - r) % g) for i in range(n)])

    def flip(x, bit):
        return lax.ppermute(x, "batch", [(i, i ^ bit) for i in range(nb)])

    def exchanged(a):
        return [a] + [cross(a, r) for r in range(1, slots)]

    xs = [tokens_in] + [rot(tokens_in, r) for r in range(1, g)]
    qkv_t = qkv_weight.transpose(1, 2, 0).reshape(3 * W, D)
    packed = exchanged(pack_weights(qkv_t, out_weight, qkv_bias, up_bias))
    small = [norm1_gain, norm1_bias, out_bias, norm2_gain, norm2_bias, down_bias]
    qkv, (flag, vecs, *n1s) = project([after(xs[0], packed[0])] + xs[1:], packed[0], long_slot, small)

    saved = []
    att = []
    for ph in range(slots):
        if ph:
            qkv, _ = project(n1s, after(packed[ph], saved[-1][3]))
        first = qkv[0] if ph == 0 else after(qkv[0], upw[0], dnw[0])
        o, st, ws, sends = attn_fwd(flag, first, *qkv[1:], g)
        saved.append((*qkv, st, o, packed[ph], ws))
        att.append([rot(sends[g - r - 1], r) for r in range(1, g)])
        if ph == 0:
            upw = exchanged(after(up_weight, st))
            dnw = exchanged(after(down_weight, st))
    oww = [packed[0]] + [after(b, saved[-1][3]) for b in packed[1:]]

    def pieces(a):
        return [rot(b, r) if r else b for r in range(g) for b in a]

    ow = pieces(oww)
    up = [upw[0]] + [None] * (g * slots - 1)
    dn = [dnw[0]] + [None] * (g * slots - 1)
    attended = [a[4] for a in saved] + [att[ph][r - 1] for r in range(1, g) for ph in range(slots)]

    def at(r, ph):
        return r * slots + ph

    def members(parts):
        return [rot(parts[(g - r) % g], r) for r in range(1, g)]

    def over_batch(terms, has_vec):
        mine, other = halve(1, terms, has_vec)
        got = yield [mine, other], flip(other, bits[1])
        mat = add_up([mine, got], has_vec)
        for bit in bits[2:]:
            got = yield [mat], flip(mat, bit)
            mat = add_up([mat, got], has_vec)
        got = yield [mat], flip(mat, bits[1])
        count = mat.shape[0] - VROWS * has_vec
        whole = join(1, mat, got, count)
        return (whole, mat[count:]) if has_vec else whole

    ug, dg = {}, {}

    def chain_u():
        others = range(1, slots)
        got = yield [ug[at(r, ph)] for r in range(1, g) for ph in others], [
            [rot(ug[at((g - r) % g, ph)], r) for r in range(1, g)] for ph in others
        ]
        sums = [add_up([ug[at(0, ph)]] + a) for ph, a in zip(others, got)]
        got = yield sums, [cross(sums[slots - r - 1], slots - r) for r in others]
        mine, other = halve(0, [ug[at(0, 0)]] + near + got)
        got = yield [mine, other], flip(other, bits[0])
        mat = yield from over_batch([mine, got], False)
        got = yield [mat], flip(mat, bits[0])
        return collect(mat, got, mat.shape[0], (D, PAD))

    def chain_d():
        got = yield list(dg.values()) + list(og), [
            [[rot(b, r) for b in (dg[at((g - r) % g, ph)], og[at((g - r) % g, ph)])] for r in range(1, g)]
            for ph in range(slots)
        ]
        sums = [
            stack_sums([dg[at(0, ph)]] + [a[0] for a in got[ph]],
                [og[at(0, ph)]] + [a[1] for a in got[ph]],
            )
            for ph in range(slots)
        ]
        got = yield sums, [cross(sums[slots - r], slots - r) for r in range(1, slots)]
        mine, other = halve(0, [sums[0]] + got, True)
        got = yield [mine, other], flip(other, bits[0])
        mat, vec = yield from over_batch([mine, got], True)
        got = yield [mat], flip(mat, bits[0])
        return [*collect(mat, got, mat.shape[0], (FS, W)), vec]

    def part(todo, **more):
        out, new_ug, new_dg = ffn(g, slots, todo, ow, up, dn, vecs, attended, **more)
        ug.update(new_ug)
        dg.update(new_dg)
        return out

    out = part([at(0, 0)], start=[tokens_in, cotangent])
    state = out
    upw, dnw = ([a[0]] + [after(b, out[5]) for b in a[1:]] for a in (upw, dnw))
    up, dn = pieces(upw), pieces(dnw)
    far = [at(r, ph) for r in range(1, g) for ph in range(1, slots)]
    out = part(far, state=state)
    state = [*state[:5], *out]
    u = Chain(chain_u())
    state[5] = after(state[5], *u.sent)
    out = part([at(0, ph) for ph in range(1, slots)], state=state)
    state = [*state[:5], *out]
    u.tick(out[0])
    state[5] = after(state[5], *u.sent)
    out = part([at(r, 0) for r in range(1, g)], state=state, last=True)
    m = g * slots
    lo, mg, atg, og = out[0], out[1], out[2 : 2 + m], out[2 + m : 2 + 2 * m]
    dos = [
        [atg[ph]] + [rot(atg[(g - r) * slots + ph], r) for r in range(1, g)] for ph in range(slots)
    ]
    near = [rot(ug[at((g - r) % g, 0)], r) for r in range(1, g)]
    chains = {"u": u, "d": Chain(chain_d())}
    plan = ["d", "u", "", "ud", "u", "d", "ud", "ud"]
    grads = {}
    crossing = {}
    done = 0

    def sent():
        return [a for c in chains.values() for a in c.sent]

    def advance(*deps):
        nonlocal done
        for name, chain in chains.items():
            if name[0] == "q" or done >= len(plan) or name in plan[done]:
                chain.tick(*deps)
        done += 1

    def chain_q(h):
        res = grads[0, h]
        vecs1 = [grads[key][2] for key in grads] if h == nh - 1 else []
        crossed = [crossing[ph, h] for ph in range(1, slots)]
        mine, other = q_halve(res[1], res[3], crossed, vecs1)
        has_vec = bool(vecs1)
        got = yield [mine, other], flip(other, bits[0])
        mat = add_up([mine, got], has_vec)
        for bit in bits[1:]:
            got = yield [mat], flip(mat, bit)
            mat = add_up([mat, got], has_vec)
        if not has_vec:
            got = yield [mat], flip(mat, bits[0])
            return collect(mat, got, mat.shape[0], (2 * mat.shape[0],))
        count = mat.shape[0] - VROWS
        vec = mat[count:]
        got, others = yield [mat, vec], (flip(mat, bits[0]), [cross(vec, r) for r in range(1, slots)])
        vec = vec_split(sum(vec_join(a) for a in [vec] + others))
        vec = sum(vec_join(a) for a in [vec] + [rot(vec, r) for r in range(1, g)])
        return [*collect(mat, got, count, (2 * count,)), vec]

    dep = ()
    for ph in list(range(1, slots)) + [0]:
        q, k, v, st, o, pk, ws = saved[ph]
        for h in range(nh):
            args = [k, v, st, o, pk, dos[ph], ws, n1s]
            half = attn_bwd(flag, h, after(q, *sent(), *dep), *args)
            advance(half[0])
            res = attn_bwd(flag, h, after(q, *sent(), half[0]), *args, half)
            grads[ph, h] = res
            dep = (res[1],)
            advance(res[1])
            if ph:
                crossing[ph, h] = cross(q_rows(res[1], res[3]), slots - ph)
            else:
                chains["q%d" % h] = Chain(chain_q(h))

    order = [(ph, h) for ph in range(slots) for h in range(nh)]
    ts = [grads[key][0] for key in order]
    pks = [saved[ph][5] for ph, h in order]
    head_list = [(h,) for ph, h in order]
    sends = {}
    for r in range(1, g):
        sends[r] = row_back(g, r, head_list, [after(ts[0], *sent())] + ts[1:], pks, R)
    got = [rot(sends[(g - r) % g], r) for r in range(1, g)]
    input_grad = row_back(g, 0, head_list, ts, pks, R, (got, tokens_in, mg, vecs))
    dep = [input_grad]
    while any(c.result is None for c in chains.values()):
        for c in list(chains.values())[::-1]:
            c.tick(*dep)
            dep = c.sent[:1] or dep
    results = {name: c.result for name, c in chains.items()}
    (up_grad, up_bias_grad), (down_grad, out_grad, vec2) = results["u"], results["d"]
    qs = [results["q%d" % h] for h in range(nh)]
    vec1 = qs[-1][1]
    qf = [a[0] for a in qs]
    vec2 = vec_join(vec2)
    gain_grad = (vec1[0] - norm1_bias.astype(F32) * vec1[1]) / norm1_gain.astype(F32)
    qkv_grad = jnp.concatenate([a[: 3 * HD].reshape(3, HD, D) for a in qf], axis=1).transpose(2, 0, 1)
    qkv_bias_grad = jnp.concatenate([a[3 * HD, : 3 * HD].reshape(3, HD) for a in qf], axis=1)
    return (
        lo,
        input_grad,
        gain_grad,
        vec1[1],
        qkv_grad,
        qkv_bias_grad,
        out_grad,
        vec2[0],
        vec2[1],
        vec2[2],
        up_grad,
        up_bias_grad[0],
        down_grad,
        vec2[3],
    )


def solution(mesh):
    rows = P(("batch", "head"), None)
    return jax.shard_map(
        per_device,
        mesh=mesh,
        in_specs=(
            rows,
            P(),
            P(),
            P(None, None, "head"),
            P(None, "head"),
            P("head", None),
            P(),
            P(),
            P(),
            P(None, "head"),
            P("head"),
            P("head", None),
            P(),
            rows,
            P("batch"),
        ),
        out_specs=(
            rows,
            rows,
            P(),
            P(),
            P(None, None, "head"),
            P(None, "head"),
            P("head", None),
            P(),
            P(),
            P(),
            P(None, "head"),
            P("head"),
            P("head", None),
            P(),
        ),
        check_vma=False,
    )
```

```python
import functools

import jax
import jax.numpy as jnp
from jax import lax
from jax.experimental import pallas as pl
from jax.experimental.pallas import tpu as pltpu
from jax.sharding import PartitionSpec as P

HD = 64
SHORT = 1024
F32 = jnp.float32
BF = jnp.bfloat16
LOG2E = 1.4426950408889634
GELU_C = 0.7978845608028654
CHUNK = 512
PAD = 64
QPAD = 32
VROWS = 16
MIB = 1024 * 1024
FWD_MIB = 11
BWD_MIB = 11
FFN_MIB = 10
BACK_MIB = 6
SUM_MIB = 3
SCALE = 0.5
S = jax.ShapeDtypeStruct
ANY = pl.BlockSpec(memory_space=pl.ANY)
SMEM = pl.BlockSpec(memory_space=pltpu.SMEM)
VMEM = pl.BlockSpec(memory_space=pltpu.VMEM)


def nt(a, b):
    return lax.dot_general(a, b, (((1,), (1,)), ((), ())), preferred_element_type=F32)


def nn(a, b):
    return lax.dot_general(a, b, (((1,), (0,)), ((), ())), preferred_element_type=F32)


def tn(a, b):
    return lax.dot_general(a, b, (((0,), (0,)), ((), ())), preferred_element_type=F32)


def head_mask(shape, h):
    lane = lax.broadcasted_iota(jnp.int32, shape, len(shape) - 1)
    return (lane >= h * HD) & (lane < (h + 1) * HD)


def lane_sum(e):
    width = min(128, e.shape[1])
    total = e[:, :width]
    for i in range(1, e.shape[1] // width):
        total = total + e[:, i * width : (i + 1) * width]
    return total


def ln_stats(v):
    c = v - jnp.mean(v, axis=1, keepdims=True)
    r = lax.rsqrt(jnp.mean(c * c, axis=1, keepdims=True) + 1e-5)
    return c * r, r


def as_row(ref):
    return ref[...].astype(F32).reshape(1, -1)


def load_rows(ref, start, count):
    return ref[pl.ds(pl.multiple_of(start, count), count), :]


def kept(shape, dtype):
    return pltpu.VMEM(shape, dtype)


def in_hbm(x):
    return pltpu.with_memory_space_constraint(x, pltpu.HBM)


def cost(us):
    return pl.CostEstimate(flops=int(us * SCALE * 1.1e9), bytes_accessed=0, transcendentals=0)


def place_in(g):
    me = lax.axis_index("head")
    return me % g, me // g


def params(mib):
    return pltpu.CompilerParams(vmem_limit_bytes=mib * MIB)


def qkv_kernel(g, norm, step, *rest):
    place, _ = place_in(g)
    rows, rest = rest[:g], rest[g:]
    if norm:
        vec_ref, *rest = rest
    pack_ref, q_ref, k_ref, v_ref = rest[:4]
    norm_out = rest[4:]
    R, D = rows[0].shape
    W = q_ref.shape[1]
    wt = pack_ref[0 : 3 * W, :]
    bias = pack_ref[4 * W : 4 * W + VROWS, :].astype(F32)[0:1, 0 : 3 * W]
    for r in range(g):
        base = (place + r) % g * R
        for j in range(0, R, step):
            a = rows[r][j : j + step, :]
            if norm:
                xh, _ = ln_stats(a.astype(F32))
                a = (xh * vec_ref[0:1, :] + vec_ref[1:2, :]).astype(BF)
                norm_out[r][j : j + step, :] = a
            t = (nt(a, wt) + bias).astype(BF)
            at = pl.ds(pl.multiple_of(base + j, step), step)
            q_ref[at, :] = t[:, :W]
            k_ref[at, :] = t[:, W : 2 * W]
            v_ref[at, :] = t[:, 2 * W :]


def project(rows, packed, vecs=None, step=256):
    g = len(rows)
    R, D = rows[0].shape
    W = (packed.shape[0] - VROWS) // 4
    L = g * R
    norm = vecs is not None
    args = [*rows, *([vecs] if norm else []), packed]
    outs = [kept((L, W), BF)] * 3
    if norm:
        outs += [kept((R, D), BF)] * g
    res = pl.pallas_call(
        functools.partial(qkv_kernel, g, norm, step),
        in_specs=[VMEM] * len(args),
        out_specs=[VMEM] * len(outs),
        out_shape=outs,
        compiler_params=params(4),
        cost_estimate=cost(2.0),
        name="norm_qkv" if norm else "qkv",
    )(*args)
    return res[:3], res[3:]


def fwd_kernel(bq, bk, nh, W, L, g, s_ref, q_ref, k_ref, v_ref, *rest):
    nck = L // CHUNK
    o_ref, st_ref = rest[:2]
    w_refs = rest[2 : 2 + nck]
    sends = rest[2 + nck :]
    nq = L // bq
    R = L // g
    place, _ = place_in(g)
    long = jnp.max(s_ref[...]) > 0

    def scaled_queries(at):
        qf = q_ref[at, :].astype(F32) * (LOG2E * HD**-0.5)
        hi = qf.astype(BF)
        lo = (qf - hi.astype(F32)).astype(BF)
        qs = []
        z = jnp.zeros_like(hi)
        for h in range(nh):
            m = head_mask(hi.shape, h)
            qs.append(jnp.concatenate([jnp.where(m, hi, z), jnp.where(m, lo, z)], axis=1))
        return qs

    def keys(at):
        kt = k_ref[at, :]
        return jnp.concatenate([kt, kt], axis=1)

    def values(at):
        vt = v_ref[at, :]
        z = jnp.zeros_like(vt)
        return [jnp.where(head_mask(vt.shape, h), vt, z) for h in range(nh)]

    def finish(at, acc, sums, bases):
        lane = lax.broadcasted_iota(jnp.int32, (bq, 128), 1)
        st = jnp.ones((bq, 128), F32)
        out = jnp.zeros((bq, W), F32)
        for h in range(nh):
            inv = 1.0 / sums[h]
            st = jnp.where(lane == h, inv, st)
            if bases is not None:
                st = jnp.where(lane == 8 + h, bases[h], st)
            out = jnp.where(head_mask(out.shape, h), acc * inv, out)
        st_ref[at, :] = st
        o_ref[at, :] = out.astype(BF)

    sq_r = lax.broadcasted_iota(jnp.int32, (bk, bk), 0)
    sq_c = lax.broadcasted_iota(jnp.int32, (bk, bk), 1)

    def fast(c, lo_blk):
        at = slice(c * bq, (c + 1) * bq)
        qs = scaled_queries(at)
        nr = bq // bk
        acc = [None] * nr
        ls = [[None] * nr for _ in range(nh)]
        for kb in range(lo_blk, (c + 1) * nr):
            base = kb * bk
            first = max(0, kb - c * nr)
            r0 = first * bk
            kt = keys(slice(base, base + bk))
            chunk = base // CHUNK
            top_row = c * bq - chunk * CHUNK
            wl = []
            for h in range(nh):
                s = nt(qs[h][r0:, :], kt)
                if base >= c * bq:
                    top = jnp.where(sq_c <= sq_r, s[:bk, :], 0.0)
                    s = top if r0 + bk == bq else jnp.concatenate([top, s[bk:, :]], axis=0)
                e = jnp.exp2(jnp.abs(s))
                x = (e - 1.0).astype(BF)
                wv = jnp.where(s.astype(BF) < 0, -x, x)
                t = lane_sum(e)
                for r in range(first, nr):
                    tr = t[(r - first) * bk : (r - first + 1) * bk, :]
                    ls[h][r] = tr if ls[h][r] is None else ls[h][r] + tr
                w_refs[chunk][h, top_row + r0 : top_row + bq, base % CHUNK : base % CHUNK + bk] = wv
                wl.append(wv)
            vcat = jnp.concatenate(values(slice(base, base + bk)), axis=0)
            res = nn(jnp.concatenate(wl, axis=1), vcat)
            for r in range(first, nr):
                part = res[(r - first) * bk : (r - first + 1) * bk, :]
                acc[r] = part if acc[r] is None else acc[r] + part
        row = lax.broadcasted_iota(jnp.int32, (bq, 1), 0)
        extra = (bk - 1 - row % bk).astype(F32)
        sums = [
            jnp.sum(jnp.concatenate(ls[h], axis=0), axis=1, keepdims=True) - extra
            for h in range(nh)
        ]
        finish(at, jnp.concatenate(acc, axis=0), sums, None)

    for c in range(nq):
        if c * bq < SHORT:
            fast(c, 0)
        else:
            pl.when(long)(functools.partial(fast, c, 0))
            pl.when(~long)(functools.partial(fast, c, SHORT // bk))

    lane = lax.broadcasted_iota(jnp.int32, (L, 128), 1)
    smallest = jnp.min(jnp.where(lane < nh, st_ref[...], 1.0))

    def slow(qi, _):
        at = pl.ds(pl.multiple_of(qi * bq, bq), bq)
        qs = scaled_queries(at)
        lo_blk = jnp.where(long | (qi * bq < SHORT), 0, SHORT // bk)
        hi_blk = (qi + 1) * (bq // bk)
        rows = lax.broadcasted_iota(jnp.int32, (bq, bk), 0) + qi * bq
        cols = lax.broadcasted_iota(jnp.int32, (bq, bk), 1)

        def scores(h, kb):
            kt = keys(pl.ds(pl.multiple_of(kb * bk, bk), bk))
            return nt(qs[h], kt), cols + kb * bk <= rows

        def top_step(kb, tops):
            new = []
            for h in range(nh):
                s, vis = scores(h, kb)
                mag = jnp.where(vis, jnp.abs(s), 0.0)
                new.append(jnp.maximum(tops[h], jnp.max(mag, axis=1, keepdims=True)))
            return tuple(new)

        tops = lax.fori_loop(lo_blk, hi_blk, top_step, (jnp.zeros((bq, 1), F32),) * nh)
        bases = [jnp.exp2(-t) for t in tops]

        def step(kb, carry):
            acc, sums = carry
            new = []
            vs = values(pl.ds(pl.multiple_of(kb * bk, bk), bk))
            for h in range(nh):
                s, vis = scores(h, kb)
                e = jnp.where(vis, jnp.exp2(jnp.abs(s) - tops[h]), 0.0)
                wv = jnp.where(s < 0, bases[h] - e, e - bases[h])
                wv = jnp.where(vis & (s != 0), wv, 0.0).astype(BF)
                new.append(sums[h] + jnp.sum(e, axis=1, keepdims=True))
                acc = acc + nn(wv, vs[h])
                for j in range(nck):

                    @pl.when(kb // (CHUNK // bk) == j)
                    def _():
                        top_row = pl.multiple_of(qi * bq - j * CHUNK, bq)
                        off = pl.multiple_of((kb % (CHUNK // bk)) * bk, bk)
                        w_refs[j][h, pl.ds(top_row, bq), pl.ds(off, bk)] = wv

            return acc, tuple(new)

        acc, sums = lax.fori_loop(
            lo_blk,
            hi_blk,
            step,
            (jnp.zeros((bq, W), F32), (jnp.zeros((bq, 1), F32),) * nh),
        )
        finish(at, acc, sums, bases)
        return 0

    @pl.when(smallest < 1e-25)
    def _():
        lax.fori_loop(0, nq, slow, 0)

    for r in range(1, g):
        sends[r - 1][...] = load_rows(o_ref, (place + r) % g * R, R)


def attn_fwd(flag, q, k, v, g, bq=512, bk=256):
    L, W = q.shape
    nh = W // HD
    nck = L // CHUNK
    res = pl.pallas_call(
        functools.partial(fwd_kernel, bq, bk, nh, W, L, g),
        in_specs=[VMEM] * 4,
        out_specs=[VMEM] * (2 + nck + g - 1),
        out_shape=[kept((L, W), BF), kept((L, 128), F32)]
        + [kept((nh, L - j * CHUNK, CHUNK), BF) for j in range(nck)]
        + [S((L // g, W), BF)] * (g - 1),
        compiler_params=params(FWD_MIB),
        cost_estimate=cost(7.0),
        name="attn_fwd",
    )(flag, q, k, v)
    return res[0], res[1], res[2 : 2 + nck], res[2 + nck :]


def bwd_kernel(h, bk, g, second, s_ref, q_ref, k_ref, v_ref, st_ref, o_ref, wt_ref, *rest):
    L, W = q_ref.shape
    nck = L // CHUNK
    do_refs = rest[:g]
    w_refs = rest[g : g + nck]
    n1_refs = rest[g + nck : 2 * g + nck]
    rest = rest[2 * g + nck :]
    if second:
        tq_ref, dk_ref, dv_ref, t_ref, gq_ref, vec_ref, bias_ref = rest
    else:
        tq_ref, dk_ref, dv_ref = rest
    D = wt_ref.shape[1]
    R = L // g
    place, _ = place_in(g)
    long = jnp.max(s_ref[...]) > 0
    sq_r = lax.broadcasted_iota(jnp.int32, (bk, bk), 0)
    sq_c = lax.broadcasted_iota(jnp.int32, (bk, bk), 1)
    lanes = slice(h * HD, (h + 1) * HD)
    bq = SHORT
    scale = HD**-0.5
    q_at, k_at, v_at = (slice(i * HD, (i + 1) * HD) for i in range(3))

    def body(c, lo_blk):
        nr = bq // bk
        rep = bk // 128
        at = slice(c * bq, (c + 1) * bq)
        tri = jnp.where(sq_c <= sq_r, 1.0, 0.0).astype(BF)
        st = st_ref[at, :]
        rows = []
        for lo in range(c * bq, (c + 1) * bq, min(bq, R)):
            here = slice(lo % R, lo % R + min(bq, R))
            x = do_refs[0][here, :]
            for r in range(1, g):
                x = jnp.where(lo // R == (place + r) % g, do_refs[r][here, :], x)
            rows.append(x)
        do = jnp.concatenate(rows, axis=0).astype(F32)
        do = jnp.where(head_mask((bq, W), h), do * st[:, h : h + 1], 0.0)
        delta = jnp.sum(do * o_ref[at, :].astype(F32), axis=1, keepdims=True)
        delta = jnp.concatenate([jnp.broadcast_to(delta, (bq, 128)).astype(BF)] * rep, 1)
        e0 = jnp.broadcast_to(st[:, 8 + h : 9 + h], (bq, 128)).astype(BF)
        e0 = jnp.concatenate([e0] * rep, 1)
        do_b = do.astype(BF)
        do_t = do.T[lanes, :].astype(BF)
        q_t = q_ref[at, :].astype(F32).T[lanes, :].astype(BF)
        dq = [None] * nr
        for kb in range(lo_blk, (c + 1) * nr):
            base = kb * bk
            first = max(0, kb - c * nr)
            r0 = first * bk
            chunk = base // CHUNK
            top_row = c * bq - chunk * CHUNK
            cols = slice(base, base + bk)
            wv = w_refs[chunk][h, top_row + r0 : top_row + bq, base % CHUNK : base % CHUNK + bk]
            wg = nt(do_b[r0:, :], v_ref[cols, :]).astype(BF)
            dl = delta[r0:, :]
            e = e0[r0:, :]
            if base >= c * bq:
                top = e[:bk, :] * tri
                e = top if r0 + bk == bq else jnp.concatenate([top, e[bk:, :]], axis=0)
            zero = jnp.zeros_like(wv)
            d = jnp.where(wv < 0, -dl, jnp.where(wv > 0, dl, zero))
            gr = (jnp.abs(wv) + e) * (wg - d)
            dv = nn(do_t[:, r0:], wv)
            dk = nn(q_t[:, r0:], gr)
            if not second:
                dv_ref[:, cols] = dv
                dk_ref[:, cols] = dk
            else:
                if base < SHORT:
                    dv = dv + dv_ref[:, cols]
                    dk = dk + dk_ref[:, cols]
                t_ref[k_at, cols] = (dk * scale).astype(BF)
                t_ref[v_at, cols] = dv.astype(BF)
            res = nn(gr, k_ref[cols, :])
            for r in range(first, nr):
                part = res[(r - first) * bk : (r - first + 1) * bk, :]
                dq[r] = part if dq[r] is None else dq[r] + part
        dq = (jnp.concatenate(dq, axis=0) * scale).T[lanes, :].astype(BF)
        if second:
            t_ref[q_at, at] = dq
        else:
            tq_ref[...] = dq

    if not second:
        body(0, 0)
        return
    t_ref[q_at, 0:SHORT] = tq_ref[...]
    pl.when(long)(functools.partial(body, 1, 0))

    @pl.when(~long)
    def _():
        t_ref[k_at, 0:SHORT] = (dk_ref[...] * scale).astype(BF)
        t_ref[v_at, 0:SHORT] = dv_ref[...].astype(BF)
        body(1, SHORT // bk)

    gq = jnp.zeros((3 * HD, D), F32)
    for r in range(g):
        start = pl.multiple_of((place + r) % g * R, R)
        gq = gq + nn(t_ref[:, pl.ds(start, R)], n1_refs[r][...])
    gq_ref[...] = gq.astype(BF)
    bias_ref[...] = nt(jnp.ones((VROWS, L), BF), t_ref[...])
    bias = jnp.sum(t_ref[...].astype(F32), axis=1, keepdims=True)
    wt = jnp.concatenate([wt_ref[i * W + h * HD : i * W + (h + 1) * HD, :] for i in range(3)], axis=0)
    wt = wt.astype(F32)
    vec_ref[...] = jnp.concatenate(
        [
            jnp.sum(wt * gq, axis=0, keepdims=True),
            jnp.sum(wt * bias, axis=0, keepdims=True),
            jnp.zeros((6, D), F32),
        ],
        axis=0,
    )


def attn_bwd(flag, h, q, k, v, st, o, wt, dos, ws, n1s, half=None, bk=256):
    L, W = q.shape
    g = len(dos)
    D = wt.shape[1]
    rows = 3 * HD
    second = half is not None
    args = [q, k, v, st, o, wt, *dos, *ws, *n1s, *(half or [])]
    if second:
        outs = [kept((rows, L), BF), kept((rows, D), BF), kept((8, D), F32), kept((VROWS, rows), F32)]
    else:
        outs = [kept((HD, SHORT), BF)] + [kept((HD, SHORT), F32)] * 2
    return pl.pallas_call(
        functools.partial(bwd_kernel, h, bk, g, second),
        in_specs=[VMEM] * (1 + len(args)),
        out_specs=[VMEM] * len(outs),
        out_shape=outs,
        compiler_params=params(BWD_MIB),
        cost_estimate=cost(2.1 + 3.0 * second),
        name="attn_bwd",
    )(flag, *args)


def ffn_kernel(g, slots, halves, todo, first, last, *refs):
    m = g * slots
    place, _ = place_in(g)
    it = iter(refs)

    def take(count):
        return [next(it) for _ in range(count)]

    ow_refs, up_refs, dn_refs = take(m if first or last else len(todo)), take(len(todo)), take(len(todo))
    (vec_ref,) = take(1)
    if first or last:
        o_refs, att_refs = take(slots), take(m - slots)
    if first:
        x_ref, cot_in = take(2)
    else:
        mids, n2, n2t, cots, cott, oacc_in, nacc_in = take(7)
    if first:
        mids, n2, n2t, cots, cott = take(5)
    if last:
        lo_ref, oacc = take(2)
        atg_refs, og_refs = take(m), take(m)
        (nacc,) = take(1)
        oacc_out = oacc
    else:
        oacc_out, nacc = take(2)
    ug_refs, dg_refs = take(len(todo)), take(len(todo))
    R, D = cots.shape
    FS = up_refs[0].shape[1]
    W = (ow_refs[0].shape[0] - VROWS) // 4
    step = R // halves
    blocks = [slice(j, j + step) for j in range(0, R, step)]

    def vec(i):
        return vec_ref[2 + i : 3 + i, :]

    def att_rows(at):
        rows = pl.ds(pl.multiple_of(place * R + at.start, step), step)
        return jnp.concatenate([o[rows, :] for o in o_refs] + [a[at, :] for a in att_refs], axis=1)

    if first or last:
        ow = jnp.concatenate([a[3 * W : 4 * W, :] for a in ow_refs], axis=0)
    if first:
        cots[...] = cot_in[...]
        for at in blocks:
            mid = x_ref[at, :].astype(F32) + nn(att_rows(at), ow) + vec(0)
            mids[at, :] = mid
            xh, _ = ln_stats(mid)
            y = xh * vec(1) + vec(2)
            n2[at, :] = y.astype(BF)
            n2t[:, at] = y.T.astype(BF)
            cott[:, at] = cots[at, :].astype(F32).T.astype(BF)

    for j, i in enumerate(todo):
        up = up_refs[j][...]
        dn = dn_refs[j][...]
        bias_ref = ow_refs[i if first or last else j]
        ub = bias_ref[4 * W : 4 * W + VROWS, :].astype(F32)[1:2, 0:FS]
        ug = dg = ubg = None
        for at in blocks:
            u = nn(n2[at, :], up) + ub
            ag = nt(cots[at, :], dn)
            u2 = u * u
            t = jnp.tanh(u * (GELU_C + (GELU_C * 0.044715) * u2))
            hh = 0.5 + 0.5 * t
            act = (u * hh).astype(BF)
            slope = hh + u * (0.5 - 0.5 * t * t) * (GELU_C + (3 * GELU_C * 0.044715) * u2)
            pgf = ag * slope
            pg = pgf.astype(BF)
            out = nn(act, dn)
            back = nt(pg, up)
            if j > 0:
                oacc_out[at, :] += out
                nacc[at, :] += back
            elif first:
                oacc_out[at, :] = mids[at, :] + vec(3) + out
                nacc[at, :] = back
            else:
                oacc_out[at, :] = oacc_in[at, :] + out
                nacc[at, :] = nacc_in[at, :] + back
            bsum = jnp.sum(pgf, axis=0, keepdims=True)
            gu = nn(n2t[:, at], pg)
            gd = nn(cott[:, at], act)
            ubg = bsum if ubg is None else ubg + bsum
            ug = gu if ug is None else ug + gu
            dg = gd if dg is None else dg + gd
        ug_refs[j][0:D, :] = ug.astype(BF)
        ug_refs[j][D:, :] = jnp.broadcast_to(ubg, (PAD, FS)).astype(BF)
        dg_refs[j][...] = dg.T.astype(BF)

    if not last:
        return
    mg_ref = oacc
    sums = [None] * 4
    og = None
    for at in blocks:
        lo_ref[at, :] = oacc[at, :].astype(BF)
        xh, rs = ln_stats(mids[at, :])
        ng = nacc[at, :]
        e = ng * vec(1)
        cf = cots[at, :].astype(F32)
        back = e - jnp.mean(e, axis=1, keepdims=True) - xh * jnp.mean(e * xh, axis=1, keepdims=True)
        mg = cf + rs * back
        mg_ref[at, :] = mg
        bg = mg.astype(BF)
        atg = nt(bg, ow).astype(BF)
        for i in range(m):
            atg_refs[i][at, :] = atg[:, i * W : (i + 1) * W]
        gr = tn(att_rows(at), bg)
        og = gr if og is None else og + gr
        for i, a in enumerate((bg.astype(F32), ng * xh, ng, cf)):
            a = jnp.sum(a, axis=0, keepdims=True)
            sums[i] = a if sums[i] is None else sums[i] + a
    og = og.astype(BF)
    both = jnp.concatenate(sums + [jnp.zeros((4, D), F32)], axis=0)
    hi = both.astype(BF).astype(F32)
    both = jnp.concatenate([hi, both - hi], axis=0).astype(BF)
    for i in range(m):
        og_refs[i][0:W, :] = og[i * W : (i + 1) * W, :]
        og_refs[i][W:, :] = both


def ffn(g, slots, todo, ow, up, dn, vecs, attended, start=None, state=None, last=False, halves=2):
    first = state is None
    R, D = (start[0] if first else state[0]).shape
    FS = up[0].shape[1]
    W = (ow[0].shape[0] - VROWS) // 4
    m = g * slots
    args = [*(ow if first or last else [ow[i] for i in todo])]
    args += [up[i] for i in todo] + [dn[i] for i in todo] + [vecs]
    if first or last:
        args += attended
    args += start if first else state
    outs = []
    if first:
        outs += [kept((R, D), F32), kept((R, D), BF), kept((D, R), BF), kept((R, D), BF), kept((D, R), BF)]
    if last:
        outs += [S((R, D), BF), kept((R, D), F32)] + [kept((R, W), BF)] * m + [kept((W + VROWS, D), BF)] * m
        outs += [kept((R, D), F32)]
    else:
        outs += [kept((R, D), F32)] * 2
    total_at = (1, 2 + 2 * m) if last else (5, 6) if first else (0, 1)
    alias = {} if first else {len(args) - 2: total_at[0], len(args) - 1: total_at[1]}
    outs += [kept((D + PAD, FS), BF)] * len(todo) + [kept((FS, D), BF)] * len(todo)
    res = pl.pallas_call(
        functools.partial(ffn_kernel, g, slots, halves, todo, first, last),
        in_specs=[VMEM] * len(args),
        out_specs=[VMEM] * len(outs),
        out_shape=outs,
        input_output_aliases=alias,
        compiler_params=params(FFN_MIB),
        cost_estimate=cost(5.0),
        name="ffn",
    )(*args)
    ugs, dgs = res[len(res) - 2 * len(todo) : len(res) - len(todo)], res[len(res) - len(todo) :]
    return res[: len(res) - 2 * len(todo)], dict(zip(todo, ugs)), dict(zip(todo, dgs))


def back_kernel(g, heads, last, rel, *refs):
    place, _ = place_in(g)
    count = len(heads)
    t_refs, wt_refs = refs[:count], refs[count : 2 * count]
    rest = refs[2 * count :]
    out_ref = rest[-1]
    R = out_ref.shape[0]
    start = pl.multiple_of((place + rel) % g * R, R)
    t = jnp.concatenate([a[:, pl.ds(start, R)] for a in t_refs], axis=0)
    wt = []
    for own, ref in zip(heads, wt_refs):
        W = (ref.shape[0] - VROWS) // 4
        wt += [ref[i * W + h * HD : i * W + (h + 1) * HD, :] for h in own for i in range(3)]
    n1g = tn(t, jnp.concatenate(wt, axis=0))
    if not last:
        out_ref[...] = n1g.astype(BF)
        return
    x_ref, mg_ref, vec_ref = rest[g - 1 : g + 2]
    for a in rest[: g - 1]:
        n1g = n1g + a[...].astype(F32)
    xh, rs = ln_stats(x_ref[...].astype(F32))
    e = n1g * vec_ref[0:1, :]
    back = e - jnp.mean(e, axis=1, keepdims=True) - xh * jnp.mean(e * xh, axis=1, keepdims=True)
    out_ref[...] = (mg_ref[...] + rs * back).astype(BF)


def row_back(g, rel, heads, ts, wts, R, last=None):
    D = wts[0].shape[1]
    args = [*ts, *wts] + ([] if last is None else [*last[0], *last[1:]])
    return pl.pallas_call(
        functools.partial(back_kernel, g, heads, last is not None, rel),
        in_specs=[VMEM] * len(args),
        out_specs=VMEM,
        out_shape=kept((R, D), BF) if last is None else S((R, D), BF),
        compiler_params=params(BACK_MIB),
        cost_estimate=cost(2.0),
        name="row_back" if last is None else "norm_back",
    )(*args)


def fuse(body, outs, *args, scratch=()):
    return pl.pallas_call(
        body,
        in_specs=[VMEM] * len(args),
        out_specs=[VMEM] * len(outs),
        out_shape=outs,
        scratch_shapes=list(scratch),
        compiler_params=params(SUM_MIB),
        name=body.__name__,
    )(*args)


def sum_of(refs, at):
    out = refs[0][at].astype(F32)
    for a in refs[1:]:
        out = out + a[at].astype(F32)
    return out.astype(BF)


def join_vec(v):
    v = v.astype(F32)
    return v[: VROWS // 2] + v[VROWS // 2 :]


def split_vec(v):
    hi = v.astype(BF).astype(F32)
    return jnp.concatenate([hi, v - hi], axis=0).astype(BF)


def vec_of(refs, at):
    return split_vec(functools.reduce(lambda a, b: a + b, [join_vec(a[at]) for a in refs]))


def pack_inputs(qkv_t, out_weight, qkv_bias, up_bias, tokens, long_slot, vecs):
    rows, D = qkv_t.shape
    W = out_weight.shape[0]
    flat = [up_bias, *vecs]
    slots = long_slot.shape[0]
    g = lax.axis_size("head") // slots

    def pack(qt_ref, ow_ref, qb_ref, x_ref, s_ref, *refs):
        flat_refs, refs = refs[: len(flat)], refs[len(flat) :]
        out, x_out, flag_ref, vec_ref, qb_in, s_in = refs[:6]
        flat_in, sems = refs[6:-1], refs[-1]
        pairs = [
            (qb_ref, qb_in),
            (s_ref, s_in),
            *zip(flat_refs, flat_in),
            (ow_ref, out.at[pl.ds(rows, W)]),
            (x_ref, x_out),
        ]
        copies = [pltpu.make_async_copy(a, b, sems.at[i]) for i, (a, b) in enumerate(pairs)]
        for c in copies:
            c.start()
        out[0:rows, :] = qt_ref[...]
        for c in copies[:-2]:
            c.wait()
        qb = qb_in[...].astype(F32)
        qb = jnp.concatenate([qb[i : i + 1, :] for i in range(3)], axis=1)
        lines = [qb, as_row(flat_in[0]), jnp.zeros((VROWS - 2, D), F32)]
        lines = [jnp.pad(a, ((0, 0), (0, D - a.shape[1]))) for a in lines]
        out[rows + W :, :] = jnp.concatenate(lines, axis=0).astype(BF)
        vec_ref[...] = jnp.concatenate(
            [as_row(a) for a in flat_in[1:]] + [jnp.zeros((2, D), F32)], axis=0
        )
        _, group = place_in(g)
        flag_ref[...] = jnp.full((8, 128), (s_in[group] > 0).astype(F32))
        for c in copies[-2:]:
            c.wait()

    hbm = [in_hbm(a) for a in (out_weight, qkv_bias, tokens, long_slot, *flat)]
    return pl.pallas_call(
        pack,
        in_specs=[VMEM] + [ANY] * len(hbm),
        out_specs=[VMEM] * 4,
        out_shape=[
            kept((rows + W + VROWS, D), BF),
            kept(tokens.shape, BF),
            kept((8, 128), F32),
            kept((8, D), F32),
        ],
        scratch_shapes=[pltpu.VMEM(qkv_bias.shape, BF), pltpu.SMEM((slots,), jnp.int32)]
        + [pltpu.VMEM(a.shape, BF) for a in flat]
        + [pltpu.SemaphoreType.DMA((4 + len(flat),))],
        compiler_params=params(SUM_MIB),
        name="pack",
    )(qkv_t, *hbm)


def half_at(bit, count, mine):
    place = lax.axis_index("batch") // 2**bit % 2
    place = place if mine else 1 - place
    return pl.ds(pl.multiple_of(place * count, count), count)


def add_up(terms, vec_rows=0):
    rows, cols = terms[0].shape
    count = rows - vec_rows

    def sum_terms(*refs):
        ins, out = refs[: len(terms)], refs[len(terms)]
        if count:
            out[0:count, :] = sum_of(ins, slice(0, count))
        if vec_rows:
            out[count:, :] = vec_of(ins, slice(count, rows))

    return fuse(sum_terms, [kept((rows, cols), BF)], *terms)[0]


def with_vec(terms, vec):
    rows, cols = terms[0].shape

    def sum_vec(*refs):
        ins, vec_ref, out = refs[: len(terms)], refs[-2], refs[-1]
        out[0:rows, :] = sum_of(ins, slice(0, rows))
        out[rows:, :] = vec_ref[...]

    return fuse(sum_vec, [kept((rows + VROWS, cols), BF)], *terms, vec)[0]


def halve(bit, terms, has_vec=False):
    rows, cols = terms[0].shape
    count = (rows - VROWS if has_vec else rows) // 2

    def sum_halves(*refs):
        ins, outs = refs[: len(terms)], refs[len(terms) :]
        for out, mine in zip(outs, (True, False)):
            out[0:count, :] = sum_of(ins, half_at(bit, count, mine))
            if has_vec:
                out[count:, :] = vec_of(ins, slice(2 * count, rows))

    return fuse(sum_halves, [kept((count + VROWS * has_vec, cols), BF)] * 2, *terms)


def stack_sums(downs, outs_):
    fs, cols = downs[0].shape
    rows = fs + outs_[0].shape[0]

    def sum_pieces(*refs):
        ins, out = refs[:-1], refs[-1]
        out[0:fs, :] = sum_of(ins[: len(downs)], slice(0, fs))
        out[fs : rows - VROWS, :] = sum_of(ins[len(downs) :], slice(0, rows - fs - VROWS))
        out[rows - VROWS :, :] = vec_of(ins[len(downs) :], slice(rows - fs - VROWS, rows - fs))

    return fuse(sum_pieces, [kept((rows, cols), BF)], *downs, *outs_)[0]


def join(bit, mine, other, count):
    def join_halves(mine_ref, other_ref, out):
        out[half_at(bit, count, True), :] = mine_ref[0:count, :]
        out[half_at(bit, count, False), :] = other_ref[0:count, :]

    return fuse(join_halves, [kept((2 * count, mine.shape[1]), BF)], mine, other)[0]


def collect(mine, other, count, splits, has_vec=False):
    cols = mine.shape[1]

    def gather_halves(mine_ref, other_ref, *refs):
        outs, whole = refs[:-1], refs[-1]
        whole[half_at(0, count, True), :] = mine_ref[0:count, :].astype(F32)
        whole[half_at(0, count, False), :] = other_ref[0:count, :].astype(F32)
        first = 0
        for out, size in zip(outs, splits):
            out[...] = whole[first : first + size, :]
            first += size
        if has_vec:
            at = slice(count, count + VROWS)
            outs[-1][...] = join_vec(mine_ref[at, :]) + join_vec(other_ref[at, :])

    return fuse(
        gather_halves,
        [S((a, cols), F32) for a in splits] + [S((VROWS // 2, cols), F32)] * has_vec,
        mine,
        other,
        scratch=[pltpu.VMEM((2 * count, cols), F32)],
    )


def fill_rows(ref, g_ref, bias_ref):
    rows = g_ref.shape[0]
    ref[0:rows, :] = g_ref[...]
    ref[rows:, :] = jnp.zeros((ref.shape[0] - rows, ref.shape[1]), BF)
    ref[rows : rows + VROWS, 0 : bias_ref.shape[1]] = bias_ref[...].astype(BF)


def q_rows(gq, bias):
    def stack_rows(g_ref, bias_ref, out):
        fill_rows(out, g_ref, bias_ref)

    return fuse(stack_rows, [kept((gq.shape[0] + QPAD, gq.shape[1]), BF)], gq, bias)[0]


def q_halve(gq, bias, crossed):
    rows, cols = gq.shape[0] + QPAD, gq.shape[1]
    count = rows // 2

    def sum_rows(g_ref, bias_ref, *refs):
        c_refs = refs[: len(crossed)]
        mine, other, whole = refs[-3:]
        fill_rows(whole, g_ref, bias_ref)
        for out, which in ((mine, True), (other, False)):
            out[...] = sum_of([whole, *c_refs], half_at(0, count, which))

    return fuse(
        sum_rows,
        [kept((count, cols), BF)] * 2,
        gq,
        bias,
        *crossed,
        scratch=[pltpu.VMEM((rows, cols), BF)],
    )


def after(x, *deps):
    return lax.optimization_barrier((x,) + deps)[0]


class Chain:
    def __init__(self, steps):
        self.steps = steps
        self.result = None
        self.sent, self.got = next(steps)

    def tick(self, *deps):
        if self.result is None:
            try:
                self.sent, self.got = self.steps.send(after(self.got, *deps))
            except StopIteration as stop:
                self.result = stop.value
                self.sent = []


def vec_split(v):
    hi = lax.reduce_precision(v, 8, 7)
    return jnp.concatenate([hi, v - hi], axis=0).astype(BF)


def vec_join(v):
    half = v.shape[0] // 2
    return v[:half].astype(F32) + v[half:].astype(F32)


def per_device(
    tokens_in,
    norm1_gain,
    norm1_bias,
    qkv_weight,
    qkv_bias,
    out_weight,
    out_bias,
    norm2_gain,
    norm2_bias,
    up_weight,
    up_bias,
    down_weight,
    down_bias,
    cotangent,
    long_slot,
):
    n = lax.axis_size("head")
    nb = lax.axis_size("batch")
    slots = long_slot.shape[0]
    g = n // slots
    R, D = tokens_in.shape
    W = qkv_weight.shape[2]
    FS = up_weight.shape[1]
    nh = W // HD
    bits = []
    while 2 ** len(bits) < nb:
        bits.append(2 ** len(bits))

    def cross(x, r):
        return lax.ppermute(x, "head", [(i, (i + r * g) % n) for i in range(n)])

    def rot(x, r):
        return lax.ppermute(x, "head", [(i, i // g * g + (i % g - r) % g) for i in range(n)])

    def flip(x, bit):
        return lax.ppermute(x, "batch", [(i, i ^ bit) for i in range(nb)])

    def exchanged(a):
        return [a] + [cross(a, r) for r in range(1, slots)]

    xs = [tokens_in] + [rot(tokens_in, r) for r in range(1, g)]
    qkv_t = qkv_weight.transpose(1, 2, 0).reshape(3 * W, D)
    small = [norm1_gain, norm1_bias, out_bias, norm2_gain, norm2_bias, down_bias]
    packed, x_own, flag, vecs = pack_inputs(
        qkv_t, out_weight, qkv_bias, up_bias, tokens_in, long_slot, small
    )
    packed = exchanged(packed)
    qkv, n1s = project([x_own] + xs[1:], packed[0], vecs)

    saved = []
    att = []
    for ph in range(slots):
        if ph:
            qkv, _ = project(n1s, after(packed[ph], saved[-1][3]))
        first = qkv[0] if ph == 0 else after(qkv[0], upw[0], dnw[0])
        o, st, ws, sends = attn_fwd(flag, first, *qkv[1:], g)
        saved.append((*qkv, st, o, packed[ph], ws))
        att.append([rot(sends[g - r - 1], r) for r in range(1, g)])
        if ph == 0:
            upw = exchanged(after(up_weight, vecs))
            dnw = exchanged(after(down_weight, st))
            oww = [packed[0]] + [after(b, st) for b in packed[1:]]

    def at(r, ph):
        return r * slots + ph

    def members_of(a):
        return {(r, ph): rot(b, r) if r else b for r in range(g) for ph, b in a}

    def listed(a):
        return [a.get((r, ph)) for r in range(g) for ph in range(slots)]

    ow = listed(members_of(list(enumerate(oww))))
    ups, dns = members_of([(0, upw[0])]), members_of([(0, dnw[0])])
    attended = [a[4] for a in saved] + [att[ph][r - 1] for r in range(1, g) for ph in range(slots)]

    def members(parts):
        return [rot(parts[(g - r) % g], r) for r in range(1, g)]

    def over_batch(terms, has_vec):
        mine, other = halve(1, terms, has_vec)
        got = yield [mine, other], flip(other, bits[1])
        mat = add_up([mine, got], VROWS * has_vec)
        for bit in bits[2:]:
            got = yield [mat], flip(mat, bit)
            mat = add_up([mat, got], VROWS * has_vec)
        got = yield [mat], flip(mat, bits[1])
        count = mat.shape[0] - VROWS * has_vec
        whole = join(1, mat, got, count)
        return (whole, mat[count:]) if has_vec else whole

    ug, dg = {}, {}

    def chain_u():
        others = range(1, slots)
        got = yield [ug[at(r, ph)] for r in range(1, g) for ph in others], [
            [rot(ug[at((g - r) % g, ph)], r) for r in range(1, g)] for ph in others
        ]
        sums = [add_up([ug[at(0, ph)]] + a) for ph, a in zip(others, got)]
        got = yield sums, [cross(sums[slots - r - 1], slots - r) for r in others]
        mine, other = halve(0, [ug[at(0, 0)]] + near + got)
        got = yield [mine, other], flip(other, bits[0])
        mat = yield from over_batch([mine, got], False)
        got = yield [mat], flip(mat, bits[0])
        return collect(mat, got, mat.shape[0], (D, PAD))

    def chain_d():
        got = yield list(dg.values()) + list(og), [
            [[rot(b, r) for b in (dg[at((g - r) % g, ph)], og[at((g - r) % g, ph)])] for r in range(1, g)]
            for ph in range(slots)
        ]
        sums = [
            stack_sums([dg[at(0, ph)]] + [a[0] for a in got[ph]],
                [og[at(0, ph)]] + [a[1] for a in got[ph]],
            )
            for ph in range(slots)
        ]
        got = yield sums, [cross(sums[slots - r], slots - r) for r in range(1, slots)]
        mine, other = halve(0, [sums[0]] + got, True)
        got = yield [mine, other], flip(other, bits[0])
        mat, vec = yield from over_batch([mine, got], True)
        got = yield [mat], flip(mat, bits[0])
        return [*collect(mat, got, mat.shape[0], (FS, W)), vec]

    def part(todo, **more):
        out, new_ug, new_dg = ffn(g, slots, todo, ow, listed(ups), listed(dns), vecs, attended, **more)
        ug.update(new_ug)
        dg.update(new_dg)
        return out

    ups.update(members_of([(ph, upw[ph]) for ph in range(1, slots)]))
    state = part([at(0, 0)], start=[after(x_own, *upw[1:]), cotangent])
    dns.update(members_of([(ph, after(dnw[ph], state[5])) for ph in range(1, slots)]))
    out = part([at(r, ph) for r in range(1, g) for ph in range(1, slots)], state=state)
    state = [*state[:5], *out]
    u = Chain(chain_u())
    state[5] = after(state[5], *u.sent)
    out = part([at(0, ph) for ph in range(1, slots)], state=state)
    state = [*state[:5], *out]
    u.tick(out[0])
    state[5] = after(state[5], *u.sent)
    out = part([at(r, 0) for r in range(1, g)], state=state, last=True)
    near = [rot(ug[at((g - r) % g, 0)], r) for r in range(1, g)]
    m = g * slots
    lo, mg, atg, og = out[0], out[1], out[2 : 2 + m], out[2 + m : 2 + 2 * m]
    dos = [
        [atg[ph]] + [rot(atg[(g - r) * slots + ph], r) for r in range(1, g)] for ph in range(slots)
    ]
    chains = {"u": u, "d": Chain(chain_d())}
    plan = ["d", "", "u", "", "ud", "ud", "d", "u"]
    grads = {}
    crossing = {}
    done = 0

    def sent():
        return [a for c in chains.values() for a in c.sent]

    def advance(*deps):
        nonlocal done
        for name, chain in chains.items():
            if name[0] == "q" or done >= len(plan) or name in plan[done]:
                chain.tick(*deps)
        done += 1

    def chain_v():
        def first_sum(*refs):
            vec = functools.reduce(lambda a, b: a + b, [v[...] for v in refs[:-1]])
            refs[-1][...] = split_vec(vec)

        parts = [grads[key][2] for key in grads]
        vec = fuse(first_sum, [kept((VROWS, D), BF)], *parts)[0]
        got = yield [vec], [rot(vec, r) for r in range(1, g)]
        vec = add_up([vec] + got, VROWS)
        got = yield [vec], [cross(vec, r) for r in range(1, slots)]
        return add_up([vec] + got, VROWS)

    def chain_q(h):
        res = grads[0, h]
        last = h == nh - 1
        crossed = [crossing[ph, h] for ph in range(1, slots)]
        mine, other = q_halve(res[1], res[3], crossed)
        got = yield [mine, other], flip(other, bits[0])
        if not last:
            mat = add_up([mine, got])
            for bit in bits[1:]:
                got = yield [mat], flip(mat, bit)
                mat = add_up([mat, got])
            got = yield [mat], flip(mat, bits[0])
            return collect(mat, got, mat.shape[0], (2 * mat.shape[0],))
        count = mine.shape[0]
        mat = with_vec([mine, got], chains["v"].result)
        for bit in bits[1:]:
            got = yield [mat], flip(mat, bit)
            mat = add_up([mat, got], VROWS)
        got = yield [mat], flip(mat, bits[0])
        return collect(mat, got, count, (2 * count,), True)

    dep = ()
    for ph in list(range(1, slots)) + [0]:
        q, k, v, st, o, pk, ws = saved[ph]
        for h in range(nh):
            args = [k, v, st, o, pk, dos[ph], ws, n1s]
            half = attn_bwd(flag, h, after(q, *sent(), *dep), *args)
            advance(half[0])
            res = attn_bwd(flag, h, after(q, *sent(), half[0]), *args, half)
            grads[ph, h] = res
            dep = (res[1],)
            advance(res[1])
            if ph:
                crossing[ph, h] = cross(q_rows(res[1], res[3]), slots - ph)
            else:
                chains["q%d" % h] = Chain(chain_q(h))
    chains["v"] = Chain(chain_v())

    order = [(ph, h) for ph in range(slots) for h in range(nh)]
    ts = [grads[key][0] for key in order]
    pks = [saved[ph][5] for ph, h in order]
    head_list = [(h,) for ph, h in order]
    sends = {}
    for r in range(1, g):
        sends[r] = row_back(g, r, head_list, [after(ts[0], *sent())] + ts[1:], pks, R)
    got = [rot(sends[(g - r) % g], r) for r in range(1, g)]
    chains["v"].tick(*sends.values())
    first = after(ts[0], *chains["v"].sent)
    input_grad = row_back(g, 0, head_list, [first] + ts[1:], pks, R, (got, x_own, mg, vecs))
    dep = [input_grad]
    chains["v"].tick(*dep)
    final = "q%d" % (nh - 1)
    tail = [[final, "u", "d"], [final, "q0", "d"], [final, "u", "d"]]
    while any(c.result is None for c in chains.values()):
        names = (tail.pop(0) if tail else None) or list(chains)[::-1]
        for name in names:
            c = chains[name]
            c.tick(*dep)
            dep = c.sent[:1] or dep
    results = {name: c.result for name, c in chains.items()}
    (up_grad, up_bias_grad), (down_grad, out_grad, vec2) = results["u"], results["d"]
    qs = [results["q%d" % h] for h in range(nh)]
    vec1 = qs[-1][1]
    qf = [a[0] for a in qs]
    vec2 = vec_join(vec2)
    gain_grad = (vec1[0] - norm1_bias.astype(F32) * vec1[1]) / norm1_gain.astype(F32)
    qkv_grad = jnp.concatenate([a[: 3 * HD].reshape(3, HD, D) for a in qf], axis=1).transpose(2, 0, 1)
    qkv_bias_grad = jnp.concatenate([a[3 * HD, : 3 * HD].reshape(3, HD) for a in qf], axis=1)
    return (
        lo,
        input_grad,
        gain_grad,
        vec1[1],
        qkv_grad,
        qkv_bias_grad,
        out_grad,
        vec2[0],
        vec2[1],
        vec2[2],
        up_grad,
        up_bias_grad[0],
        down_grad,
        vec2[3],
    )


def solution(mesh):
    rows = P(("batch", "head"), None)
    return jax.shard_map(
        per_device,
        mesh=mesh,
        in_specs=(
            rows,
            P(),
            P(),
            P(None, None, "head"),
            P(None, "head"),
            P("head", None),
            P(),
            P(),
            P(),
            P(None, "head"),
            P("head"),
            P("head", None),
            P(),
            rows,
            P("batch"),
        ),
        out_specs=(
            rows,
            rows,
            P(),
            P(),
            P(None, None, "head"),
            P(None, "head"),
            P("head", None),
            P(),
            P(),
            P(),
            P(None, "head"),
            P("head"),
            P("head", None),
            P(),
        ),
        check_vma=False,
    )
```

```python
import functools

import jax
import jax.numpy as jnp
from jax import lax
from jax.experimental import pallas as pl
from jax.experimental.pallas import tpu as pltpu
from jax.sharding import PartitionSpec as P

HD = 64
SHORT = 1024
F32 = jnp.float32
BF = jnp.bfloat16
LOG2E = 1.4426950408889634
GELU_C = 0.7978845608028654
CHUNK = 512
PAD = 64
QPAD = 32
VROWS = 16
MIB = 1024 * 1024
FWD_MIB = 11
BWD_MIB = 11
FFN_MIB = 10
BACK_MIB = 6
SUM_MIB = 3
SCALE = 0.5
S = jax.ShapeDtypeStruct
ANY = pl.BlockSpec(memory_space=pl.ANY)
SMEM = pl.BlockSpec(memory_space=pltpu.SMEM)
VMEM = pl.BlockSpec(memory_space=pltpu.VMEM)


def nt(a, b):
    return lax.dot_general(a, b, (((1,), (1,)), ((), ())), preferred_element_type=F32)


def nn(a, b):
    return lax.dot_general(a, b, (((1,), (0,)), ((), ())), preferred_element_type=F32)


def tn(a, b):
    return lax.dot_general(a, b, (((0,), (0,)), ((), ())), preferred_element_type=F32)


def head_mask(shape, h):
    lane = lax.broadcasted_iota(jnp.int32, shape, len(shape) - 1)
    return (lane >= h * HD) & (lane < (h + 1) * HD)


def lane_sum(e):
    width = min(128, e.shape[1])
    total = e[:, :width]
    for i in range(1, e.shape[1] // width):
        total = total + e[:, i * width : (i + 1) * width]
    return total


def ln_stats(v):
    c = v - jnp.mean(v, axis=1, keepdims=True)
    r = lax.rsqrt(jnp.mean(c * c, axis=1, keepdims=True) + 1e-5)
    return c * r, r


def as_row(ref):
    return ref[...].astype(F32).reshape(1, -1)


def load_rows(ref, start, count):
    return ref[pl.ds(pl.multiple_of(start, count), count), :]


def kept(shape, dtype):
    return pltpu.VMEM(shape, dtype)


def in_hbm(x):
    return pltpu.with_memory_space_constraint(x, pltpu.HBM)


def cost(us):
    return pl.CostEstimate(flops=int(us * SCALE * 1.1e9), bytes_accessed=0, transcendentals=0)


def place_in(g):
    me = lax.axis_index("head")
    return me % g, me // g


def params(mib):
    return pltpu.CompilerParams(vmem_limit_bytes=mib * MIB)


def qkv_kernel(g, norm, step, *rest):
    place, _ = place_in(g)
    rows, rest = rest[:g], rest[g:]
    if norm:
        vec_ref, *rest = rest
    pack_ref, q_ref, k_ref, v_ref = rest[:4]
    norm_out = rest[4:]
    R, D = rows[0].shape
    W = q_ref.shape[1]
    wt = pack_ref[0 : 3 * W, :]
    bias = pack_ref[4 * W : 4 * W + VROWS, :].astype(F32)[0:1, 0 : 3 * W]
    for r in range(g):
        base = (place + r) % g * R
        for j in range(0, R, step):
            a = rows[r][j : j + step, :]
            if norm:
                xh, _ = ln_stats(a.astype(F32))
                a = (xh * vec_ref[0:1, :] + vec_ref[1:2, :]).astype(BF)
                norm_out[r][j : j + step, :] = a
            t = (nt(a, wt) + bias).astype(BF)
            at = pl.ds(pl.multiple_of(base + j, step), step)
            q_ref[at, :] = t[:, :W]
            k_ref[at, :] = t[:, W : 2 * W]
            v_ref[at, :] = t[:, 2 * W :]


def project(rows, packed, vecs=None, step=256):
    g = len(rows)
    R, D = rows[0].shape
    W = (packed.shape[0] - VROWS) // 4
    L = g * R
    norm = vecs is not None
    args = [*rows, *([vecs] if norm else []), packed]
    outs = [kept((L, W), BF)] * 3
    if norm:
        outs += [kept((R, D), BF)] * g
    res = pl.pallas_call(
        functools.partial(qkv_kernel, g, norm, step),
        in_specs=[VMEM] * len(args),
        out_specs=[VMEM] * len(outs),
        out_shape=outs,
        compiler_params=params(4),
        cost_estimate=cost(2.0),
        name="norm_qkv" if norm else "qkv",
    )(*args)
    return res[:3], res[3:]


def fwd_kernel(bq, bk, nh, W, L, g, s_ref, q_ref, k_ref, v_ref, *rest):
    nck = L // CHUNK
    o_ref, st_ref = rest[:2]
    w_refs = rest[2 : 2 + nck]
    sends = rest[2 + nck :]
    nq = L // bq
    R = L // g
    place, _ = place_in(g)
    long = jnp.max(s_ref[...]) > 0

    def scaled_queries(at):
        qf = q_ref[at, :].astype(F32) * (LOG2E * HD**-0.5)
        hi = qf.astype(BF)
        lo = (qf - hi.astype(F32)).astype(BF)
        qs = []
        z = jnp.zeros_like(hi)
        for h in range(nh):
            m = head_mask(hi.shape, h)
            qs.append(jnp.concatenate([jnp.where(m, hi, z), jnp.where(m, lo, z)], axis=1))
        return qs

    def keys(at):
        kt = k_ref[at, :]
        return jnp.concatenate([kt, kt], axis=1)

    def values(at):
        vt = v_ref[at, :]
        z = jnp.zeros_like(vt)
        return [jnp.where(head_mask(vt.shape, h), vt, z) for h in range(nh)]

    def finish(at, acc, sums, bases):
        lane = lax.broadcasted_iota(jnp.int32, (bq, 128), 1)
        st = jnp.ones((bq, 128), F32)
        out = jnp.zeros((bq, W), F32)
        for h in range(nh):
            inv = 1.0 / sums[h]
            st = jnp.where(lane == h, inv, st)
            if bases is not None:
                st = jnp.where(lane == 8 + h, bases[h], st)
            out = jnp.where(head_mask(out.shape, h), acc * inv, out)
        st_ref[at, :] = st
        o_ref[at, :] = out.astype(BF)

    sq_r = lax.broadcasted_iota(jnp.int32, (bk, bk), 0)
    sq_c = lax.broadcasted_iota(jnp.int32, (bk, bk), 1)

    def fast(c, lo_blk):
        at = slice(c * bq, (c + 1) * bq)
        qs = scaled_queries(at)
        nr = bq // bk
        acc = [None] * nr
        ls = [[None] * nr for _ in range(nh)]
        for kb in range(lo_blk, (c + 1) * nr):
            base = kb * bk
            first = max(0, kb - c * nr)
            r0 = first * bk
            kt = keys(slice(base, base + bk))
            chunk = base // CHUNK
            top_row = c * bq - chunk * CHUNK
            wl = []
            for h in range(nh):
                s = nt(qs[h][r0:, :], kt)
                if base >= c * bq:
                    top = jnp.where(sq_c <= sq_r, s[:bk, :], 0.0)
                    s = top if r0 + bk == bq else jnp.concatenate([top, s[bk:, :]], axis=0)
                e = jnp.exp2(jnp.abs(s))
                x = (e - 1.0).astype(BF)
                wv = jnp.where(s.astype(BF) < 0, -x, x)
                t = lane_sum(e)
                for r in range(first, nr):
                    tr = t[(r - first) * bk : (r - first + 1) * bk, :]
                    ls[h][r] = tr if ls[h][r] is None else ls[h][r] + tr
                w_refs[chunk][h, top_row + r0 : top_row + bq, base % CHUNK : base % CHUNK + bk] = wv
                wl.append(wv)
            vcat = jnp.concatenate(values(slice(base, base + bk)), axis=0)
            res = nn(jnp.concatenate(wl, axis=1), vcat)
            for r in range(first, nr):
                part = res[(r - first) * bk : (r - first + 1) * bk, :]
                acc[r] = part if acc[r] is None else acc[r] + part
        row = lax.broadcasted_iota(jnp.int32, (bq, 1), 0)
        extra = (bk - 1 - row % bk).astype(F32)
        sums = [
            jnp.sum(jnp.concatenate(ls[h], axis=0), axis=1, keepdims=True) - extra
            for h in range(nh)
        ]
        finish(at, jnp.concatenate(acc, axis=0), sums, None)

    for c in range(nq):
        if c * bq < SHORT:
            fast(c, 0)
        else:
            pl.when(long)(functools.partial(fast, c, 0))
            pl.when(~long)(functools.partial(fast, c, SHORT // bk))

    lane = lax.broadcasted_iota(jnp.int32, (L, 128), 1)
    smallest = jnp.min(jnp.where(lane < nh, st_ref[...], 1.0))

    def slow(qi, _):
        at = pl.ds(pl.multiple_of(qi * bq, bq), bq)
        qs = scaled_queries(at)
        lo_blk = jnp.where(long | (qi * bq < SHORT), 0, SHORT // bk)
        hi_blk = (qi + 1) * (bq // bk)
        rows = lax.broadcasted_iota(jnp.int32, (bq, bk), 0) + qi * bq
        cols = lax.broadcasted_iota(jnp.int32, (bq, bk), 1)

        def scores(h, kb):
            kt = keys(pl.ds(pl.multiple_of(kb * bk, bk), bk))
            return nt(qs[h], kt), cols + kb * bk <= rows

        def top_step(kb, tops):
            new = []
            for h in range(nh):
                s, vis = scores(h, kb)
                mag = jnp.where(vis, jnp.abs(s), 0.0)
                new.append(jnp.maximum(tops[h], jnp.max(mag, axis=1, keepdims=True)))
            return tuple(new)

        tops = lax.fori_loop(lo_blk, hi_blk, top_step, (jnp.zeros((bq, 1), F32),) * nh)
        bases = [jnp.exp2(-t) for t in tops]

        def step(kb, carry):
            acc, sums = carry
            new = []
            vs = values(pl.ds(pl.multiple_of(kb * bk, bk), bk))
            for h in range(nh):
                s, vis = scores(h, kb)
                e = jnp.where(vis, jnp.exp2(jnp.abs(s) - tops[h]), 0.0)
                wv = jnp.where(s < 0, bases[h] - e, e - bases[h])
                wv = jnp.where(vis & (s != 0), wv, 0.0).astype(BF)
                new.append(sums[h] + jnp.sum(e, axis=1, keepdims=True))
                acc = acc + nn(wv, vs[h])
                for j in range(nck):

                    @pl.when(kb // (CHUNK // bk) == j)
                    def _():
                        top_row = pl.multiple_of(qi * bq - j * CHUNK, bq)
                        off = pl.multiple_of((kb % (CHUNK // bk)) * bk, bk)
                        w_refs[j][h, pl.ds(top_row, bq), pl.ds(off, bk)] = wv

            return acc, tuple(new)

        acc, sums = lax.fori_loop(
            lo_blk,
            hi_blk,
            step,
            (jnp.zeros((bq, W), F32), (jnp.zeros((bq, 1), F32),) * nh),
        )
        finish(at, acc, sums, bases)
        return 0

    @pl.when(smallest < 1e-25)
    def _():
        lax.fori_loop(0, nq, slow, 0)

    for r in range(1, g):
        sends[r - 1][...] = load_rows(o_ref, (place + r) % g * R, R)


def attn_fwd(flag, q, k, v, g, bq=512, bk=256):
    L, W = q.shape
    nh = W // HD
    nck = L // CHUNK
    res = pl.pallas_call(
        functools.partial(fwd_kernel, bq, bk, nh, W, L, g),
        in_specs=[VMEM] * 4,
        out_specs=[VMEM] * (2 + nck + g - 1),
        out_shape=[kept((L, W), BF), kept((L, 128), F32)]
        + [kept((nh, L - j * CHUNK, CHUNK), BF) for j in range(nck)]
        + [S((L // g, W), BF)] * (g - 1),
        compiler_params=params(FWD_MIB),
        cost_estimate=cost(7.0),
        name="attn_fwd",
    )(flag, q, k, v)
    return res[0], res[1], res[2 : 2 + nck], res[2 + nck :]


def bwd_kernel(h, bk, g, second, s_ref, q_ref, k_ref, v_ref, st_ref, o_ref, wt_ref, *rest):
    L, W = q_ref.shape
    nck = L // CHUNK
    do_refs = rest[:g]
    w_refs = rest[g : g + nck]
    n1_refs = rest[g + nck : 2 * g + nck]
    rest = rest[2 * g + nck :]
    if second:
        tq_ref, dk_ref, dv_ref, t_ref, gq_ref, vec_ref, bias_ref = rest
    else:
        tq_ref, dk_ref, dv_ref = rest
    D = wt_ref.shape[1]
    R = L // g
    place, _ = place_in(g)
    long = jnp.max(s_ref[...]) > 0
    sq_r = lax.broadcasted_iota(jnp.int32, (bk, bk), 0)
    sq_c = lax.broadcasted_iota(jnp.int32, (bk, bk), 1)
    lanes = slice(h * HD, (h + 1) * HD)
    bq = SHORT
    scale = HD**-0.5
    q_at, k_at, v_at = (slice(i * HD, (i + 1) * HD) for i in range(3))

    def body(c, lo_blk):
        nr = bq // bk
        rep = bk // 128
        at = slice(c * bq, (c + 1) * bq)
        tri = jnp.where(sq_c <= sq_r, 1.0, 0.0).astype(BF)
        st = st_ref[at, :]
        rows = []
        for lo in range(c * bq, (c + 1) * bq, min(bq, R)):
            here = slice(lo % R, lo % R + min(bq, R))
            x = do_refs[0][here, :]
            for r in range(1, g):
                x = jnp.where(lo // R == (place + r) % g, do_refs[r][here, :], x)
            rows.append(x)
        do = jnp.concatenate(rows, axis=0).astype(F32)
        do = jnp.where(head_mask((bq, W), h), do * st[:, h : h + 1], 0.0)
        delta = jnp.sum(do * o_ref[at, :].astype(F32), axis=1, keepdims=True)
        delta = jnp.concatenate([jnp.broadcast_to(delta, (bq, 128)).astype(BF)] * rep, 1)
        e0 = jnp.broadcast_to(st[:, 8 + h : 9 + h], (bq, 128)).astype(BF)
        e0 = jnp.concatenate([e0] * rep, 1)
        do_b = do.astype(BF)
        do_t = do.T[lanes, :].astype(BF)
        q_t = q_ref[at, :].astype(F32).T[lanes, :].astype(BF)
        dq = [None] * nr
        for kb in range(lo_blk, (c + 1) * nr):
            base = kb * bk
            first = max(0, kb - c * nr)
            r0 = first * bk
            chunk = base // CHUNK
            top_row = c * bq - chunk * CHUNK
            cols = slice(base, base + bk)
            wv = w_refs[chunk][h, top_row + r0 : top_row + bq, base % CHUNK : base % CHUNK + bk]
            wg = nt(do_b[r0:, :], v_ref[cols, :]).astype(BF)
            dl = delta[r0:, :]
            e = e0[r0:, :]
            if base >= c * bq:
                top = e[:bk, :] * tri
                e = top if r0 + bk == bq else jnp.concatenate([top, e[bk:, :]], axis=0)
            zero = jnp.zeros_like(wv)
            d = jnp.where(wv < 0, -dl, jnp.where(wv > 0, dl, zero))
            gr = (jnp.abs(wv) + e) * (wg - d)
            dv = nn(do_t[:, r0:], wv)
            dk = nn(q_t[:, r0:], gr)
            if not second:
                dv_ref[:, cols] = dv
                dk_ref[:, cols] = dk
            else:
                if base < SHORT:
                    dv = dv + dv_ref[:, cols]
                    dk = dk + dk_ref[:, cols]
                t_ref[k_at, cols] = (dk * scale).astype(BF)
                t_ref[v_at, cols] = dv.astype(BF)
            res = nn(gr, k_ref[cols, :])
            for r in range(first, nr):
                part = res[(r - first) * bk : (r - first + 1) * bk, :]
                dq[r] = part if dq[r] is None else dq[r] + part
        dq = (jnp.concatenate(dq, axis=0) * scale).T[lanes, :].astype(BF)
        if second:
            t_ref[q_at, at] = dq
        else:
            tq_ref[...] = dq

    if not second:
        body(0, 0)
        return
    t_ref[q_at, 0:SHORT] = tq_ref[...]
    pl.when(long)(functools.partial(body, 1, 0))

    @pl.when(~long)
    def _():
        t_ref[k_at, 0:SHORT] = (dk_ref[...] * scale).astype(BF)
        t_ref[v_at, 0:SHORT] = dv_ref[...].astype(BF)
        body(1, SHORT // bk)

    gq = jnp.zeros((3 * HD, D), F32)
    for r in range(g):
        start = pl.multiple_of((place + r) % g * R, R)
        gq = gq + nn(t_ref[:, pl.ds(start, R)], n1_refs[r][...])
    gq_ref[...] = gq.astype(BF)
    bias_ref[...] = nt(jnp.ones((VROWS, L), BF), t_ref[...])
    bias = jnp.sum(t_ref[...].astype(F32), axis=1, keepdims=True)
    wt = jnp.concatenate([wt_ref[i * W + h * HD : i * W + (h + 1) * HD, :] for i in range(3)], axis=0)
    wt = wt.astype(F32)
    vec_ref[...] = jnp.concatenate(
        [
            jnp.sum(wt * gq, axis=0, keepdims=True),
            jnp.sum(wt * bias, axis=0, keepdims=True),
            jnp.zeros((6, D), F32),
        ],
        axis=0,
    )


def attn_bwd(flag, h, q, k, v, st, o, wt, dos, ws, n1s, half=None, bk=256):
    L, W = q.shape
    g = len(dos)
    D = wt.shape[1]
    rows = 3 * HD
    second = half is not None
    args = [q, k, v, st, o, wt, *dos, *ws, *n1s, *(half or [])]
    if second:
        outs = [kept((rows, L), BF), kept((rows, D), BF), kept((8, D), F32), kept((VROWS, rows), F32)]
    else:
        outs = [kept((HD, SHORT), BF)] + [kept((HD, SHORT), F32)] * 2
    return pl.pallas_call(
        functools.partial(bwd_kernel, h, bk, g, second),
        in_specs=[VMEM] * (1 + len(args)),
        out_specs=[VMEM] * len(outs),
        out_shape=outs,
        compiler_params=params(BWD_MIB),
        cost_estimate=cost(2.1 + 3.0 * second),
        name="attn_bwd",
    )(flag, *args)


def ffn_kernel(g, slots, halves, todo, first, last, *refs):
    m = g * slots
    place, _ = place_in(g)
    it = iter(refs)

    def take(count):
        return [next(it) for _ in range(count)]

    ow_refs, up_refs, dn_refs = take(m if first or last else len(todo)), take(len(todo)), take(len(todo))
    (vec_ref,) = take(1)
    if first or last:
        o_refs, att_refs = take(slots), take(m - slots)
    if first:
        x_ref, cot_in = take(2)
    else:
        mids, n2, n2t, cots, cott, oacc_in, nacc_in = take(7)
    if first:
        mids, n2, n2t, cots, cott = take(5)
    if last:
        lo_ref, oacc = take(2)
        atg_refs, og_refs = take(m), take(m)
        (nacc,) = take(1)
        oacc_out = oacc
    else:
        oacc_out, nacc = take(2)
    ug_refs, dg_refs = take(len(todo)), take(len(todo))
    R, D = cots.shape
    FS = up_refs[0].shape[1]
    W = (ow_refs[0].shape[0] - VROWS) // 4
    step = R // halves
    blocks = [slice(j, j + step) for j in range(0, R, step)]

    def vec(i):
        return vec_ref[2 + i : 3 + i, :]

    def att_rows(at):
        rows = pl.ds(pl.multiple_of(place * R + at.start, step), step)
        return jnp.concatenate([o[rows, :] for o in o_refs] + [a[at, :] for a in att_refs], axis=1)

    if first or last:
        ow = jnp.concatenate([a[3 * W : 4 * W, :] for a in ow_refs], axis=0)
    if first:
        cots[...] = cot_in[...]
        for at in blocks:
            mid = x_ref[at, :].astype(F32) + nn(att_rows(at), ow) + vec(0)
            mids[at, :] = mid
            xh, _ = ln_stats(mid)
            y = xh * vec(1) + vec(2)
            n2[at, :] = y.astype(BF)
            n2t[:, at] = y.T.astype(BF)
            cott[:, at] = cots[at, :].astype(F32).T.astype(BF)

    for j, i in enumerate(todo):
        up = up_refs[j][...]
        dn = dn_refs[j][...]
        bias_ref = ow_refs[i if first or last else j]
        ub = bias_ref[4 * W : 4 * W + VROWS, :].astype(F32)[1:2, 0:FS]
        ug = dg = ubg = None
        for at in blocks:
            u = nn(n2[at, :], up) + ub
            ag = nt(cots[at, :], dn)
            u2 = u * u
            t = jnp.tanh(u * (GELU_C + (GELU_C * 0.044715) * u2))
            hh = 0.5 + 0.5 * t
            act = (u * hh).astype(BF)
            slope = hh + u * (0.5 - 0.5 * t * t) * (GELU_C + (3 * GELU_C * 0.044715) * u2)
            pgf = ag * slope
            pg = pgf.astype(BF)
            out = nn(act, dn)
            back = nt(pg, up)
            if j > 0:
                oacc_out[at, :] += out
                nacc[at, :] += back
            elif first:
                oacc_out[at, :] = mids[at, :] + vec(3) + out
                nacc[at, :] = back
            else:
                oacc_out[at, :] = oacc_in[at, :] + out
                nacc[at, :] = nacc_in[at, :] + back
            bsum = jnp.sum(pgf, axis=0, keepdims=True)
            gu = nn(n2t[:, at], pg)
            gd = nn(cott[:, at], act)
            ubg = bsum if ubg is None else ubg + bsum
            ug = gu if ug is None else ug + gu
            dg = gd if dg is None else dg + gd
        ug_refs[j][0:D, :] = ug.astype(BF)
        ug_refs[j][D:, :] = jnp.broadcast_to(ubg, (PAD, FS)).astype(BF)
        dg_refs[j][...] = dg.T.astype(BF)

    if not last:
        return
    mg_ref = oacc
    sums = [None] * 4
    og = None
    for at in blocks:
        lo_ref[at, :] = oacc[at, :].astype(BF)
        xh, rs = ln_stats(mids[at, :])
        ng = nacc[at, :]
        e = ng * vec(1)
        cf = cots[at, :].astype(F32)
        back = e - jnp.mean(e, axis=1, keepdims=True) - xh * jnp.mean(e * xh, axis=1, keepdims=True)
        mg = cf + rs * back
        mg_ref[at, :] = mg
        bg = mg.astype(BF)
        atg = nt(bg, ow).astype(BF)
        for i in range(m):
            atg_refs[i][at, :] = atg[:, i * W : (i + 1) * W]
        gr = tn(att_rows(at), bg)
        og = gr if og is None else og + gr
        for i, a in enumerate((bg.astype(F32), ng * xh, ng, cf)):
            a = jnp.sum(a, axis=0, keepdims=True)
            sums[i] = a if sums[i] is None else sums[i] + a
    og = og.astype(BF)
    both = jnp.concatenate(sums + [jnp.zeros((4, D), F32)], axis=0)
    hi = both.astype(BF).astype(F32)
    both = jnp.concatenate([hi, both - hi], axis=0).astype(BF)
    for i in range(m):
        og_refs[i][0:W, :] = og[i * W : (i + 1) * W, :]
        og_refs[i][W:, :] = both


def ffn(g, slots, todo, ow, up, dn, vecs, attended, start=None, state=None, last=False, halves=2):
    first = state is None
    R, D = (start[0] if first else state[0]).shape
    FS = up[0].shape[1]
    W = (ow[0].shape[0] - VROWS) // 4
    m = g * slots
    args = [*(ow if first or last else [ow[i] for i in todo])]
    args += [up[i] for i in todo] + [dn[i] for i in todo] + [vecs]
    if first or last:
        args += attended
    args += start if first else state
    outs = []
    if first:
        outs += [kept((R, D), F32), kept((R, D), BF), kept((D, R), BF), kept((R, D), BF), kept((D, R), BF)]
    if last:
        outs += [S((R, D), BF), kept((R, D), F32)] + [kept((R, W), BF)] * m + [kept((W + VROWS, D), BF)] * m
        outs += [kept((R, D), F32)]
    else:
        outs += [kept((R, D), F32)] * 2
    total_at = (1, 2 + 2 * m) if last else (5, 6) if first else (0, 1)
    alias = {} if first else {len(args) - 2: total_at[0], len(args) - 1: total_at[1]}
    outs += [kept((D + PAD, FS), BF)] * len(todo) + [kept((FS, D), BF)] * len(todo)
    res = pl.pallas_call(
        functools.partial(ffn_kernel, g, slots, halves, todo, first, last),
        in_specs=[VMEM] * len(args),
        out_specs=[VMEM] * len(outs),
        out_shape=outs,
        input_output_aliases=alias,
        compiler_params=params(FFN_MIB),
        cost_estimate=cost(5.0),
        name="ffn",
    )(*args)
    ugs, dgs = res[len(res) - 2 * len(todo) : len(res) - len(todo)], res[len(res) - len(todo) :]
    return res[: len(res) - 2 * len(todo)], dict(zip(todo, ugs)), dict(zip(todo, dgs))


def back_kernel(g, heads, last, rel, *refs):
    place, _ = place_in(g)
    count = len(heads)
    t_refs, wt_refs = refs[:count], refs[count : 2 * count]
    rest = refs[2 * count :]
    out_ref = rest[-1]
    R = out_ref.shape[0]
    start = pl.multiple_of((place + rel) % g * R, R)
    t = jnp.concatenate([a[:, pl.ds(start, R)] for a in t_refs], axis=0)
    wt = []
    for own, ref in zip(heads, wt_refs):
        W = (ref.shape[0] - VROWS) // 4
        wt += [ref[i * W + h * HD : i * W + (h + 1) * HD, :] for h in own for i in range(3)]
    n1g = tn(t, jnp.concatenate(wt, axis=0))
    if not last:
        out_ref[...] = n1g.astype(BF)
        return
    x_ref, mg_ref, vec_ref = rest[g - 1 : g + 2]
    for a in rest[: g - 1]:
        n1g = n1g + a[...].astype(F32)
    xh, rs = ln_stats(x_ref[...].astype(F32))
    e = n1g * vec_ref[0:1, :]
    back = e - jnp.mean(e, axis=1, keepdims=True) - xh * jnp.mean(e * xh, axis=1, keepdims=True)
    out_ref[...] = (mg_ref[...] + rs * back).astype(BF)


def row_back(g, rel, heads, ts, wts, R, last=None):
    D = wts[0].shape[1]
    args = [*ts, *wts] + ([] if last is None else [*last[0], *last[1:]])
    return pl.pallas_call(
        functools.partial(back_kernel, g, heads, last is not None, rel),
        in_specs=[VMEM] * len(args),
        out_specs=VMEM,
        out_shape=kept((R, D), BF) if last is None else S((R, D), BF),
        compiler_params=params(BACK_MIB),
        cost_estimate=cost(2.0),
        name="row_back" if last is None else "norm_back",
    )(*args)


def fuse(body, outs, *args, scratch=()):
    return pl.pallas_call(
        body,
        in_specs=[VMEM] * len(args),
        out_specs=[VMEM] * len(outs),
        out_shape=outs,
        scratch_shapes=list(scratch),
        compiler_params=params(SUM_MIB),
        name=body.__name__,
    )(*args)


def sum_of(refs, at):
    out = refs[0][at].astype(F32)
    for a in refs[1:]:
        out = out + a[at].astype(F32)
    return out.astype(BF)


def join_vec(v):
    v = v.astype(F32)
    return v[: VROWS // 2] + v[VROWS // 2 :]


def split_vec(v):
    hi = v.astype(BF).astype(F32)
    return jnp.concatenate([hi, v - hi], axis=0).astype(BF)


def vec_of(refs, at):
    return split_vec(functools.reduce(lambda a, b: a + b, [join_vec(a[at]) for a in refs]))


def pack_inputs(qkv_t, out_weight, qkv_bias, up_bias, tokens, long_slot, vecs):
    rows, D = qkv_t.shape
    W = out_weight.shape[0]
    flat = [up_bias, *vecs]
    slots = long_slot.shape[0]
    g = lax.axis_size("head") // slots

    def pack(qt_ref, ow_ref, qb_ref, x_ref, s_ref, *refs):
        flat_refs, refs = refs[: len(flat)], refs[len(flat) :]
        out, x_out, flag_ref, vec_ref, qb_in, s_in = refs[:6]
        flat_in, sems = refs[6:-1], refs[-1]
        pairs = [
            (qb_ref, qb_in),
            (s_ref, s_in),
            *zip(flat_refs, flat_in),
            (ow_ref, out.at[pl.ds(rows, W)]),
            (x_ref, x_out),
        ]
        copies = [pltpu.make_async_copy(a, b, sems.at[i]) for i, (a, b) in enumerate(pairs)]
        for c in copies:
            c.start()
        out[0:rows, :] = qt_ref[...]
        for c in copies[:-2]:
            c.wait()
        qb = qb_in[...].astype(F32)
        qb = jnp.concatenate([qb[i : i + 1, :] for i in range(3)], axis=1)
        lines = [qb, as_row(flat_in[0]), jnp.zeros((VROWS - 2, D), F32)]
        lines = [jnp.pad(a, ((0, 0), (0, D - a.shape[1]))) for a in lines]
        out[rows + W :, :] = jnp.concatenate(lines, axis=0).astype(BF)
        vec_ref[...] = jnp.concatenate(
            [as_row(a) for a in flat_in[1:]] + [jnp.zeros((2, D), F32)], axis=0
        )
        _, group = place_in(g)
        flag_ref[...] = jnp.full((8, 128), (s_in[group] > 0).astype(F32))
        for c in copies[-2:]:
            c.wait()

    hbm = [in_hbm(a) for a in (out_weight, qkv_bias, tokens, long_slot, *flat)]
    return pl.pallas_call(
        pack,
        in_specs=[VMEM] + [ANY] * len(hbm),
        out_specs=[VMEM] * 4,
        out_shape=[
            kept((rows + W + VROWS, D), BF),
            kept(tokens.shape, BF),
            kept((8, 128), F32),
            kept((8, D), F32),
        ],
        scratch_shapes=[pltpu.VMEM(qkv_bias.shape, BF), pltpu.SMEM((slots,), jnp.int32)]
        + [pltpu.VMEM(a.shape, BF) for a in flat]
        + [pltpu.SemaphoreType.DMA((4 + len(flat),))],
        compiler_params=params(SUM_MIB),
        name="pack",
    )(qkv_t, *hbm)


def half_at(bit, count, mine):
    place = lax.axis_index("batch") // 2**bit % 2
    place = place if mine else 1 - place
    return pl.ds(pl.multiple_of(place * count, count), count)


def add_up(terms, vec_rows=0):
    rows, cols = terms[0].shape
    count = rows - vec_rows

    def sum_terms(*refs):
        ins, out = refs[: len(terms)], refs[len(terms)]
        if count:
            out[0:count, :] = sum_of(ins, slice(0, count))
        if vec_rows:
            out[count:, :] = vec_of(ins, slice(count, rows))

    return fuse(sum_terms, [kept((rows, cols), BF)], *terms)[0]


def with_vec(terms, vec):
    rows, cols = terms[0].shape

    def sum_vec(*refs):
        ins, vec_ref, out = refs[: len(terms)], refs[-2], refs[-1]
        out[0:rows, :] = sum_of(ins, slice(0, rows))
        out[rows:, :] = vec_ref[...]

    return fuse(sum_vec, [kept((rows + VROWS, cols), BF)], *terms, vec)[0]


def halve(bit, terms, has_vec=False):
    rows, cols = terms[0].shape
    count = (rows - VROWS if has_vec else rows) // 2

    def sum_halves(*refs):
        ins, outs = refs[: len(terms)], refs[len(terms) :]
        for out, mine in zip(outs, (True, False)):
            out[0:count, :] = sum_of(ins, half_at(bit, count, mine))
            if has_vec:
                out[count:, :] = vec_of(ins, slice(2 * count, rows))

    return fuse(sum_halves, [kept((count + VROWS * has_vec, cols), BF)] * 2, *terms)


def stack_sums(downs, outs_):
    fs, cols = downs[0].shape
    rows = fs + outs_[0].shape[0]

    def sum_pieces(*refs):
        ins, out = refs[:-1], refs[-1]
        out[0:fs, :] = sum_of(ins[: len(downs)], slice(0, fs))
        out[fs : rows - VROWS, :] = sum_of(ins[len(downs) :], slice(0, rows - fs - VROWS))
        out[rows - VROWS :, :] = vec_of(ins[len(downs) :], slice(rows - fs - VROWS, rows - fs))

    return fuse(sum_pieces, [kept((rows, cols), BF)], *downs, *outs_)[0]


def join(bit, mine, other, count):
    def join_halves(mine_ref, other_ref, out):
        out[half_at(bit, count, True), :] = mine_ref[0:count, :]
        out[half_at(bit, count, False), :] = other_ref[0:count, :]

    return fuse(join_halves, [kept((2 * count, mine.shape[1]), BF)], mine, other)[0]


def collect(mine, other, count, splits, has_vec=False):
    cols = mine.shape[1]

    def gather_halves(mine_ref, other_ref, *refs):
        outs, whole = refs[:-1], refs[-1]
        whole[half_at(0, count, True), :] = mine_ref[0:count, :].astype(F32)
        whole[half_at(0, count, False), :] = other_ref[0:count, :].astype(F32)
        first = 0
        for out, size in zip(outs, splits):
            out[...] = whole[first : first + size, :]
            first += size
        if has_vec:
            at = slice(count, count + VROWS)
            outs[-1][...] = join_vec(mine_ref[at, :]) + join_vec(other_ref[at, :])

    return fuse(
        gather_halves,
        [S((a, cols), F32) for a in splits] + [S((VROWS // 2, cols), F32)] * has_vec,
        mine,
        other,
        scratch=[pltpu.VMEM((2 * count, cols), F32)],
    )


def fill_rows(ref, g_ref, bias_ref):
    rows = g_ref.shape[0]
    ref[0:rows, :] = g_ref[...]
    ref[rows:, :] = jnp.zeros((ref.shape[0] - rows, ref.shape[1]), BF)
    ref[rows : rows + VROWS, 0 : bias_ref.shape[1]] = bias_ref[...].astype(BF)


def q_rows(gq, bias):
    def stack_rows(g_ref, bias_ref, out):
        fill_rows(out, g_ref, bias_ref)

    return fuse(stack_rows, [kept((gq.shape[0] + QPAD, gq.shape[1]), BF)], gq, bias)[0]


def q_halve(gq, bias, crossed):
    rows, cols = gq.shape[0] + QPAD, gq.shape[1]
    count = rows // 2

    def sum_rows(g_ref, bias_ref, *refs):
        c_refs = refs[: len(crossed)]
        mine, other, whole = refs[-3:]
        fill_rows(whole, g_ref, bias_ref)
        for out, which in ((mine, True), (other, False)):
            out[...] = sum_of([whole, *c_refs], half_at(0, count, which))

    return fuse(
        sum_rows,
        [kept((count, cols), BF)] * 2,
        gq,
        bias,
        *crossed,
        scratch=[pltpu.VMEM((rows, cols), BF)],
    )


def after(x, *deps):
    return lax.optimization_barrier((x,) + deps)[0]


class Chain:
    def __init__(self, steps):
        self.steps = steps
        self.result = None
        self.sent, self.got = next(steps)

    def tick(self, *deps):
        if self.result is None:
            try:
                self.sent, self.got = self.steps.send(after(self.got, *deps))
            except StopIteration as stop:
                self.result = stop.value
                self.sent = []


def vec_split(v):
    hi = lax.reduce_precision(v, 8, 7)
    return jnp.concatenate([hi, v - hi], axis=0).astype(BF)


def vec_join(v):
    half = v.shape[0] // 2
    return v[:half].astype(F32) + v[half:].astype(F32)


def per_device(
    tokens_in,
    norm1_gain,
    norm1_bias,
    qkv_weight,
    qkv_bias,
    out_weight,
    out_bias,
    norm2_gain,
    norm2_bias,
    up_weight,
    up_bias,
    down_weight,
    down_bias,
    cotangent,
    long_slot,
):
    n = lax.axis_size("head")
    nb = lax.axis_size("batch")
    slots = long_slot.shape[0]
    g = n // slots
    R, D = tokens_in.shape
    W = qkv_weight.shape[2]
    FS = up_weight.shape[1]
    nh = W // HD
    bits = []
    while 2 ** len(bits) < nb:
        bits.append(2 ** len(bits))

    def cross(x, r):
        return lax.ppermute(x, "head", [(i, (i + r * g) % n) for i in range(n)])

    def rot(x, r):
        return lax.ppermute(x, "head", [(i, i // g * g + (i % g - r) % g) for i in range(n)])

    def flip(x, bit):
        return lax.ppermute(x, "batch", [(i, i ^ bit) for i in range(nb)])

    def exchanged(a):
        return [a] + [cross(a, r) for r in range(1, slots)]

    xs = [tokens_in] + [rot(tokens_in, r) for r in range(1, g)]
    qkv_t = qkv_weight.transpose(1, 2, 0).reshape(3 * W, D)
    small = [norm1_gain, norm1_bias, out_bias, norm2_gain, norm2_bias, down_bias]
    packed, x_own, flag, vecs = pack_inputs(
        qkv_t, out_weight, qkv_bias, up_bias, tokens_in, long_slot, small
    )
    packed = exchanged(packed)
    qkv, n1s = project([x_own] + xs[1:], packed[0], vecs)

    saved = []
    att = []
    for ph in range(slots):
        if ph:
            qkv, _ = project(n1s, after(packed[ph], saved[-1][3]))
        first = qkv[0] if ph == 0 else after(qkv[0], upw[0], dnw[0])
        o, st, ws, sends = attn_fwd(flag, first, *qkv[1:], g)
        saved.append((*qkv, st, o, packed[ph], ws))
        att.append([rot(sends[g - r - 1], r) for r in range(1, g)])
        if ph == 0:
            upw = exchanged(after(up_weight, vecs))
            dnw = exchanged(after(down_weight, st))
            oww = [packed[0]] + [after(b, st) for b in packed[1:]]

    def at(r, ph):
        return r * slots + ph

    def members_of(a):
        return {(r, ph): rot(b, r) if r else b for r in range(g) for ph, b in a}

    def listed(a):
        return [a.get((r, ph)) for r in range(g) for ph in range(slots)]

    ow = listed(members_of(list(enumerate(oww))))
    ups, dns = members_of([(0, upw[0])]), members_of([(0, dnw[0])])
    attended = [a[4] for a in saved] + [att[ph][r - 1] for r in range(1, g) for ph in range(slots)]

    def members(parts):
        return [rot(parts[(g - r) % g], r) for r in range(1, g)]

    def over_batch(terms, has_vec):
        mine, other = halve(1, terms, has_vec)
        got = yield [mine, other], flip(other, bits[1])
        mat = add_up([mine, got], VROWS * has_vec)
        for bit in bits[2:]:
            got = yield [mat], flip(mat, bit)
            mat = add_up([mat, got], VROWS * has_vec)
        got = yield [mat], flip(mat, bits[1])
        count = mat.shape[0] - VROWS * has_vec
        whole = join(1, mat, got, count)
        return (whole, mat[count:]) if has_vec else whole

    ug, dg = {}, {}

    def chain_u():
        others = range(1, slots)
        got = yield [ug[at(r, ph)] for r in range(1, g) for ph in others], [
            [rot(ug[at((g - r) % g, ph)], r) for r in range(1, g)] for ph in others
        ]
        sums = [add_up([ug[at(0, ph)]] + a) for ph, a in zip(others, got)]
        got = yield sums, [cross(sums[slots - r - 1], slots - r) for r in others]
        mine, other = halve(0, [ug[at(0, 0)]] + near + got)
        got = yield [mine, other], flip(other, bits[0])
        mat = yield from over_batch([mine, got], False)
        got = yield [mat], flip(mat, bits[0])
        return collect(mat, got, mat.shape[0], (D, PAD))

    def chain_d():
        got = yield list(dg.values()) + list(og), [
            [[rot(b, r) for b in (dg[at((g - r) % g, ph)], og[at((g - r) % g, ph)])] for r in range(1, g)]
            for ph in range(slots)
        ]
        sums = [
            stack_sums([dg[at(0, ph)]] + [a[0] for a in got[ph]],
                [og[at(0, ph)]] + [a[1] for a in got[ph]],
            )
            for ph in range(slots)
        ]
        got = yield sums, [cross(sums[slots - r], slots - r) for r in range(1, slots)]
        mine, other = halve(0, [sums[0]] + got, True)
        got = yield [mine, other], flip(other, bits[0])
        mat, vec = yield from over_batch([mine, got], True)
        got = yield [mat], flip(mat, bits[0])
        return [*collect(mat, got, mat.shape[0], (FS, W)), vec]

    def part(todo, **more):
        out, new_ug, new_dg = ffn(g, slots, todo, ow, listed(ups), listed(dns), vecs, attended, **more)
        ug.update(new_ug)
        dg.update(new_dg)
        return out

    state = list(part([at(0, 0)], start=[after(x_own, *upw[1:]), cotangent]))
    ups.update(members_of([(ph, upw[ph]) for ph in range(1, slots)]))
    dns.update(members_of([(ph, after(dnw[ph], state[5])) for ph in range(1, slots)]))
    state[5] = after(state[5], *[dns[0, ph] for ph in range(1, slots)])
    out = part([at(r, 0) for r in range(1, g)], state=state)
    state = [*state[:5], *out]
    near = [rot(ug[at((g - r) % g, 0)], r) for r in range(1, g)]
    out = part([at(r, ph) for r in range(1, g) for ph in range(1, slots)], state=state)
    state = [*state[:5], *out]
    u = Chain(chain_u())
    state[5] = after(state[5], *u.sent)
    out = part([at(0, ph) for ph in range(1, slots)], state=state, last=True)
    u.tick(out[0])
    m = g * slots
    lo, mg, atg, og = out[0], out[1], out[2 : 2 + m], out[2 + m : 2 + 2 * m]
    dos = [
        [atg[ph]] + [rot(atg[(g - r) * slots + ph], r) for r in range(1, g)] for ph in range(slots)
    ]
    chains = {"u": u, "d": Chain(chain_d())}
    plan = ["d", "", "u", "", "ud", "ud", "d", "u"]
    grads = {}
    crossing = {}
    done = 0

    def sent():
        return [a for c in chains.values() for a in c.sent]

    def advance(*deps):
        nonlocal done
        for name, chain in chains.items():
            if name[0] == "q" or done >= len(plan) or name in plan[done]:
                chain.tick(*deps)
        done += 1

    def chain_v():
        def first_sum(*refs):
            vec = functools.reduce(lambda a, b: a + b, [v[...] for v in refs[:-1]])
            refs[-1][...] = split_vec(vec)

        parts = [grads[key][2] for key in grads]
        vec = fuse(first_sum, [kept((VROWS, D), BF)], *parts)[0]
        got = yield [vec], [rot(vec, r) for r in range(1, g)]
        vec = add_up([vec] + got, VROWS)
        got = yield [vec], [cross(vec, r) for r in range(1, slots)]
        return add_up([vec] + got, VROWS)

    def chain_q(h):
        res = grads[0, h]
        last = h == nh - 1
        crossed = [crossing[ph, h] for ph in range(1, slots)]
        mine, other = q_halve(res[1], res[3], crossed)
        got = yield [mine, other], flip(other, bits[0])
        if not last:
            mat = add_up([mine, got])
            for bit in bits[1:]:
                got = yield [mat], flip(mat, bit)
                mat = add_up([mat, got])
            got = yield [mat], flip(mat, bits[0])
            return collect(mat, got, mat.shape[0], (2 * mat.shape[0],))
        count = mine.shape[0]
        mat = with_vec([mine, got], chains["v"].result)
        for bit in bits[1:]:
            got = yield [mat], flip(mat, bit)
            mat = add_up([mat, got], VROWS)
        got = yield [mat], flip(mat, bits[0])
        return collect(mat, got, count, (2 * count,), True)

    dep = ()
    for ph in list(range(1, slots)) + [0]:
        q, k, v, st, o, pk, ws = saved[ph]
        for h in range(nh):
            args = [k, v, st, o, pk, dos[ph], ws, n1s]
            half = attn_bwd(flag, h, after(q, *sent(), *dep), *args)
            advance(half[0])
            res = attn_bwd(flag, h, after(q, *sent(), half[0]), *args, half)
            grads[ph, h] = res
            dep = (res[1],)
            advance(res[1])
            if ph:
                crossing[ph, h] = cross(q_rows(res[1], res[3]), slots - ph)
            else:
                chains["q%d" % h] = Chain(chain_q(h))
    chains["v"] = Chain(chain_v())

    order = [(ph, h) for ph in range(slots) for h in range(nh)]
    ts = [grads[key][0] for key in order]
    pks = [saved[ph][5] for ph, h in order]
    head_list = [(h,) for ph, h in order]
    sends = {}
    for r in range(1, g):
        sends[r] = row_back(g, r, head_list, [after(ts[0], *sent())] + ts[1:], pks, R)
    got = [rot(sends[(g - r) % g], r) for r in range(1, g)]
    chains["v"].tick(*sends.values())
    first = after(ts[0], *chains["v"].sent)
    input_grad = row_back(g, 0, head_list, [first] + ts[1:], pks, R, (got, x_own, mg, vecs))
    dep = [input_grad]
    chains["v"].tick(*dep)
    final = "q%d" % (nh - 1)
    tail = [[final, "u", "d"], [final, "q0", "d"], [final, "u", "d"]]
    while any(c.result is None for c in chains.values()):
        names = (tail.pop(0) if tail else None) or list(chains)[::-1]
        for name in names:
            c = chains[name]
            c.tick(*dep)
            dep = c.sent[:1] or dep
    results = {name: c.result for name, c in chains.items()}
    (up_grad, up_bias_grad), (down_grad, out_grad, vec2) = results["u"], results["d"]
    qs = [results["q%d" % h] for h in range(nh)]
    vec1 = qs[-1][1]
    qf = [a[0] for a in qs]
    vec2 = vec_join(vec2)
    gain_grad = (vec1[0] - norm1_bias.astype(F32) * vec1[1]) / norm1_gain.astype(F32)
    qkv_grad = jnp.concatenate([a[: 3 * HD].reshape(3, HD, D) for a in qf], axis=1).transpose(2, 0, 1)
    qkv_bias_grad = jnp.concatenate([a[3 * HD, : 3 * HD].reshape(3, HD) for a in qf], axis=1)
    return (
        lo,
        input_grad,
        gain_grad,
        vec1[1],
        qkv_grad,
        qkv_bias_grad,
        out_grad,
        vec2[0],
        vec2[1],
        vec2[2],
        up_grad,
        up_bias_grad[0],
        down_grad,
        vec2[3],
    )


def solution(mesh):
    rows = P(("batch", "head"), None)
    return jax.shard_map(
        per_device,
        mesh=mesh,
        in_specs=(
            rows,
            P(),
            P(),
            P(None, None, "head"),
            P(None, "head"),
            P("head", None),
            P(),
            P(),
            P(),
            P(None, "head"),
            P("head"),
            P("head", None),
            P(),
            rows,
            P("batch"),
        ),
        out_specs=(
            rows,
            rows,
            P(),
            P(),
            P(None, None, "head"),
            P(None, "head"),
            P("head", None),
            P(),
            P(),
            P(),
            P(None, "head"),
            P("head"),
            P("head", None),
            P(),
        ),
        check_vma=False,
    )
```

```python
import functools

import jax
import jax.numpy as jnp
from jax import lax
from jax.experimental import pallas as pl
from jax.experimental.pallas import tpu as pltpu
from jax.sharding import PartitionSpec as P

HD = 64
SHORT = 1024
F32 = jnp.float32
BF = jnp.bfloat16
LOG2E = 1.4426950408889634
GELU_C = 0.7978845608028654
CHUNK = 512
PAD = 64
QPAD = 32
VROWS = 16
MIB = 1024 * 1024
FWD_MIB = 11
BWD_MIB = 11
FFN_MIB = 10
BACK_MIB = 6
SUM_MIB = 3
SCALE = 0.5
S = jax.ShapeDtypeStruct
ANY = pl.BlockSpec(memory_space=pl.ANY)
SMEM = pl.BlockSpec(memory_space=pltpu.SMEM)
VMEM = pl.BlockSpec(memory_space=pltpu.VMEM)


def nt(a, b):
    return lax.dot_general(a, b, (((1,), (1,)), ((), ())), preferred_element_type=F32)


def nn(a, b):
    return lax.dot_general(a, b, (((1,), (0,)), ((), ())), preferred_element_type=F32)


def tn(a, b):
    return lax.dot_general(a, b, (((0,), (0,)), ((), ())), preferred_element_type=F32)


def head_mask(shape, h):
    lane = lax.broadcasted_iota(jnp.int32, shape, len(shape) - 1)
    return (lane >= h * HD) & (lane < (h + 1) * HD)


def lane_sum(e):
    width = min(128, e.shape[1])
    total = e[:, :width]
    for i in range(1, e.shape[1] // width):
        total = total + e[:, i * width : (i + 1) * width]
    return total


def ln_stats(v):
    c = v - jnp.mean(v, axis=1, keepdims=True)
    r = lax.rsqrt(jnp.mean(c * c, axis=1, keepdims=True) + 1e-5)
    return c * r, r


def as_row(ref):
    return ref[...].astype(F32).reshape(1, -1)


def load_rows(ref, start, count):
    return ref[pl.ds(pl.multiple_of(start, count), count), :]


def kept(shape, dtype):
    return pltpu.VMEM(shape, dtype)


def in_hbm(x):
    return pltpu.with_memory_space_constraint(x, pltpu.HBM)


def cost(us):
    return pl.CostEstimate(flops=int(us * SCALE * 1.1e9), bytes_accessed=0, transcendentals=0)


def place_in(g):
    me = lax.axis_index("head")
    return me % g, me // g


def params(mib):
    return pltpu.CompilerParams(vmem_limit_bytes=mib * MIB)


def qkv_kernel(g, norm, step, *rest):
    place, _ = place_in(g)
    rows, rest = rest[:g], rest[g:]
    if norm:
        vec_ref, *rest = rest
    pack_ref, q_ref, k_ref, v_ref = rest[:4]
    norm_out = rest[4:]
    R, D = rows[0].shape
    W = q_ref.shape[1]
    wt = pack_ref[0 : 3 * W, :]
    bias = pack_ref[4 * W : 4 * W + VROWS, :].astype(F32)[0:1, 0 : 3 * W]
    for r in range(g):
        base = (place + r) % g * R
        for j in range(0, R, step):
            a = rows[r][j : j + step, :]
            if norm:
                xh, _ = ln_stats(a.astype(F32))
                a = (xh * vec_ref[0:1, :] + vec_ref[1:2, :]).astype(BF)
                norm_out[r][j : j + step, :] = a
            t = (nt(a, wt) + bias).astype(BF)
            at = pl.ds(pl.multiple_of(base + j, step), step)
            q_ref[at, :] = t[:, :W]
            k_ref[at, :] = t[:, W : 2 * W]
            v_ref[at, :] = t[:, 2 * W :]


def project(rows, packed, vecs=None, step=512):
    g = len(rows)
    R, D = rows[0].shape
    W = (packed.shape[0] - VROWS) // 4
    L = g * R
    norm = vecs is not None
    args = [*rows, *([vecs] if norm else []), packed]
    outs = [kept((L, W), BF)] * 3
    if norm:
        outs += [kept((R, D), BF)] * g
    res = pl.pallas_call(
        functools.partial(qkv_kernel, g, norm, step),
        in_specs=[VMEM] * len(args),
        out_specs=[VMEM] * len(outs),
        out_shape=outs,
        compiler_params=params(7),
        cost_estimate=cost(2.0),
        name="norm_qkv" if norm else "qkv",
    )(*args)
    return res[:3], res[3:]


def fwd_kernel(bq, bk, nh, W, L, g, s_ref, q_ref, k_ref, v_ref, *rest):
    nck = L // CHUNK
    o_ref, st_ref = rest[:2]
    w_refs = rest[2 : 2 + nck]
    sends = rest[2 + nck :]
    nq = L // bq
    R = L // g
    place, _ = place_in(g)
    long = jnp.max(s_ref[...]) > 0

    def scaled_queries(at):
        qf = q_ref[at, :].astype(F32) * (LOG2E * HD**-0.5)
        hi = qf.astype(BF)
        lo = (qf - hi.astype(F32)).astype(BF)
        qs = []
        z = jnp.zeros_like(hi)
        for h in range(nh):
            m = head_mask(hi.shape, h)
            qs.append(jnp.concatenate([jnp.where(m, hi, z), jnp.where(m, lo, z)], axis=1))
        return qs

    def keys(at):
        kt = k_ref[at, :]
        return jnp.concatenate([kt, kt], axis=1)

    def values(at):
        vt = v_ref[at, :]
        z = jnp.zeros_like(vt)
        return [jnp.where(head_mask(vt.shape, h), vt, z) for h in range(nh)]

    def finish(at, acc, sums, bases):
        lane = lax.broadcasted_iota(jnp.int32, (bq, 128), 1)
        st = jnp.ones((bq, 128), F32)
        out = jnp.zeros((bq, W), F32)
        for h in range(nh):
            inv = 1.0 / sums[h]
            st = jnp.where(lane == h, inv, st)
            if bases is not None:
                st = jnp.where(lane == 8 + h, bases[h], st)
            out = jnp.where(head_mask(out.shape, h), acc * inv, out)
        st_ref[at, :] = st
        o_ref[at, :] = out.astype(BF)

    sq_r = lax.broadcasted_iota(jnp.int32, (bk, bk), 0)
    sq_c = lax.broadcasted_iota(jnp.int32, (bk, bk), 1)

    def fast(c, lo_blk):
        at = slice(c * bq, (c + 1) * bq)
        qs = scaled_queries(at)
        nr = bq // bk
        acc = [None] * nr
        ls = [[None] * nr for _ in range(nh)]
        for kb in range(lo_blk, (c + 1) * nr):
            base = kb * bk
            first = max(0, kb - c * nr)
            r0 = first * bk
            kt = keys(slice(base, base + bk))
            chunk = base // CHUNK
            top_row = c * bq - chunk * CHUNK
            wl = []
            for h in range(nh):
                s = nt(qs[h][r0:, :], kt)
                if base >= c * bq:
                    top = jnp.where(sq_c <= sq_r, s[:bk, :], 0.0)
                    s = top if r0 + bk == bq else jnp.concatenate([top, s[bk:, :]], axis=0)
                e = jnp.exp2(jnp.abs(s))
                x = (e - 1.0).astype(BF)
                wv = jnp.where(s.astype(BF) < 0, -x, x)
                t = lane_sum(e)
                for r in range(first, nr):
                    tr = t[(r - first) * bk : (r - first + 1) * bk, :]
                    ls[h][r] = tr if ls[h][r] is None else ls[h][r] + tr
                w_refs[chunk][h, top_row + r0 : top_row + bq, base % CHUNK : base % CHUNK + bk] = wv
                wl.append(wv)
            vcat = jnp.concatenate(values(slice(base, base + bk)), axis=0)
            res = nn(jnp.concatenate(wl, axis=1), vcat)
            for r in range(first, nr):
                part = res[(r - first) * bk : (r - first + 1) * bk, :]
                acc[r] = part if acc[r] is None else acc[r] + part
        row = lax.broadcasted_iota(jnp.int32, (bq, 1), 0)
        extra = (bk - 1 - row % bk).astype(F32)
        sums = [
            jnp.sum(jnp.concatenate(ls[h], axis=0), axis=1, keepdims=True) - extra
            for h in range(nh)
        ]
        finish(at, jnp.concatenate(acc, axis=0), sums, None)

    for c in range(nq):
        if c * bq < SHORT:
            fast(c, 0)
        else:
            pl.when(long)(functools.partial(fast, c, 0))
            pl.when(~long)(functools.partial(fast, c, SHORT // bk))

    lane = lax.broadcasted_iota(jnp.int32, (L, 128), 1)
    smallest = jnp.min(jnp.where(lane < nh, st_ref[...], 1.0))

    def slow(qi, _):
        at = pl.ds(pl.multiple_of(qi * bq, bq), bq)
        qs = scaled_queries(at)
        lo_blk = jnp.where(long | (qi * bq < SHORT), 0, SHORT // bk)
        hi_blk = (qi + 1) * (bq // bk)
        rows = lax.broadcasted_iota(jnp.int32, (bq, bk), 0) + qi * bq
        cols = lax.broadcasted_iota(jnp.int32, (bq, bk), 1)

        def scores(h, kb):
            kt = keys(pl.ds(pl.multiple_of(kb * bk, bk), bk))
            return nt(qs[h], kt), cols + kb * bk <= rows

        def top_step(kb, tops):
            new = []
            for h in range(nh):
                s, vis = scores(h, kb)
                mag = jnp.where(vis, jnp.abs(s), 0.0)
                new.append(jnp.maximum(tops[h], jnp.max(mag, axis=1, keepdims=True)))
            return tuple(new)

        tops = lax.fori_loop(lo_blk, hi_blk, top_step, (jnp.zeros((bq, 1), F32),) * nh)
        bases = [jnp.exp2(-t) for t in tops]

        def step(kb, carry):
            acc, sums = carry
            new = []
            vs = values(pl.ds(pl.multiple_of(kb * bk, bk), bk))
            for h in range(nh):
                s, vis = scores(h, kb)
                e = jnp.where(vis, jnp.exp2(jnp.abs(s) - tops[h]), 0.0)
                wv = jnp.where(s < 0, bases[h] - e, e - bases[h])
                wv = jnp.where(vis & (s != 0), wv, 0.0).astype(BF)
                new.append(sums[h] + jnp.sum(e, axis=1, keepdims=True))
                acc = acc + nn(wv, vs[h])
                for j in range(nck):

                    @pl.when(kb // (CHUNK // bk) == j)
                    def _():
                        top_row = pl.multiple_of(qi * bq - j * CHUNK, bq)
                        off = pl.multiple_of((kb % (CHUNK // bk)) * bk, bk)
                        w_refs[j][h, pl.ds(top_row, bq), pl.ds(off, bk)] = wv

            return acc, tuple(new)

        acc, sums = lax.fori_loop(
            lo_blk,
            hi_blk,
            step,
            (jnp.zeros((bq, W), F32), (jnp.zeros((bq, 1), F32),) * nh),
        )
        finish(at, acc, sums, bases)
        return 0

    @pl.when(smallest < 1e-25)
    def _():
        lax.fori_loop(0, nq, slow, 0)

    for r in range(1, g):
        sends[r - 1][...] = load_rows(o_ref, (place + r) % g * R, R)


def attn_fwd(flag, q, k, v, g, bq=512, bk=256):
    L, W = q.shape
    nh = W // HD
    nck = L // CHUNK
    res = pl.pallas_call(
        functools.partial(fwd_kernel, bq, bk, nh, W, L, g),
        in_specs=[VMEM] * 4,
        out_specs=[VMEM] * (2 + nck + g - 1),
        out_shape=[kept((L, W), BF), kept((L, 128), F32)]
        + [kept((nh, L - j * CHUNK, CHUNK), BF) for j in range(nck)]
        + [S((L // g, W), BF)] * (g - 1),
        compiler_params=params(FWD_MIB),
        cost_estimate=cost(7.0),
        name="attn_fwd",
    )(flag, q, k, v)
    return res[0], res[1], res[2 : 2 + nck], res[2 + nck :]


def bwd_kernel(h, bk, g, second, s_ref, q_ref, k_ref, v_ref, st_ref, o_ref, wt_ref, *rest):
    L, W = q_ref.shape
    nck = L // CHUNK
    do_refs = rest[:g]
    w_refs = rest[g : g + nck]
    n1_refs = rest[g + nck : 2 * g + nck]
    rest = rest[2 * g + nck :]
    if second:
        tq_ref, dk_ref, dv_ref, t_ref, gq_ref, vec_ref, bias_ref = rest
    else:
        tq_ref, dk_ref, dv_ref = rest
    D = wt_ref.shape[1]
    R = L // g
    place, _ = place_in(g)
    long = jnp.max(s_ref[...]) > 0
    sq_r = lax.broadcasted_iota(jnp.int32, (bk, bk), 0)
    sq_c = lax.broadcasted_iota(jnp.int32, (bk, bk), 1)
    lanes = slice(h * HD, (h + 1) * HD)
    bq = SHORT
    scale = HD**-0.5
    q_at, k_at, v_at = (slice(i * HD, (i + 1) * HD) for i in range(3))

    def body(c, lo_blk):
        nr = bq // bk
        rep = bk // 128
        at = slice(c * bq, (c + 1) * bq)
        tri = jnp.where(sq_c <= sq_r, 1.0, 0.0).astype(BF)
        st = st_ref[at, :]
        rows = []
        for lo in range(c * bq, (c + 1) * bq, min(bq, R)):
            here = slice(lo % R, lo % R + min(bq, R))
            x = do_refs[0][here, :]
            for r in range(1, g):
                x = jnp.where(lo // R == (place + r) % g, do_refs[r][here, :], x)
            rows.append(x)
        do = jnp.concatenate(rows, axis=0).astype(F32)
        do = jnp.where(head_mask((bq, W), h), do * st[:, h : h + 1], 0.0)
        delta = jnp.sum(do * o_ref[at, :].astype(F32), axis=1, keepdims=True)
        delta = jnp.concatenate([jnp.broadcast_to(delta, (bq, 128)).astype(BF)] * rep, 1)
        e0 = jnp.broadcast_to(st[:, 8 + h : 9 + h], (bq, 128)).astype(BF)
        e0 = jnp.concatenate([e0] * rep, 1)
        do_b = do.astype(BF)
        do_t = do.T[lanes, :].astype(BF)
        q_t = q_ref[at, :].astype(F32).T[lanes, :].astype(BF)
        dq = [None] * nr
        for kb in range(lo_blk, (c + 1) * nr):
            base = kb * bk
            first = max(0, kb - c * nr)
            r0 = first * bk
            chunk = base // CHUNK
            top_row = c * bq - chunk * CHUNK
            cols = slice(base, base + bk)
            wv = w_refs[chunk][h, top_row + r0 : top_row + bq, base % CHUNK : base % CHUNK + bk]
            wg = nt(do_b[r0:, :], v_ref[cols, :]).astype(BF)
            dl = delta[r0:, :]
            e = e0[r0:, :]
            if base >= c * bq:
                top = e[:bk, :] * tri
                e = top if r0 + bk == bq else jnp.concatenate([top, e[bk:, :]], axis=0)
            zero = jnp.zeros_like(wv)
            d = jnp.where(wv < 0, -dl, jnp.where(wv > 0, dl, zero))
            gr = (jnp.abs(wv) + e) * (wg - d)
            dv = nn(do_t[:, r0:], wv)
            dk = nn(q_t[:, r0:], gr)
            if not second:
                dv_ref[:, cols] = dv
                dk_ref[:, cols] = dk
            else:
                if base < SHORT:
                    dv = dv + dv_ref[:, cols]
                    dk = dk + dk_ref[:, cols]
                t_ref[k_at, cols] = (dk * scale).astype(BF)
                t_ref[v_at, cols] = dv.astype(BF)
            res = nn(gr, k_ref[cols, :])
            for r in range(first, nr):
                part = res[(r - first) * bk : (r - first + 1) * bk, :]
                dq[r] = part if dq[r] is None else dq[r] + part
        dq = (jnp.concatenate(dq, axis=0) * scale).T[lanes, :].astype(BF)
        if second:
            t_ref[q_at, at] = dq
        else:
            tq_ref[...] = dq

    if not second:
        body(0, 0)
        return
    t_ref[q_at, 0:SHORT] = tq_ref[...]
    pl.when(long)(functools.partial(body, 1, 0))

    @pl.when(~long)
    def _():
        t_ref[k_at, 0:SHORT] = (dk_ref[...] * scale).astype(BF)
        t_ref[v_at, 0:SHORT] = dv_ref[...].astype(BF)
        body(1, SHORT // bk)

    gq = jnp.zeros((3 * HD, D), F32)
    for r in range(g):
        start = pl.multiple_of((place + r) % g * R, R)
        gq = gq + nn(t_ref[:, pl.ds(start, R)], n1_refs[r][...])
    gq_ref[...] = gq.astype(BF)
    bias_ref[...] = nt(jnp.ones((VROWS, L), BF), t_ref[...])
    bias = jnp.sum(t_ref[...].astype(F32), axis=1, keepdims=True)
    wt = jnp.concatenate([wt_ref[i * W + h * HD : i * W + (h + 1) * HD, :] for i in range(3)], axis=0)
    wt = wt.astype(F32)
    vec_ref[...] = jnp.concatenate(
        [
            jnp.sum(wt * gq, axis=0, keepdims=True),
            jnp.sum(wt * bias, axis=0, keepdims=True),
            jnp.zeros((6, D), F32),
        ],
        axis=0,
    )


def attn_bwd(flag, h, q, k, v, st, o, wt, dos, ws, n1s, half=None, bk=256):
    L, W = q.shape
    g = len(dos)
    D = wt.shape[1]
    rows = 3 * HD
    second = half is not None
    args = [q, k, v, st, o, wt, *dos, *ws, *n1s, *(half or [])]
    if second:
        outs = [kept((rows, L), BF), kept((rows, D), BF), kept((8, D), F32), kept((VROWS, rows), F32)]
    else:
        outs = [kept((HD, SHORT), BF)] + [kept((HD, SHORT), F32)] * 2
    return pl.pallas_call(
        functools.partial(bwd_kernel, h, bk, g, second),
        in_specs=[VMEM] * (1 + len(args)),
        out_specs=[VMEM] * len(outs),
        out_shape=outs,
        compiler_params=params(BWD_MIB),
        cost_estimate=cost(2.1 + 3.0 * second),
        name="attn_bwd",
    )(flag, *args)


def ffn_kernel(g, slots, halves, todo, first, last, *refs):
    m = g * slots
    place, _ = place_in(g)
    it = iter(refs)

    def take(count):
        return [next(it) for _ in range(count)]

    ow_refs, up_refs, dn_refs = take(m if first or last else len(todo)), take(len(todo)), take(len(todo))
    (vec_ref,) = take(1)
    if first or last:
        o_refs, att_refs = take(slots), take(m - slots)
    if first:
        x_ref, cot_in = take(2)
    else:
        mids, n2, n2t, cots, cott, oacc_in, nacc_in = take(7)
    if first:
        mids, n2, n2t, cots, cott = take(5)
    if last:
        lo_ref, oacc = take(2)
        atg_refs, og_refs = take(m), take(m)
        (nacc,) = take(1)
        oacc_out = oacc
    else:
        oacc_out, nacc = take(2)
    ug_refs, dg_refs = take(len(todo)), take(len(todo))
    R, D = cots.shape
    FS = up_refs[0].shape[1]
    W = (ow_refs[0].shape[0] - VROWS) // 4
    step = R // halves
    blocks = [slice(j, j + step) for j in range(0, R, step)]

    def vec(i):
        return vec_ref[2 + i : 3 + i, :]

    def att_rows(at):
        rows = pl.ds(pl.multiple_of(place * R + at.start, step), step)
        return jnp.concatenate([o[rows, :] for o in o_refs] + [a[at, :] for a in att_refs], axis=1)

    if first or last:
        ow = jnp.concatenate([a[3 * W : 4 * W, :] for a in ow_refs], axis=0)
    if first:
        cots[...] = cot_in[...]
        for at in blocks:
            mid = x_ref[at, :].astype(F32) + nn(att_rows(at), ow) + vec(0)
            mids[at, :] = mid
            xh, _ = ln_stats(mid)
            y = xh * vec(1) + vec(2)
            n2[at, :] = y.astype(BF)
            n2t[:, at] = y.T.astype(BF)
            cott[:, at] = cots[at, :].astype(F32).T.astype(BF)

    for j, i in enumerate(todo):
        up = up_refs[j][...]
        dn = dn_refs[j][...]
        bias_ref = ow_refs[i if first or last else j]
        ub = bias_ref[4 * W : 4 * W + VROWS, :].astype(F32)[1:2, 0:FS]
        ug = dg = ubg = None
        for at in blocks:
            u = nn(n2[at, :], up) + ub
            ag = nt(cots[at, :], dn)
            u2 = u * u
            t = jnp.tanh(u * (GELU_C + (GELU_C * 0.044715) * u2))
            hh = 0.5 + 0.5 * t
            act = (u * hh).astype(BF)
            slope = hh + u * (0.5 - 0.5 * t * t) * (GELU_C + (3 * GELU_C * 0.044715) * u2)
            pgf = ag * slope
            pg = pgf.astype(BF)
            out = nn(act, dn)
            back = nt(pg, up)
            if j > 0:
                oacc_out[at, :] += out
                nacc[at, :] += back
            elif first:
                oacc_out[at, :] = mids[at, :] + vec(3) + out
                nacc[at, :] = back
            else:
                oacc_out[at, :] = oacc_in[at, :] + out
                nacc[at, :] = nacc_in[at, :] + back
            bsum = jnp.sum(pgf, axis=0, keepdims=True)
            gu = nn(n2t[:, at], pg)
            gd = nn(cott[:, at], act)
            ubg = bsum if ubg is None else ubg + bsum
            ug = gu if ug is None else ug + gu
            dg = gd if dg is None else dg + gd
        ug_refs[j][0:D, :] = ug.astype(BF)
        ug_refs[j][D:, :] = jnp.broadcast_to(ubg, (PAD, FS)).astype(BF)
        dg_refs[j][...] = dg.T.astype(BF)

    if not last:
        return
    mg_ref = oacc
    sums = [None] * 4
    og = None
    for at in blocks:
        lo_ref[at, :] = oacc[at, :].astype(BF)
        xh, rs = ln_stats(mids[at, :])
        ng = nacc[at, :]
        e = ng * vec(1)
        cf = cots[at, :].astype(F32)
        back = e - jnp.mean(e, axis=1, keepdims=True) - xh * jnp.mean(e * xh, axis=1, keepdims=True)
        mg = cf + rs * back
        mg_ref[at, :] = mg
        bg = mg.astype(BF)
        atg = nt(bg, ow).astype(BF)
        for i in range(m):
            atg_refs[i][at, :] = atg[:, i * W : (i + 1) * W]
        gr = tn(att_rows(at), bg)
        og = gr if og is None else og + gr
        for i, a in enumerate((bg.astype(F32), ng * xh, ng, cf)):
            a = jnp.sum(a, axis=0, keepdims=True)
            sums[i] = a if sums[i] is None else sums[i] + a
    og = og.astype(BF)
    both = jnp.concatenate(sums + [jnp.zeros((4, D), F32)], axis=0)
    hi = both.astype(BF).astype(F32)
    both = jnp.concatenate([hi, both - hi], axis=0).astype(BF)
    for i in range(m):
        og_refs[i][0:W, :] = og[i * W : (i + 1) * W, :]
        og_refs[i][W:, :] = both


def ffn(g, slots, todo, ow, up, dn, vecs, attended, start=None, state=None, last=False, halves=2):
    first = state is None
    R, D = (start[0] if first else state[0]).shape
    FS = up[0].shape[1]
    W = (ow[0].shape[0] - VROWS) // 4
    m = g * slots
    args = [*(ow if first or last else [ow[i] for i in todo])]
    args += [up[i] for i in todo] + [dn[i] for i in todo] + [vecs]
    if first or last:
        args += attended
    args += start if first else state
    outs = []
    if first:
        outs += [kept((R, D), F32), kept((R, D), BF), kept((D, R), BF), kept((R, D), BF), kept((D, R), BF)]
    if last:
        outs += [S((R, D), BF), kept((R, D), F32)] + [kept((R, W), BF)] * m + [kept((W + VROWS, D), BF)] * m
        outs += [kept((R, D), F32)]
    else:
        outs += [kept((R, D), F32)] * 2
    total_at = (1, 2 + 2 * m) if last else (5, 6) if first else (0, 1)
    alias = {} if first else {len(args) - 2: total_at[0], len(args) - 1: total_at[1]}
    outs += [kept((D + PAD, FS), BF)] * len(todo) + [kept((FS, D), BF)] * len(todo)
    res = pl.pallas_call(
        functools.partial(ffn_kernel, g, slots, halves, todo, first, last),
        in_specs=[VMEM] * len(args),
        out_specs=[VMEM] * len(outs),
        out_shape=outs,
        input_output_aliases=alias,
        compiler_params=params(FFN_MIB),
        cost_estimate=cost(5.0),
        name="ffn",
    )(*args)
    ugs, dgs = res[len(res) - 2 * len(todo) : len(res) - len(todo)], res[len(res) - len(todo) :]
    return res[: len(res) - 2 * len(todo)], dict(zip(todo, ugs)), dict(zip(todo, dgs))


def back_kernel(g, heads, last, rel, *refs):
    place, _ = place_in(g)
    count = len(heads)
    t_refs, wt_refs = refs[:count], refs[count : 2 * count]
    rest = refs[2 * count :]
    out_ref = rest[-1]
    R = out_ref.shape[0]
    start = pl.multiple_of((place + rel) % g * R, R)
    t = jnp.concatenate([a[:, pl.ds(start, R)] for a in t_refs], axis=0)
    wt = []
    for own, ref in zip(heads, wt_refs):
        W = (ref.shape[0] - VROWS) // 4
        wt += [ref[i * W + h * HD : i * W + (h + 1) * HD, :] for h in own for i in range(3)]
    n1g = tn(t, jnp.concatenate(wt, axis=0))
    if not last:
        out_ref[...] = n1g.astype(BF)
        return
    x_ref, mg_ref, vec_ref = rest[g - 1 : g + 2]
    for a in rest[: g - 1]:
        n1g = n1g + a[...].astype(F32)
    xh, rs = ln_stats(x_ref[...].astype(F32))
    e = n1g * vec_ref[0:1, :]
    back = e - jnp.mean(e, axis=1, keepdims=True) - xh * jnp.mean(e * xh, axis=1, keepdims=True)
    out_ref[...] = (mg_ref[...] + rs * back).astype(BF)


def row_back(g, rel, heads, ts, wts, R, last=None):
    D = wts[0].shape[1]
    args = [*ts, *wts] + ([] if last is None else [*last[0], *last[1:]])
    return pl.pallas_call(
        functools.partial(back_kernel, g, heads, last is not None, rel),
        in_specs=[VMEM] * len(args),
        out_specs=VMEM,
        out_shape=kept((R, D), BF) if last is None else S((R, D), BF),
        compiler_params=params(BACK_MIB),
        cost_estimate=cost(2.0),
        name="row_back" if last is None else "norm_back",
    )(*args)


def fuse(body, outs, *args, scratch=()):
    return pl.pallas_call(
        body,
        in_specs=[VMEM] * len(args),
        out_specs=[VMEM] * len(outs),
        out_shape=outs,
        scratch_shapes=list(scratch),
        compiler_params=params(SUM_MIB),
        name=body.__name__,
    )(*args)


def sum_of(refs, at):
    out = refs[0][at].astype(F32)
    for a in refs[1:]:
        out = out + a[at].astype(F32)
    return out.astype(BF)


def join_vec(v):
    v = v.astype(F32)
    return v[: VROWS // 2] + v[VROWS // 2 :]


def split_vec(v):
    hi = v.astype(BF).astype(F32)
    return jnp.concatenate([hi, v - hi], axis=0).astype(BF)


def vec_of(refs, at):
    return split_vec(functools.reduce(lambda a, b: a + b, [join_vec(a[at]) for a in refs]))


def pack_inputs(qkv_t, out_weight, qkv_bias, up_bias, tokens, long_slot, vecs):
    rows, D = qkv_t.shape
    W = out_weight.shape[0]
    flat = [up_bias, *vecs]
    slots = long_slot.shape[0]
    g = lax.axis_size("head") // slots

    def pack(qt_ref, ow_ref, qb_ref, x_ref, s_ref, *refs):
        flat_refs, refs = refs[: len(flat)], refs[len(flat) :]
        out, x_out, flag_ref, vec_ref, qb_in, s_in = refs[:6]
        flat_in, sems = refs[6:-1], refs[-1]
        pairs = [
            (qb_ref, qb_in),
            (s_ref, s_in),
            *zip(flat_refs, flat_in),
            (ow_ref, out.at[pl.ds(rows, W)]),
            (x_ref, x_out),
        ]
        copies = [pltpu.make_async_copy(a, b, sems.at[i]) for i, (a, b) in enumerate(pairs)]
        for c in copies:
            c.start()
        out[0:rows, :] = qt_ref[...]
        for c in copies[:-2]:
            c.wait()
        qb = qb_in[...].astype(F32)
        qb = jnp.concatenate([qb[i : i + 1, :] for i in range(3)], axis=1)
        lines = [qb, as_row(flat_in[0]), jnp.zeros((VROWS - 2, D), F32)]
        lines = [jnp.pad(a, ((0, 0), (0, D - a.shape[1]))) for a in lines]
        out[rows + W :, :] = jnp.concatenate(lines, axis=0).astype(BF)
        vec_ref[...] = jnp.concatenate(
            [as_row(a) for a in flat_in[1:]] + [jnp.zeros((2, D), F32)], axis=0
        )
        _, group = place_in(g)
        flag_ref[...] = jnp.full((8, 128), (s_in[group] > 0).astype(F32))
        for c in copies[-2:]:
            c.wait()

    hbm = [in_hbm(a) for a in (out_weight, qkv_bias, tokens, long_slot, *flat)]
    return pl.pallas_call(
        pack,
        in_specs=[VMEM] + [ANY] * len(hbm),
        out_specs=[VMEM] * 4,
        out_shape=[
            kept((rows + W + VROWS, D), BF),
            kept(tokens.shape, BF),
            kept((8, 128), F32),
            kept((8, D), F32),
        ],
        scratch_shapes=[pltpu.VMEM(qkv_bias.shape, BF), pltpu.SMEM((slots,), jnp.int32)]
        + [pltpu.VMEM(a.shape, BF) for a in flat]
        + [pltpu.SemaphoreType.DMA((4 + len(flat),))],
        compiler_params=params(SUM_MIB),
        name="pack",
    )(qkv_t, *hbm)


def half_at(bit, count, mine):
    place = lax.axis_index("batch") // 2**bit % 2
    place = place if mine else 1 - place
    return pl.ds(pl.multiple_of(place * count, count), count)


def add_up(terms, vec_rows=0):
    rows, cols = terms[0].shape
    count = rows - vec_rows

    def sum_terms(*refs):
        ins, out = refs[: len(terms)], refs[len(terms)]
        if count:
            out[0:count, :] = sum_of(ins, slice(0, count))
        if vec_rows:
            out[count:, :] = vec_of(ins, slice(count, rows))

    return fuse(sum_terms, [kept((rows, cols), BF)], *terms)[0]


def with_vec(terms, vec):
    rows, cols = terms[0].shape

    def sum_vec(*refs):
        ins, vec_ref, out = refs[: len(terms)], refs[-2], refs[-1]
        out[0:rows, :] = sum_of(ins, slice(0, rows))
        out[rows:, :] = vec_ref[...]

    return fuse(sum_vec, [kept((rows + VROWS, cols), BF)], *terms, vec)[0]


def halve(bit, terms, has_vec=False):
    rows, cols = terms[0].shape
    count = (rows - VROWS if has_vec else rows) // 2

    def sum_halves(*refs):
        ins, outs = refs[: len(terms)], refs[len(terms) :]
        for out, mine in zip(outs, (True, False)):
            out[0:count, :] = sum_of(ins, half_at(bit, count, mine))
            if has_vec:
                out[count:, :] = vec_of(ins, slice(2 * count, rows))

    return fuse(sum_halves, [kept((count + VROWS * has_vec, cols), BF)] * 2, *terms)


def stack_sums(downs, outs_):
    fs, cols = downs[0].shape
    rows = fs + outs_[0].shape[0]

    def sum_pieces(*refs):
        ins, out = refs[:-1], refs[-1]
        out[0:fs, :] = sum_of(ins[: len(downs)], slice(0, fs))
        out[fs : rows - VROWS, :] = sum_of(ins[len(downs) :], slice(0, rows - fs - VROWS))
        out[rows - VROWS :, :] = vec_of(ins[len(downs) :], slice(rows - fs - VROWS, rows - fs))

    return fuse(sum_pieces, [kept((rows, cols), BF)], *downs, *outs_)[0]


def join(bit, mine, other, count):
    def join_halves(mine_ref, other_ref, out):
        out[half_at(bit, count, True), :] = mine_ref[0:count, :]
        out[half_at(bit, count, False), :] = other_ref[0:count, :]

    return fuse(join_halves, [kept((2 * count, mine.shape[1]), BF)], mine, other)[0]


def collect(mine, other, count, splits, has_vec=False):
    cols = mine.shape[1]

    def gather_halves(mine_ref, other_ref, *refs):
        outs, whole = refs[:-1], refs[-1]
        whole[half_at(0, count, True), :] = mine_ref[0:count, :].astype(F32)
        whole[half_at(0, count, False), :] = other_ref[0:count, :].astype(F32)
        first = 0
        for out, size in zip(outs, splits):
            out[...] = whole[first : first + size, :]
            first += size
        if has_vec:
            at = slice(count, count + VROWS)
            outs[-1][...] = join_vec(mine_ref[at, :]) + join_vec(other_ref[at, :])

    return fuse(
        gather_halves,
        [S((a, cols), F32) for a in splits] + [S((VROWS // 2, cols), F32)] * has_vec,
        mine,
        other,
        scratch=[pltpu.VMEM((2 * count, cols), F32)],
    )


def fill_rows(ref, g_ref, bias_ref):
    rows = g_ref.shape[0]
    ref[0:rows, :] = g_ref[...]
    ref[rows:, :] = jnp.zeros((ref.shape[0] - rows, ref.shape[1]), BF)
    ref[rows : rows + VROWS, 0 : bias_ref.shape[1]] = bias_ref[...].astype(BF)


def q_rows(gq, bias):
    def stack_rows(g_ref, bias_ref, out):
        fill_rows(out, g_ref, bias_ref)

    return fuse(stack_rows, [kept((gq.shape[0] + QPAD, gq.shape[1]), BF)], gq, bias)[0]


def q_halve(gq, bias, crossed):
    rows, cols = gq.shape[0] + QPAD, gq.shape[1]
    count = rows // 2

    def sum_rows(g_ref, bias_ref, *refs):
        c_refs = refs[: len(crossed)]
        mine, other, whole = refs[-3:]
        fill_rows(whole, g_ref, bias_ref)
        for out, which in ((mine, True), (other, False)):
            out[...] = sum_of([whole, *c_refs], half_at(0, count, which))

    return fuse(
        sum_rows,
        [kept((count, cols), BF)] * 2,
        gq,
        bias,
        *crossed,
        scratch=[pltpu.VMEM((rows, cols), BF)],
    )


def after(x, *deps):
    return lax.optimization_barrier((x,) + deps)[0]


class Chain:
    def __init__(self, steps):
        self.steps = steps
        self.result = None
        self.sent, self.got = next(steps)

    def tick(self, *deps):
        if self.result is None:
            try:
                self.sent, self.got = self.steps.send(after(self.got, *deps))
            except StopIteration as stop:
                self.result = stop.value
                self.sent = []


def vec_split(v):
    hi = lax.reduce_precision(v, 8, 7)
    return jnp.concatenate([hi, v - hi], axis=0).astype(BF)


def vec_join(v):
    half = v.shape[0] // 2
    return v[:half].astype(F32) + v[half:].astype(F32)


def per_device(
    tokens_in,
    norm1_gain,
    norm1_bias,
    qkv_weight,
    qkv_bias,
    out_weight,
    out_bias,
    norm2_gain,
    norm2_bias,
    up_weight,
    up_bias,
    down_weight,
    down_bias,
    cotangent,
    long_slot,
):
    n = lax.axis_size("head")
    nb = lax.axis_size("batch")
    slots = long_slot.shape[0]
    g = n // slots
    R, D = tokens_in.shape
    W = qkv_weight.shape[2]
    FS = up_weight.shape[1]
    nh = W // HD
    bits = []
    while 2 ** len(bits) < nb:
        bits.append(2 ** len(bits))

    def cross(x, r):
        return lax.ppermute(x, "head", [(i, (i + r * g) % n) for i in range(n)])

    def rot(x, r):
        return lax.ppermute(x, "head", [(i, i // g * g + (i % g - r) % g) for i in range(n)])

    def flip(x, bit):
        return lax.ppermute(x, "batch", [(i, i ^ bit) for i in range(nb)])

    def exchanged(a):
        return [a] + [cross(a, r) for r in range(1, slots)]

    xs = [tokens_in] + [rot(tokens_in, r) for r in range(1, g)]
    qkv_t = qkv_weight.transpose(1, 2, 0).reshape(3 * W, D)
    small = [norm1_gain, norm1_bias, out_bias, norm2_gain, norm2_bias, down_bias]
    packed, x_own, flag, vecs = pack_inputs(
        qkv_t, out_weight, qkv_bias, up_bias, tokens_in, long_slot, small
    )
    packed = exchanged(packed)
    qkv, n1s = project([x_own] + xs[1:], packed[0], vecs)

    saved = []
    att = []
    for ph in range(slots):
        if ph:
            qkv, _ = project(n1s, after(packed[ph], saved[-1][3]))
        first = qkv[0] if ph == 0 else after(qkv[0], upw[0], dnw[0])
        o, st, ws, sends = attn_fwd(flag, first, *qkv[1:], g)
        saved.append((*qkv, st, o, packed[ph], ws))
        att.append([rot(sends[g - r - 1], r) for r in range(1, g)])
        if ph == 0:
            upw = exchanged(after(up_weight, vecs))
            dnw = exchanged(after(down_weight, st))
            oww = [packed[0]] + [after(b, st) for b in packed[1:]]

    def at(r, ph):
        return r * slots + ph

    def members_of(a):
        return {(r, ph): rot(b, r) if r else b for r in range(g) for ph, b in a}

    def listed(a):
        return [a.get((r, ph)) for r in range(g) for ph in range(slots)]

    ow = listed(members_of(list(enumerate(oww))))
    ups, dns = members_of([(0, upw[0])]), members_of([(0, dnw[0])])
    attended = [a[4] for a in saved] + [att[ph][r - 1] for r in range(1, g) for ph in range(slots)]

    def members(parts):
        return [rot(parts[(g - r) % g], r) for r in range(1, g)]

    def over_batch(terms, has_vec):
        mine, other = halve(1, terms, has_vec)
        got = yield [mine, other], flip(other, bits[1])
        mat = add_up([mine, got], VROWS * has_vec)
        for bit in bits[2:]:
            got = yield [mat], flip(mat, bit)
            mat = add_up([mat, got], VROWS * has_vec)
        got = yield [mat], flip(mat, bits[1])
        count = mat.shape[0] - VROWS * has_vec
        whole = join(1, mat, got, count)
        return (whole, mat[count:]) if has_vec else whole

    ug, dg = {}, {}

    def chain_u():
        others = range(1, slots)
        got = yield [ug[at(r, ph)] for r in range(1, g) for ph in others], [
            [rot(ug[at((g - r) % g, ph)], r) for r in range(1, g)] for ph in others
        ]
        sums = [add_up([ug[at(0, ph)]] + a) for ph, a in zip(others, got)]
        got = yield sums, [cross(sums[slots - r - 1], slots - r) for r in others]
        mine, other = halve(0, [ug[at(0, 0)]] + near + got)
        got = yield [mine, other], flip(other, bits[0])
        mat = yield from over_batch([mine, got], False)
        got = yield [mat], flip(mat, bits[0])
        return collect(mat, got, mat.shape[0], (D, PAD))

    def chain_d():
        got = yield list(dg.values()) + list(og), [
            [[rot(b, r) for b in (dg[at((g - r) % g, ph)], og[at((g - r) % g, ph)])] for r in range(1, g)]
            for ph in range(slots)
        ]
        sums = [
            stack_sums([dg[at(0, ph)]] + [a[0] for a in got[ph]],
                [og[at(0, ph)]] + [a[1] for a in got[ph]],
            )
            for ph in range(slots)
        ]
        got = yield sums, [cross(sums[slots - r], slots - r) for r in range(1, slots)]
        mine, other = halve(0, [sums[0]] + got, True)
        got = yield [mine, other], flip(other, bits[0])
        mat, vec = yield from over_batch([mine, got], True)
        got = yield [mat], flip(mat, bits[0])
        return [*collect(mat, got, mat.shape[0], (FS, W)), vec]

    def part(todo, **more):
        out, new_ug, new_dg = ffn(g, slots, todo, ow, listed(ups), listed(dns), vecs, attended, **more)
        ug.update(new_ug)
        dg.update(new_dg)
        return out

    state = list(part([at(0, 0)], start=[after(x_own, *upw[1:]), cotangent]))
    ups.update(members_of([(ph, upw[ph]) for ph in range(1, slots)]))
    dns.update(members_of([(ph, after(dnw[ph], state[5])) for ph in range(1, slots)]))
    state[5] = after(state[5], *[dns[0, ph] for ph in range(1, slots)])
    out = part([at(r, 0) for r in range(1, g)], state=state)
    state = [*state[:5], *out]
    near = [rot(ug[at((g - r) % g, 0)], r) for r in range(1, g)]
    out = part([at(r, ph) for r in range(1, g) for ph in range(1, slots)], state=state)
    state = [*state[:5], *out]
    u = Chain(chain_u())
    state[5] = after(state[5], *u.sent)
    out = part([at(0, ph) for ph in range(1, slots)], state=state, last=True)
    u.tick(out[0])
    m = g * slots
    lo, mg, atg, og = out[0], out[1], out[2 : 2 + m], out[2 + m : 2 + 2 * m]
    dos = [
        [atg[ph]] + [rot(atg[(g - r) * slots + ph], r) for r in range(1, g)] for ph in range(slots)
    ]
    chains = {"u": u, "d": Chain(chain_d())}
    plan = ["d", "", "u", "", "ud", "ud", "d", "u"]
    grads = {}
    crossing = {}
    done = 0

    def sent():
        return [a for c in chains.values() for a in c.sent]

    def advance(*deps):
        nonlocal done
        for name, chain in chains.items():
            if name[0] == "q" or done >= len(plan) or name in plan[done]:
                chain.tick(*deps)
        done += 1

    def chain_v():
        def first_sum(*refs):
            vec = functools.reduce(lambda a, b: a + b, [v[...] for v in refs[:-1]])
            refs[-1][...] = split_vec(vec)

        parts = [grads[key][2] for key in grads]
        vec = fuse(first_sum, [kept((VROWS, D), BF)], *parts)[0]
        got = yield [vec], [rot(vec, r) for r in range(1, g)]
        vec = add_up([vec] + got, VROWS)
        got = yield [vec], [cross(vec, r) for r in range(1, slots)]
        return add_up([vec] + got, VROWS)

    def chain_q(h):
        res = grads[0, h]
        last = h == nh - 1
        crossed = [crossing[ph, h] for ph in range(1, slots)]
        mine, other = q_halve(res[1], res[3], crossed)
        got = yield [mine, other], flip(other, bits[0])
        if not last:
            mat = add_up([mine, got])
            for bit in bits[1:]:
                got = yield [mat], flip(mat, bit)
                mat = add_up([mat, got])
            got = yield [mat], flip(mat, bits[0])
            return collect(mat, got, mat.shape[0], (2 * mat.shape[0],))
        count = mine.shape[0]
        mat = with_vec([mine, got], chains["v"].result)
        for bit in bits[1:]:
            got = yield [mat], flip(mat, bit)
            mat = add_up([mat, got], VROWS)
        got = yield [mat], flip(mat, bits[0])
        return collect(mat, got, count, (2 * count,), True)

    dep = ()
    for ph in list(range(1, slots)) + [0]:
        q, k, v, st, o, pk, ws = saved[ph]
        for h in range(nh):
            args = [k, v, st, o, pk, dos[ph], ws, n1s]
            half = attn_bwd(flag, h, after(q, *sent(), *dep), *args)
            advance(half[0])
            res = attn_bwd(flag, h, after(q, *sent(), half[0]), *args, half)
            grads[ph, h] = res
            dep = (res[1],)
            advance(res[1])
            if ph:
                crossing[ph, h] = cross(q_rows(res[1], res[3]), slots - ph)
            else:
                chains["q%d" % h] = Chain(chain_q(h))
    chains["v"] = Chain(chain_v())

    order = [(ph, h) for ph in range(slots) for h in range(nh)]
    ts = [grads[key][0] for key in order]
    pks = [saved[ph][5] for ph, h in order]
    head_list = [(h,) for ph, h in order]
    sends = {}
    for r in range(1, g):
        sends[r] = row_back(g, r, head_list, [after(ts[0], *sent())] + ts[1:], pks, R)
    got = [rot(sends[(g - r) % g], r) for r in range(1, g)]
    chains["v"].tick(*sends.values())
    first = after(ts[0], *chains["v"].sent)
    input_grad = row_back(g, 0, head_list, [first] + ts[1:], pks, R, (got, x_own, mg, vecs))
    dep = [input_grad]
    chains["v"].tick(*dep)
    final = "q%d" % (nh - 1)
    tail = [[final, "u", "d"], [final, "q0", "d"], [final, "u", "d"]]
    while any(c.result is None for c in chains.values()):
        names = (tail.pop(0) if tail else None) or list(chains)[::-1]
        for name in names:
            c = chains[name]
            c.tick(*dep)
            dep = c.sent[:1] or dep
    results = {name: c.result for name, c in chains.items()}
    (up_grad, up_bias_grad), (down_grad, out_grad, vec2) = results["u"], results["d"]
    qs = [results["q%d" % h] for h in range(nh)]
    vec1 = qs[-1][1]
    qf = [a[0] for a in qs]
    vec2 = vec_join(vec2)
    gain_grad = (vec1[0] - norm1_bias.astype(F32) * vec1[1]) / norm1_gain.astype(F32)
    qkv_grad = jnp.concatenate([a[: 3 * HD].reshape(3, HD, D) for a in qf], axis=1).transpose(2, 0, 1)
    qkv_bias_grad = jnp.concatenate([a[3 * HD, : 3 * HD].reshape(3, HD) for a in qf], axis=1)
    return (
        lo,
        input_grad,
        gain_grad,
        vec1[1],
        qkv_grad,
        qkv_bias_grad,
        out_grad,
        vec2[0],
        vec2[1],
        vec2[2],
        up_grad,
        up_bias_grad[0],
        down_grad,
        vec2[3],
    )


def solution(mesh):
    rows = P(("batch", "head"), None)
    return jax.shard_map(
        per_device,
        mesh=mesh,
        in_specs=(
            rows,
            P(),
            P(),
            P(None, None, "head"),
            P(None, "head"),
            P("head", None),
            P(),
            P(),
            P(),
            P(None, "head"),
            P("head"),
            P("head", None),
            P(),
            rows,
            P("batch"),
        ),
        out_specs=(
            rows,
            rows,
            P(),
            P(),
            P(None, None, "head"),
            P(None, "head"),
            P("head", None),
            P(),
            P(),
            P(),
            P(None, "head"),
            P("head"),
            P("head", None),
            P(),
        ),
        check_vma=False,
    )
```
